256 devices in a mesh: lon: 128 (over z, y, x_hi, core), lat: 2 (over x_lo).
Axes of the slice: x: 4 (x_hi: 2, x_lo: 2; x = x_hi * 2 + x_lo), y: 4, z: 8, core: 2. Of those that a mesh axis runs over, the one named last changes fastest.
Arguments:
- tokens: bfloat16 [48, 1536, 2, 1024], P('lat', 'lon'), may hold values from -420 to 420
- land_mask: int32 [48, 1536], P('lat', 'lon'), may hold values from 0 to 1
- land_bias: float32 [8], replicated, may hold values from -300 to 300
- qkv_weight: bfloat16 [1024, 1536], replicated, may hold values from -0.1875 to 0.1875
- out_weight: bfloat16 [512, 1024], replicated, may hold values from -0.25 to 0.25
- cotangent: bfloat16 [48, 1536, 2, 1024], P('lat', 'lon'), may hold values from -24 to 24
Outputs:
- block_out: bfloat16 [48, 1536, 2, 1024], P('lat', 'lon')
- grad_tokens: bfloat16 [48, 1536, 2, 1024], P('lat', 'lon')
- grad_qkv: float32 [1024, 1536], P('lon')
- grad_out: float32 [512, 1024], P(None, 'lon')
The draws below stay inside these ranges and needn't reach their ends.
All inputs are finite; a program needn't handle non-finite values.
Results may differ from the reference program's by a relative error of at most 0.012.
Values may be sent and summed in bfloat16 or wider, within the bound.
No kernel may reach another device: no remote copies, remote signals or barrier semaphores. Data moves between devices by JAX's collectives and lax.ppermute only.
A program may use at most 128 MiB of HBM per device.

```python
import math
import jax
import jax.numpy as jnp
from jax import lax

D = 1024
HEADS = 8
HSIZE = 64
WIN_LAT = 6
WIN_LON = 12
LEV = 2
SHIFT_LAT = 3
SHIFT_LON = 6
HD = 512
NLAT = 48
NLON = 1536
TOKENS = 147456


def draw_tokens(key, part):
    key = jax.random.fold_in(key, 11)
    key_base, key_cols = jax.random.split(key, 2)
    shape = (NLAT, NLON, LEV, D)
    col_scale = jnp.exp(jax.random.uniform(key_cols, (D,), minval=0.0, maxval=math.log(10.0)))
    result = jnp.clip(jax.random.normal(key_base, shape), -4.0, 4.0) * col_scale
    return result.astype(jnp.float32).astype(jnp.bfloat16)


def draw_land_mask(key, part):
    key = jax.random.fold_in(key, 23)
    key_tiles, key_lakes = jax.random.split(key, 2)
    tiles = jax.random.randint(key_tiles, (NLAT // WIN_LAT, NLON // WIN_LON), 0, 2)
    coarse = jnp.repeat(jnp.repeat(tiles, WIN_LAT, 0), WIN_LON, 1)
    lakes = jax.random.randint(key_lakes, (NLAT, NLON), 0, 8)
    return (coarse * jnp.minimum(lakes, 1)).astype(jnp.int32)


def draw_land_bias(key, part):
    key = jax.random.fold_in(key, 37)
    key_size = jax.random.fold_in(key, 0)
    result = jax.random.uniform(key_size, (HEADS,), minval=-3.0, maxval=3.0)
    return result.astype(jnp.float32)


def raised(values, stream_key, source, target, blocks, factor):
    def block_of(axis_at):
        return (jnp.arange(values.shape[axis_at]) // (values.shape[axis_at] // blocks)).reshape((-1,) + (1,) * (values.ndim - 1 - axis_at))

    one_side = jax.random.permutation(stream_key, blocks)[block_of(target)]
    other_side = (block_of(target) + blocks // 2) % blocks
    return jnp.where((block_of(source) == one_side) | (block_of(source) == other_side), factor * values, values)


def levels(stream_key, dims, pieces, low, largest):
    gain, own = 1.0, jax.random.fold_in(stream_key, 6)
    for axis_at, parts in pieces:
        draws = jnp.exp(jax.random.uniform(jax.random.fold_in(own, axis_at), (parts,), jnp.float32, low / len(pieces), largest / len(pieces)))
        gain = gain * jnp.repeat(draws, dims[axis_at] // parts).reshape([-1 if axis == axis_at else 1 for axis in range(len(dims))])
    return gain


def normal_values(own_key, shape, scale, limit, shards=(), held_as=jnp.bfloat16):
    entries = jax.random.normal(own_key, shape, jnp.float32) * scale
    if len(shards) > 0:
        entries = levels(own_key, shape, shards, -0.22, 0.18) * entries
    return jnp.clip(entries, min=-limit, max=limit).astype(held_as)


def heavy_noise(key, extent, deviation, most, pieces, heavy, kind=jnp.bfloat16):
    values = deviation * jax.random.normal(key, extent, jnp.float32)
    if pieces:
        values = values * levels(key, extent, pieces, -0.22, 0.18)
    return jnp.clip(raised(values, jax.random.fold_in(key, 3), *heavy), -most, most).astype(kind)


def setup_inputs(seed: int = 0) -> dict:
    streams_of = jax.random.split(jax.random.key(seed), 7)
    return {
        "tokens": draw_tokens(jax.random.fold_in(streams_of[6], 71), 0),
        "land_mask": draw_land_mask(jax.random.fold_in(streams_of[6], 71), 0),
        "land_bias": draw_land_bias(jax.random.fold_in(streams_of[6], 71), 0),
        "qkv_weight": normal_values(streams_of[3], (D, 3 * HD), D ** -0.5, 0.1875),
        "out_weight": normal_values(streams_of[4], (HD, D), HD ** -0.5, 0.25),
        "cotangent": heavy_noise(streams_of[5], (NLAT, NLON, LEV, D), 1.0, 24.0, ((0, 2), (1, 128)), (1, 3, 128, 5.5)),
    }


def to_windows(grid_block):
    row_count, col_count = (grid_block.shape[0], grid_block.shape[1])
    trailing = grid_block.shape[2:]
    parted = grid_block.reshape((row_count // WIN_LAT, WIN_LAT, col_count // WIN_LON, WIN_LON) + trailing)
    ordered = parted.transpose((0, 2, 1, 3) + tuple(range(4, parted.ndim)))
    return ordered.reshape((row_count // WIN_LAT * (col_count // WIN_LON), WIN_LAT * WIN_LON * LEV) + trailing[1:])

def from_windows(window_rows, row_count, col_count):
    feature = window_rows.shape[-1]
    parted = window_rows.reshape(row_count // WIN_LAT, col_count // WIN_LON, WIN_LAT, WIN_LON, LEV, feature)
    return parted.transpose(0, 2, 1, 3, 4, 5).reshape(row_count, col_count, LEV, feature)

def normalize(flat_rows):
    as_float = flat_rows.astype(jnp.float32)
    centred = as_float - lax.optimization_barrier(jnp.mean(as_float, -1, keepdims=True))
    inverse = lax.rsqrt(lax.optimization_barrier(jnp.mean(centred * centred, -1, keepdims=True)) + 1e-05)
    return (centred * inverse, inverse)

def pair_f(left, right, form):
    return jnp.einsum(form, left.astype(jnp.float32), right.astype(jnp.float32))

def layer_step(shifted, land_cells, cotan, first_row, total_rows, land_bias, qkv_weight, out_weight):
    row_count, col_count, feature = (shifted.shape[0], shifted.shape[1], shifted.shape[3])
    row_ids = first_row + lax.broadcasted_iota(jnp.int32, (row_count, col_count, LEV), 0)
    region = to_windows((row_ids >= total_rows - SHIFT_LAT).astype(jnp.int32))
    allowed = region[:, :, None] == region[:, None, :]
    land_tok = to_windows(jnp.broadcast_to(land_cells[:, :, None], (row_count, col_count, LEV)).astype(jnp.float32))
    key_bias = land_tok[:, None, None, :] * land_bias[None, :, None, None]
    windows_in = to_windows(shifted)
    win_count, win_size = (windows_in.shape[0], windows_in.shape[1])
    flat_rows = windows_in.reshape(-1, feature)
    unit, inverse = normalize(flat_rows)
    normed = unit.astype(jnp.bfloat16)
    qkv = jnp.dot(normed, qkv_weight, preferred_element_type=jnp.float32).astype(jnp.bfloat16)
    query_heads = qkv[:, :HD].reshape(win_count, win_size, HEADS, HSIZE)
    key_heads = qkv[:, HD:2 * HD].reshape(win_count, win_size, HEADS, HSIZE)
    value_heads = qkv[:, 2 * HD:].reshape(win_count, win_size, HEADS, HSIZE)
    factor = HSIZE ** (-0.5)
    scores = pair_f(query_heads, key_heads, 'wqhd,wkhd->whqk') * factor + key_bias
    scores = jnp.where(allowed[:, None], scores, -jnp.inf)
    row_max = lax.optimization_barrier(jnp.max(scores, -1, keepdims=True))
    exp_scores = jnp.exp(scores - row_max)
    attn = exp_scores / lax.optimization_barrier(jnp.sum(exp_scores, -1, keepdims=True))
    attn_b = attn.astype(jnp.bfloat16)
    attended = pair_f(attn_b, value_heads, 'whqk,wkhd->wqhd').astype(jnp.bfloat16).reshape(-1, HD)
    out_rows = jnp.dot(attended, out_weight, preferred_element_type=jnp.float32).astype(jnp.bfloat16)
    cot_rows = to_windows(cotan).reshape(-1, feature)
    grad_out = jnp.dot(attended.T, cot_rows, preferred_element_type=jnp.float32)
    d_att = jnp.dot(cot_rows, out_weight.T, preferred_element_type=jnp.float32).astype(jnp.bfloat16)
    d_att = d_att.reshape(win_count, win_size, HEADS, HSIZE)
    d_value = pair_f(attn_b, d_att, 'whqk,wqhd->wkhd').astype(jnp.bfloat16)
    d_attn = pair_f(d_att, value_heads, 'wqhd,wkhd->whqk')
    d_scores = (attn * (d_attn - lax.optimization_barrier(jnp.sum(d_attn * attn, -1, keepdims=True))) * factor).astype(jnp.bfloat16)
    d_query = pair_f(d_scores, key_heads, 'whqk,wkhd->wqhd').astype(jnp.bfloat16)
    d_key = pair_f(d_scores, query_heads, 'whqk,wqhd->wkhd').astype(jnp.bfloat16)
    d_qkv = jnp.concatenate([d_query.reshape(-1, HD), d_key.reshape(-1, HD), d_value.reshape(-1, HD)], -1)
    grad_qkv = jnp.dot(normed.T, d_qkv, preferred_element_type=jnp.float32)
    d_normed = jnp.dot(d_qkv, qkv_weight.T, preferred_element_type=jnp.float32)
    d_flat = inverse * (d_normed - lax.optimization_barrier(jnp.mean(d_normed, -1, keepdims=True)) - unit * lax.optimization_barrier(jnp.mean(d_normed * unit, -1, keepdims=True)))
    d_flat = d_flat.astype(jnp.bfloat16)
    out_grid = from_windows(out_rows.reshape(win_count, win_size, feature), row_count, col_count)
    d_grid = from_windows(d_flat.reshape(win_count, win_size, feature), row_count, col_count)
    return (out_grid, d_grid, grad_qkv, grad_out)

def reference(tokens, land_mask, land_bias, qkv_weight, out_weight, cotangent):
    shifted = jnp.roll(tokens, (-SHIFT_LAT, -SHIFT_LON), (0, 1))
    land_shift = jnp.roll(land_mask, (-SHIFT_LAT, -SHIFT_LON), (0, 1)).astype(jnp.float32)
    cot_shift = jnp.roll(cotangent, (-SHIFT_LAT, -SHIFT_LON), (0, 1))

    def column_step(totals, column_index):
        offset = (column_index * WIN_LON).astype(jnp.int32)
        slab_in = lax.dynamic_slice_in_dim(shifted, offset, WIN_LON, 1)
        land_in = lax.dynamic_slice_in_dim(land_shift, offset, WIN_LON, 1)
        cot_in = lax.dynamic_slice_in_dim(cot_shift, offset, WIN_LON, 1)
        out_grid, d_grid, grad_qkv, grad_out = layer_step(slab_in, land_in, cot_in, 0, NLAT, land_bias, qkv_weight, out_weight)
        return ((totals[0] + grad_qkv, totals[1] + grad_out), (out_grid, d_grid))
    start_sums = (jnp.zeros((D, 3 * HD), jnp.float32), jnp.zeros((HD, D), jnp.float32))
    sums, stacked = lax.scan(column_step, start_sums, jnp.arange(NLON // WIN_LON, dtype=jnp.int32))
    out_all = stacked[0].transpose(1, 0, 2, 3, 4).reshape(NLAT, NLON, LEV, D)
    grad_all = stacked[1].transpose(1, 0, 2, 3, 4).reshape(NLAT, NLON, LEV, D)
    block_out = jnp.roll(out_all, (SHIFT_LAT, SHIFT_LON), (0, 1))
    grad_tokens = jnp.roll(grad_all, (SHIFT_LAT, SHIFT_LON), (0, 1))
    grad_scale = 1.0 / math.sqrt(TOKENS)
    return (block_out, grad_tokens, sums[0] * grad_scale, sums[1] * grad_scale)
```

```python
import math

import jax
import jax.numpy as jnp
from jax import lax
from jax.experimental import pallas as pl
from jax.experimental.pallas import tpu as pltpu
from jax.sharding import Mesh, PartitionSpec as P

D = 1024
HEADS = 8
HSIZE = 64
HD = 512
WIN = 144
HALF = 72
WINS = 4
TOK = 576
SLAB = 128
TOKENS = 147456
GRAD_SCALE = 1.0 / math.sqrt(TOKENS)
FACTOR = HSIZE ** (-0.5)
FAR = -1e30
BF = jnp.bfloat16
F32 = jnp.float32
LON = ("z", "y", "xh", "core")
RING = ("xh", "lat")


def nn(a, b):
    return lax.dot_general(a, b, (((1,), (0,)), ((), ())), preferred_element_type=F32)


def nt(a, b):
    return lax.dot_general(a, b, (((1,), (1,)), ((), ())), preferred_element_type=F32)


def tn(a, b):
    return lax.dot_general(a, b, (((0,), (0,)), ((), ())), preferred_element_type=F32)


def window_rows(own, main, lat, diag, w):
    if w < WINS - 1:
        parts = [own[3 + 6 * w : 9 + 6 * w, 6:12], main[6 * w : 6 * w + 6]]
    else:
        parts = [own[21:24, 6:12], lat[...], main[18:21], diag[...]]
    return jnp.concatenate([p.astype(F32).reshape(-1, D) for p in parts], 0)


def attention_kernel(
    place, bias, tok, cot, main, lat, diag, land, wqkv, wout,
    keep, send, out_own, out_main, out_lat, out_diag, nrm, unit_s, inv_s, dqkv,
    cotb, qkv, datt, att,
):
    core = place[0]
    lat_id = place[1]
    for w in range(WINS):
        x = window_rows(tok, main.at[0], lat.at[0], diag.at[0], w)
        centred = x - jnp.mean(x, -1, keepdims=True)
        inverse = lax.rsqrt(jnp.mean(centred * centred, -1, keepdims=True) + 1e-05)
        unit = centred * inverse
        rows = slice(WIN * w, WIN * w + WIN)
        unit_s[rows] = unit
        inv_s[rows] = jnp.broadcast_to(inverse, (WIN, 128))
        nrm[rows] = unit.astype(BF)
        cotb[rows] = window_rows(cot, main.at[1], lat.at[1], diag.at[1], w).astype(BF)

    for i in range(3):
        cols = slice(HD * i, HD * i + HD)
        r = nn(nrm[...], wqkv[:, cols])
        qkv[:, cols] = (r.astype(BF) * FACTOR).astype(BF) if i == 0 else r.astype(BF)
    datt[...] = nt(cotb[...], wout[...]).astype(BF)

    lane = lax.broadcasted_iota(jnp.int32, (WIN, SLAB), 1)
    first = lane < HSIZE
    k_at = lax.broadcasted_iota(jnp.int32, (WIN, WIN), 0) % HALF
    q_at = lax.broadcasted_iota(jnp.int32, (WIN, WIN), 1) % HALF
    apart = (k_at >= HALF // 2) != (q_at >= HALF // 2)
    zero = jnp.zeros((WIN, SLAB), BF)

    def window(w, carry):
        rows = pl.ds(pl.multiple_of(w * WIN, 16), WIN)
        cut = jnp.logical_and(w == WINS - 1, lat_id == 1)
        mask = jnp.where(jnp.logical_and(apart, cut), FAR, 0.0)
        land_key = jnp.broadcast_to(land[rows], (WIN, WIN))
        for s in range(HEADS // 2):
            q = qkv[rows, SLAB * s : SLAB * s + SLAB]
            k = qkv[rows, HD + SLAB * s : HD + SLAB * s + SLAB]
            v = qkv[rows, 2 * HD + SLAB * s : 2 * HD + SLAB * s + SLAB]
            do = datt[rows, SLAB * s : SLAB * s + SLAB]
            o_pair, dq_pair, dk_pair, dv_pair = [], [], [], []
            for e in range(2):
                mine = first if e == 0 else jnp.logical_not(first)
                k_own = jnp.where(mine, k, zero)
                v_own = jnp.where(mine, v, zero)
                sc = nt(k_own, q) + (land_key * bias[2 * s + e] + mask)
                ex = jnp.exp(sc - jnp.max(sc, 0, keepdims=True))
                attn = ex * (1.0 / jnp.sum(ex, 0, keepdims=True))
                attn_b = attn.astype(BF)
                d_attn = nt(v_own, do)
                delta = jnp.sum(attn * d_attn, 0, keepdims=True)
                d_sc = (attn * (d_attn - delta)).astype(BF)
                o_pair.append(tn(attn_b, v))
                dv_pair.append(nn(attn_b, do))
                dq_pair.append(tn(d_sc, k))
                dk_pair.append(nn(d_sc, q))
            cols = slice(SLAB * s, SLAB * s + SLAB)
            att[rows, cols] = jnp.where(first, o_pair[0], o_pair[1]).astype(BF)
            dqkv[rows, cols] = (jnp.where(first, dq_pair[0], dq_pair[1]) * FACTOR).astype(BF)
            cols = slice(HD + SLAB * s, HD + SLAB * s + SLAB)
            dqkv[rows, cols] = jnp.where(first, dk_pair[0], dk_pair[1]).astype(BF)
            cols = slice(2 * HD + SLAB * s, 2 * HD + SLAB * s + SLAB)
            dqkv[rows, cols] = jnp.where(first, dv_pair[0], dv_pair[1]).astype(BF)
        return carry

    lax.fori_loop(0, WINS, window, 0)

    def put(r, i, half, lo):
        wide = r.shape[1]
        r = (r * GRAD_SCALE).reshape(2, 4, 2, 2, 8, wide)
        for y in range(4):
            for xh in range(2):
                here = r[:, y, xh, 0].reshape(16, wide)
                there = r[:, y, xh, 1].reshape(16, wide)
                at = pl.ds((y * 8 + 2 * i) * 8, 16)
                cols = slice(lo, lo + wide)
                keep[xh * 2 + half, at, cols] = jnp.where(core == 0, here, there)
                send[xh * 2 + half, at, cols] = jnp.where(core == 0, there, here).astype(BF)

    for i in range(4):
        feats = slice(256 * i, 256 * i + 256)
        put(tn(nrm[:, feats], dqkv[:, : 2 * HD]), i, 0, 0)
        put(tn(nrm[:, feats], dqkv[:, 2 * HD :]), i, 1, 0)
        put(tn(cotb[:, feats], att[...]), i, 1, HD)

    for w in range(WINS):
        rows = slice(WIN * w, WIN * w + WIN)
        store_rows(nn(att[rows], wout[...]), out_own, out_main, out_lat, out_diag, w)


def store_rows(r, own, main, lat, diag, w):
    if w < WINS - 1:
        own[3 + 6 * w : 9 + 6 * w, 6:12] = r[:HALF].astype(BF).reshape(6, 6, 2, D)
        main[6 * w : 6 * w + 6] = r[HALF:].astype(BF).reshape(6, 6, 2, D)
    else:
        own[21:24, 6:12] = r[:36].astype(BF).reshape(3, 6, 2, D)
        lat[...] = r[36:72].astype(BF).reshape(3, 6, 2, D)
        main[18:21] = r[72:108].astype(BF).reshape(3, 6, 2, D)
        diag[...] = r[108:].astype(BF).reshape(3, 6, 2, D)


def token_grad_kernel(dqkv, wqkv, unit_s, inv_s, own, main, lat, diag):
    for w in range(WINS):
        rows = slice(WIN * w, WIN * w + WIN)
        d_normed = nt(dqkv[rows], wqkv[...])
        unit = unit_s[rows]
        d_flat = inv_s[rows, 0:1] * (
            d_normed
            - jnp.mean(d_normed, -1, keepdims=True)
            - unit * jnp.mean(d_normed * unit, -1, keepdims=True)
        )
        store_rows(d_flat, own, main, lat, diag, w)


def ring_kernel(place, keep, arrived, kept, s1, s2, s3):
    at = place[2]
    total = lambda i: keep[i] + arrived[i].astype(F32)
    kept[...] = total(at)
    for d, ref in ((1, s1), (2, s2), (3, s3)):
        ref[...] = total((at + d) % 4).astype(BF)


def y_kernel(place, keep, a1, a2, a3, kept, s1, s2, s3):
    def total(i):
        rows = pl.ds(pl.multiple_of(i * 64, 64), 64)
        return keep[rows] + a1[rows].astype(F32) + a2[rows].astype(F32) + a3[rows].astype(F32)

    at = place[3]
    kept[...] = total(at)
    for d, ref in ((1, s1), (2, s2), (3, s3)):
        ref[...] = total((at + d) % 4).astype(BF)


def z_kernel(place, keep, a1, a2, a3, kept, *sends):
    total = keep[...] + a1[...].astype(F32) + a2[...].astype(F32) + a3[...].astype(F32)
    work = sends[-1]
    work[...] = total.reshape(8, 8, D)
    at = place[4]
    kept[...] = work[at]
    for d in range(1, 8):
        r = work[(at + d) % 8]
        sends[d - 1][...] = jnp.concatenate([r[:, :512], r[:, 512:]], 0).astype(BF)


def last_kernel(keep, *refs):
    total = keep[...]
    for a in refs[:-1]:
        r = a[...].astype(F32)
        total = total + jnp.concatenate([r[:8], r[8:]], 1)
    refs[-1][...] = total


def finish_kernel(own, main, lat, diag, out, sems):
    copies = [
        pltpu.make_async_copy(main, out.at[3:24, 0:6], sems.at[0]),
        pltpu.make_async_copy(lat, out.at[0:3, 6:12], sems.at[1]),
        pltpu.make_async_copy(diag, out.at[0:3, 0:6], sems.at[2]),
    ]
    for c in copies:
        c.start()
    for c in copies:
        c.wait()


VM = pl.BlockSpec(memory_space=pltpu.VMEM)
SM = pl.BlockSpec(memory_space=pltpu.SMEM)
ANY = pl.BlockSpec(memory_space=pl.ANY)


def shaped(dims, kind=BF):
    return jax.ShapeDtypeStruct(dims, kind)


def call(body, ins, outs, scratch=(), limit=16, flops=0, name=None, aliases=None, out_spec=VM):
    return pl.pallas_call(
        body,
        in_specs=ins,
        out_specs=[out_spec] * len(outs),
        out_shape=outs,
        scratch_shapes=list(scratch),
        input_output_aliases=aliases or {},
        compiler_params=pltpu.CompilerParams(vmem_limit_bytes=limit * 2**20),
        cost_estimate=pl.CostEstimate(flops=flops, bytes_accessed=8 * 2**20, transcendentals=0),
        name=name,
    )


def shift(block, axis, step):
    count = lax.axis_size(axis)
    return lax.ppermute(block, axis, [(i, (i + step) % count) for i in range(count)])


def shift_both(block, step):
    count = lax.axis_size(LON)
    route = [
        (i * 2 + b, ((i + step) % count) * 2 + 1 - b) for i in range(count) for b in range(2)
    ]
    return lax.ppermute(block, LON + ("lat",), route)


def land_in_windows(land):
    def rows(lo, hi, left):
        cells = land[lo:hi, 0:6] if left else land[lo:hi, 6:12]
        return jnp.broadcast_to(cells[:, :, None], cells.shape + (2,)).reshape(-1)

    land = land.astype(F32)
    left_main = shift(land[3:24, 0:6], LON, -1)
    left_top = shift_both(land[0:3, 0:6], -1)
    right_top = shift(land[0:3, 6:12], "lat", -1)
    left = jnp.concatenate([left_main, left_top], 0).reshape(4, 6, 6)
    right = jnp.concatenate([land[3:24, 6:12], right_top], 0).reshape(4, 6, 6)
    cells = jnp.stack([right, left], 1).reshape(TOK // 2, 1)
    return jnp.broadcast_to(cells, (TOK // 2, 2)).reshape(TOK, 1)


def per_device(tokens, land_mask, land_bias, qkv_weight, out_weight, cotangent):
    xi = lax.axis_index(RING)
    place = jnp.stack(
        [lax.axis_index("core"), lax.axis_index("lat"), xi, lax.axis_index("y"), lax.axis_index("z")]
    ).astype(jnp.int32)
    land = land_in_windows(land_mask)
    main = shift(jnp.stack([tokens[3:24, 0:6], cotangent[3:24, 0:6]]), LON, -1)
    diag = shift_both(jnp.stack([tokens[0:3, 0:6], cotangent[0:3, 0:6]]), -1)
    lat = shift(jnp.stack([tokens[0:3, 6:12], cotangent[0:3, 6:12]]), "lat", -1)

    full, part, edge = (24, 12, 2, D), (21, 6, 2, D), (3, 6, 2, D)
    keep, send, o_own, o_main, o_lat, o_diag, nrm, unit, inverse, dqkv = call(
        attention_kernel,
        [SM, SM] + [VM] * 8,
        [
            shaped((4, 256, D), F32),
            shaped((4, 256, D)),
            shaped(full),
            shaped(part),
            shaped(edge),
            shaped(edge),
            shaped((TOK, D)),
            shaped((TOK, D), F32),
            shaped((TOK, 128), F32),
            shaped((TOK, 3 * HD)),
        ],
        scratch=[
            pltpu.VMEM((TOK, D), BF),
            pltpu.VMEM((TOK, 3 * HD), BF),
            pltpu.VMEM((TOK, HD), BF),
            pltpu.VMEM((TOK, HD), BF),
        ],
        limit=56,
        flops=6 * 10**9,
        name="attention",
    )(place, land_bias, tokens, cotangent, main, lat, diag, land, qkv_weight, out_weight)

    arrived = shift(send, "core", 1)
    t_own, t_main, t_lat, t_diag = call(
        token_grad_kernel,
        [VM] * 4,
        [shaped(full), shaped(part), shaped(edge), shaped(edge)],
        limit=40,
        flops=2 * 10**9,
        name="token_grad",
    )(dqkv, qkv_weight, unit, inverse)

    quarter = (256, D)
    kept, s1, s2, s3 = call(
        ring_kernel,
        [SM, VM, VM],
        [shaped(quarter, F32)] + [shaped(quarter)] * 3,
        limit=24,
        name="sum_core",
    )(place, keep, arrived)
    a = [shift(s, RING, d) for d, s in ((1, s1), (2, s2), (3, s3))]
    kept, s1, s2, s3 = call(
        y_kernel,
        [SM] + [VM] * 4,
        [shaped((64, D), F32)] + [shaped((64, D))] * 3,
        name="sum_ring",
    )(place, kept, *a)
    a = [shift(s, "y", d) for d, s in ((1, s1), (2, s2), (3, s3))]
    kept, *sends = call(
        z_kernel,
        [SM] + [VM] * 4,
        [shaped((8, D), F32)] + [shaped((16, 512))] * 7,
        scratch=[pltpu.VMEM((8, 8, D), F32)],
        name="sum_y",
    )(place, kept, *a)
    a = [shift(s, "z", d + 1) for d, s in enumerate(sends)]
    (mine,) = call(last_kernel, [VM] * 8, [shaped((8, D), F32)], name="sum_z")(kept, *a)
    other = shift(mine, "lat", 1)
    band = lax.axis_index("lat") == 0
    first = jnp.where(band, mine, other)
    second = jnp.where(band, other, mine)
    grad_qkv = jnp.concatenate([first, second[:, :HD]], 1)
    grad_out = second[:, HD:].T

    def home(own, main, lat, diag):
        return call(
            finish_kernel,
            [ANY] * 4,
            [shaped(full)],
            scratch=[pltpu.SemaphoreType.DMA((3,))],
            aliases={0: 0},
            out_spec=ANY,
            name="assemble",
        )(own, shift(main, LON, 1), shift(lat, "lat", 1), shift_both(diag, 1))[0]

    block_out = home(o_own, o_main, o_lat, o_diag)
    grad_tokens = home(t_own, t_main, t_lat, t_diag)
    return (block_out, grad_tokens, grad_qkv, grad_out)


def solution(mesh):
    fine = Mesh(mesh.devices.reshape(8, 4, 2, 2, 2), LON + ("lat",))
    grid = P("lat", LON, None, None)
    in_specs = (grid, P("lat", LON), P(), P(), P(), grid)
    out_specs = (grid, grid, P(LON, None), P(None, LON))
    return jax.shard_map(
        per_device, mesh=fine, in_specs=in_specs, out_specs=out_specs, check_vma=False
    )
```

```python
import math

import jax
import jax.numpy as jnp
import numpy as np
from jax import lax
from jax.experimental import pallas as pl
from jax.experimental.pallas import tpu as pltpu
from jax.sharding import Mesh, PartitionSpec as P

D = 1024
HEADS = 8
HSIZE = 64
HD = 512
WIN = 144
HALF = 72
WINS = 4
TOK = 576
SLAB = 128
TOKENS = 147456
GRAD_SCALE = 1.0 / math.sqrt(TOKENS)
FACTOR = HSIZE ** (-0.5)
FAR = -1e30
BF = jnp.bfloat16
F32 = jnp.float32
LON = ("z", "y", "xh", "core")
ALL = LON + ("lat",)
SIZES = (8, 4, 2, 2, 2)
PEERS = ((0, 1), (1, 0), (1, 1))


def nn(a, b):
    return lax.dot_general(a, b, (((1,), (0,)), ((), ())), preferred_element_type=F32)


def nt(a, b):
    return lax.dot_general(a, b, (((1,), (1,)), ((), ())), preferred_element_type=F32)


def tn(a, b):
    return lax.dot_general(a, b, (((0,), (0,)), ((), ())), preferred_element_type=F32)


def window_rows(own, main, lat, diag, w):
    if w < WINS - 1:
        parts = [own[3 + 6 * w : 9 + 6 * w, 6:12], main[6 * w : 6 * w + 6]]
    else:
        parts = [own[21:24, 6:12], lat[...], main[18:21], diag[...]]
    return jnp.concatenate([p.astype(F32).reshape(-1, D) for p in parts], 0)


def attention_kernel(
    place, bias, tok, cot, main, lat, diag, land, wqkv, wout,
    keep, send, nrm, inv_s, dqkv, att,
    cotb, qkv, datt,
):
    core = place[0]
    lat_id = place[1]
    for w in range(WINS):
        x = window_rows(tok, main.at[0], lat.at[0], diag.at[0], w)
        centred = x - jnp.mean(x, -1, keepdims=True)
        inverse = lax.rsqrt(jnp.mean(centred * centred, -1, keepdims=True) + 1e-05)
        unit = centred * inverse
        rows = slice(WIN * w, WIN * w + WIN)
        inv_s[rows] = jnp.broadcast_to(inverse, (WIN, 128))
        nrm[rows] = unit.astype(BF)
        cotb[rows] = window_rows(cot, main.at[1], lat.at[1], diag.at[1], w).astype(BF)

    for i in range(3):
        cols = slice(HD * i, HD * i + HD)
        r = nn(nrm[...], wqkv[:, cols])
        qkv[:, cols] = (r.astype(BF) * FACTOR).astype(BF) if i == 0 else r.astype(BF)
    datt[...] = nt(cotb[...], wout[...]).astype(BF)

    lane = lax.broadcasted_iota(jnp.int32, (WIN, SLAB), 1)
    first = lane < HSIZE
    k_at = lax.broadcasted_iota(jnp.int32, (WIN, WIN), 0) % HALF
    q_at = lax.broadcasted_iota(jnp.int32, (WIN, WIN), 1) % HALF
    apart = (k_at >= HALF // 2) != (q_at >= HALF // 2)
    zero = jnp.zeros((WIN, SLAB), BF)

    def window(w, carry):
        rows = pl.ds(pl.multiple_of(w * WIN, 16), WIN)
        cut = jnp.logical_and(w == WINS - 1, lat_id == 1)
        mask = jnp.where(jnp.logical_and(apart, cut), FAR, 0.0)
        land_key = jnp.broadcast_to(land[rows], (WIN, WIN))
        for s in range(HEADS // 2):
            q = qkv[rows, SLAB * s : SLAB * s + SLAB]
            k = qkv[rows, HD + SLAB * s : HD + SLAB * s + SLAB]
            v = qkv[rows, 2 * HD + SLAB * s : 2 * HD + SLAB * s + SLAB]
            do = datt[rows, SLAB * s : SLAB * s + SLAB]
            o_pair, dq_pair, dk_pair, dv_pair = [], [], [], []
            for e in range(2):
                mine = first if e == 0 else jnp.logical_not(first)
                k_own = jnp.where(mine, k, zero)
                v_own = jnp.where(mine, v, zero)
                sc = nt(k_own, q) + (land_key * bias[2 * s + e] + mask)
                ex = jnp.exp(sc - jnp.max(sc, 0, keepdims=True))
                attn = ex * (1.0 / jnp.sum(ex, 0, keepdims=True))
                attn_b = attn.astype(BF)
                d_attn = nt(v_own, do)
                delta = jnp.sum(attn * d_attn, 0, keepdims=True)
                d_sc = (attn * (d_attn - delta)).astype(BF)
                o_pair.append(tn(attn_b, v))
                dv_pair.append(nn(attn_b, do))
                dq_pair.append(tn(d_sc, k))
                dk_pair.append(nn(d_sc, q))
            cols = slice(SLAB * s, SLAB * s + SLAB)
            att[rows, cols] = jnp.where(first, o_pair[0], o_pair[1]).astype(BF)
            dqkv[rows, cols] = (jnp.where(first, dq_pair[0], dq_pair[1]) * FACTOR).astype(BF)
            cols = slice(HD + SLAB * s, HD + SLAB * s + SLAB)
            dqkv[rows, cols] = jnp.where(first, dk_pair[0], dk_pair[1]).astype(BF)
            cols = slice(2 * HD + SLAB * s, 2 * HD + SLAB * s + SLAB)
            dqkv[rows, cols] = jnp.where(first, dv_pair[0], dv_pair[1]).astype(BF)
        return carry

    lax.fori_loop(0, WINS, window, 0)

    def put(r, i, lo):
        wide = r.shape[1]
        r = (r * GRAD_SCALE).reshape(2, 4, 2, 2, 8, wide)
        cols = slice(lo, lo + wide)
        for z in range(2):
            for y in range(4):
                even = r[z, y, :, 0].reshape(16, wide)
                odd = r[z, y, :, 1].reshape(16, wide)
                at = y * 8 + 2 * i + z
                keep[at, :, cols] = jnp.where(core == 0, even, odd)
                send[at, :, cols] = jnp.where(core == 0, odd, even).astype(BF)

    for i in range(4):
        feats = slice(256 * i, 256 * i + 256)
        put(tn(nrm[:, feats], dqkv[...]), i, 0)
        put(tn(cotb[:, feats], att[...]), i, 3 * HD)


def store_rows(r, own, main, lat, diag, w):
    r = r.astype(BF)
    if w < WINS - 1:
        own[3 + 6 * w : 9 + 6 * w, 6:12] = r[:HALF].reshape(6, 6, 2, D)
        main[6 * w : 6 * w + 6] = r[HALF:].reshape(6, 6, 2, D)
    else:
        own[21:24, 6:12] = r[:36].reshape(3, 6, 2, D)
        lat[...] = r[36:72].reshape(3, 6, 2, D)
        main[18:21] = r[72:108].reshape(3, 6, 2, D)
        diag[...] = r[108:].reshape(3, 6, 2, D)


def token_kernel(att, wout, dqkv, wqkv, nrm, inv_s, out_own, tok_own, main, lat, diag):
    for w in range(WINS):
        rows = slice(WIN * w, WIN * w + WIN)
        store_rows(nn(att[rows], wout[...]), out_own, main.at[0], lat.at[0], diag.at[0], w)
        d_normed = nt(dqkv[rows], wqkv[...])
        unit = nrm[rows].astype(F32)
        d_flat = inv_s[rows, 0:1] * (
            d_normed
            - jnp.mean(d_normed, -1, keepdims=True)
            - unit * jnp.mean(d_normed * unit, -1, keepdims=True)
        )
        store_rows(d_flat, tok_own, main.at[1], lat.at[1], diag.at[1], w)


def core_kernel(place, keep, arrived, kept, s1, s2, s3, held, landed, sems):
    def copies(n):
        at = place[2 + n]
        return (
            pltpu.make_async_copy(keep.at[at], held.at[n], sems.at[0, n]),
            pltpu.make_async_copy(arrived.at[at], landed.at[n], sems.at[1, n]),
        )

    order = list(range(8, 32)) + list(range(8))
    for n in order:
        for c in copies(n):
            c.start()
    for n in order:
        for c in copies(n):
            c.wait()
        total = held[n] + landed[n].astype(F32)
        if n < 8:
            kept[n] = total
        else:
            (s1, s2, s3)[n // 8 - 1][n % 8] = total.astype(BF)


def middle_kernel(place, keep, a1, a2, a3, kept, s1, s2, s3):
    def total(i):
        at = pl.ds(2 * i, 2)
        return keep[at] + a1[at].astype(F32) + a2[at].astype(F32) + a3[at].astype(F32)

    mine = place[34]
    kept[...] = total(mine)
    for (dy, dz), ref in zip(PEERS, (s1, s2, s3)):
        ref[...] = total(mine ^ (2 * dy + dz)).astype(BF)


def late_kernel(place, keep, a1, a2, a3, kept, s1, s2, s3, work):
    total = keep[...] + a1[...].astype(F32) + a2[...].astype(F32) + a3[...].astype(F32)
    work[...] = total.reshape(2, 2, 8, 2 * D)
    z, x = place[35], place[36]
    kept[...] = work[z, x]
    for (dz, dx), ref in zip(PEERS, (s1, s2, s3)):
        r = work[z ^ dz, x ^ dx]
        ref[...] = jnp.concatenate([r[:, :D], r[:, D:]], 0).astype(BF)


def last_kernel(keep, a1, a2, a3, out):
    total = keep[...]
    for a in (a1, a2, a3):
        r = a[...].astype(F32)
        total = total + jnp.concatenate([r[:8], r[8:]], 1)
    out[...] = total


def finish_kernel(out_own, tok_own, main, lat, diag, out, tok, sems):
    copies = []
    for i, ref in enumerate((out, tok)):
        copies += [
            pltpu.make_async_copy(main.at[i], ref.at[3:24, 0:6], sems.at[i, 0]),
            pltpu.make_async_copy(lat.at[i], ref.at[0:3, 6:12], sems.at[i, 1]),
            pltpu.make_async_copy(diag.at[i], ref.at[0:3, 0:6], sems.at[i, 2]),
        ]
    for c in copies:
        c.start()
    for c in copies:
        c.wait()


VM = pl.BlockSpec(memory_space=pltpu.VMEM)
SM = pl.BlockSpec(memory_space=pltpu.SMEM)
ANY = pl.BlockSpec(memory_space=pl.ANY)


def shaped(dims, kind=BF):
    return jax.ShapeDtypeStruct(dims, kind)


def call(body, ins, outs, scratch=(), limit=16, flops=0, name=None, aliases=None, out_spec=VM):
    return pl.pallas_call(
        body,
        in_specs=ins,
        out_specs=[out_spec] * len(outs),
        out_shape=outs,
        scratch_shapes=list(scratch),
        input_output_aliases=aliases or {},
        compiler_params=pltpu.CompilerParams(vmem_limit_bytes=limit * 2**20),
        cost_estimate=pl.CostEstimate(flops=flops, bytes_accessed=8 * 2**20, transcendentals=0),
        name=name,
    )


def shift(block, axis, step):
    count = lax.axis_size(axis)
    return lax.ppermute(block, axis, [(i, (i + step) % count) for i in range(count)])


def shift_both(block, step):
    count = lax.axis_size(LON)
    route = [
        (i * 2 + b, ((i + step) % count) * 2 + 1 - b) for i in range(count) for b in range(2)
    ]
    return lax.ppermute(block, ALL, route)


def flipped(at, y_bits, z_bits, xh):
    z, y, x, core, lat = at
    y2 = (((y + core) % 4) ^ y_bits) - core
    z2 = (((z + core) % 8) ^ z_bits) - core
    return (z2 % 8, y2 % 4, x ^ xh, core, lat)


def exchange(block, y_bits, z_bits, xh=0):
    route = []
    for i, at in enumerate(np.ndindex(*SIZES)):
        route.append((i, int(np.ravel_multi_index(flipped(at, y_bits, z_bits, xh), SIZES))))
    return lax.ppermute(block, ALL, route)


def places():
    rows = []
    for z, y, xh, core, lat in np.ndindex(*SIZES):
        y_label, z_label = (y + core) % 4, (z + core) % 8
        row = [core, lat]
        for dy, dz in ((0, 0),) + PEERS:
            y0, z0 = (y_label & 1) ^ dy, (z_label & 1) ^ dz
            for y1, z1, z2 in np.ndindex(2, 2, 2):
                y_true = (2 * y1 + y0 - core) % 4
                z_true = (4 * z2 + 2 * z1 + z0 - core) % 8
                row.append(y_true * 8 + z_true)
        row += [(y_label >> 1) * 2 + ((z_label >> 1) & 1), z_label >> 2, xh]
        rows.append(row)
    return np.array(rows, np.int32)


def land_in_windows(land):
    def rows(lo, hi, left):
        cells = land[lo:hi, 0:6] if left else land[lo:hi, 6:12]
        return jnp.broadcast_to(cells[:, :, None], cells.shape + (2,)).reshape(-1)

    land = land.astype(F32)
    left_main = shift(land[3:24, 0:6], LON, -1)
    left_top = shift_both(land[0:3, 0:6], -1)
    right_top = shift(land[0:3, 6:12], "lat", -1)
    left = jnp.concatenate([left_main, left_top], 0).reshape(4, 6, 6)
    right = jnp.concatenate([land[3:24, 6:12], right_top], 0).reshape(4, 6, 6)
    cells = jnp.stack([right, left], 1).reshape(TOK // 2, 1)
    return jnp.broadcast_to(cells, (TOK // 2, 2)).reshape(TOK, 1)


def per_device(tokens, land_mask, land_bias, qkv_weight, out_weight, cotangent):
    place = lax.dynamic_index_in_dim(jnp.asarray(places()), lax.axis_index(ALL), 0, False)
    land = land_in_windows(land_mask)
    main = shift(jnp.stack([tokens[3:24, 0:6], cotangent[3:24, 0:6]]), LON, -1)
    diag = shift_both(jnp.stack([tokens[0:3, 0:6], cotangent[0:3, 0:6]]), -1)
    lat = shift(jnp.stack([tokens[0:3, 6:12], cotangent[0:3, 6:12]]), "lat", -1)

    full, part, edge = (24, 12, 2, D), (21, 6, 2, D), (3, 6, 2, D)
    chunks = (32, 16, 2 * D)
    keep, send, nrm, inverse, dqkv, att = call(
        attention_kernel,
        [SM, SM] + [VM] * 8,
        [
            shaped(chunks, F32),
            shaped(chunks),
            shaped((TOK, D)),
            shaped((TOK, 128), F32),
            shaped((TOK, 3 * HD)),
            shaped((TOK, HD)),
        ],
        scratch=[
            pltpu.VMEM((TOK, D), BF),
            pltpu.VMEM((TOK, 3 * HD), BF),
            pltpu.VMEM((TOK, HD), BF),
        ],
        limit=36,
        flops=6 * 10**9,
        name="attention",
    )(place, land_bias, tokens, cotangent, main, lat, diag, land, qkv_weight, out_weight)

    arrived = shift(send, "core", 1)
    def staged(body, scratch, rows, operands, name, sent=None, specs=None):
        kept, *sends = call(
            body,
            specs or [SM] + [VM] * 4,
            [shaped(rows, F32)] + [shaped(sent or rows)] * 3,
            scratch=scratch,
            limit=24,
            name=name,
        )(place, *operands)
        return kept, sends

    kept, sends = staged(
        core_kernel,
        [pltpu.VMEM(chunks, F32), pltpu.VMEM(chunks, BF), pltpu.SemaphoreType.DMA((2, 32))],
        (8, 16, 2 * D),
        (keep, arrived),
        "sum_core",
        specs=[SM, ANY, ANY],
    )
    a = [exchange(s, dy, dz) for (dy, dz), s in zip(PEERS, sends)]
    dqkv, kept = lax.optimization_barrier((dqkv, kept))
    out_own, tok_own, main, lat, diag = call(
        token_kernel,
        [VM] * 6,
        [
            shaped(full),
            shaped(full),
            shaped((2,) + part),
            shaped((2,) + edge),
            shaped((2,) + edge),
        ],
        limit=40,
        flops=3 * 10**9,
        name="token_grad",
    )(att, out_weight, dqkv, qkv_weight, nrm, inverse)

    kept, sends = staged(middle_kernel, [], (2, 16, 2 * D), [kept] + a, "sum_low")
    main, lat, diag, kept = lax.optimization_barrier((main, lat, diag, kept))
    a = [exchange(s, 2 * dy, 2 * dz) for (dy, dz), s in zip(PEERS, sends)]
    kept, sends = staged(
        late_kernel,
        [pltpu.VMEM((2, 2, 8, 2 * D), F32)],
        (8, 2 * D),
        [kept] + a,
        "sum_next",
        sent=(16, D),
    )
    a = [exchange(s, 0, 4 * dz, dx) for (dz, dx), s in zip(PEERS, sends)]
    lat, diag = shift(lat, "lat", 1), shift_both(diag, 1)
    lat, diag, kept = lax.optimization_barrier((lat, diag, kept))
    (mine,) = call(last_kernel, [VM] * 4, [shaped((8, 2 * D), F32)], name="sum_last")(kept, *a)
    total = mine + shift(mine, "lat", 1)

    block_out, grad_tokens = call(
        finish_kernel,
        [ANY] * 5,
        [shaped(full), shaped(full)],
        scratch=[pltpu.SemaphoreType.DMA((2, 3))],
        aliases={0: 0, 1: 1},
        out_spec=ANY,
        name="assemble",
    )(out_own, tok_own, shift(main, LON, 1), lat, diag)
    return (block_out, grad_tokens, total[:, : 3 * HD], total[:, 3 * HD :].T)


def solution(mesh):
    fine = Mesh(mesh.devices.reshape(SIZES), ALL)
    grid = P("lat", LON, None, None)
    in_specs = (grid, P("lat", LON), P(), P(), P(), grid)
    out_specs = (grid, grid, P(LON, None), P(None, LON))
    return jax.shard_map(
        per_device, mesh=fine, in_specs=in_specs, out_specs=out_specs, check_vma=False
    )
```

```python
import math

import jax
import jax.numpy as jnp
import numpy as np
from jax import lax
from jax.experimental import pallas as pl
from jax.experimental.pallas import tpu as pltpu
from jax.sharding import Mesh, PartitionSpec as P

D = 1024
HEADS = 8
HSIZE = 64
HD = 512
WIN = 144
HALF = 72
WINS = 4
TOK = 576
SLAB = 128
TOKENS = 147456
GRAD_SCALE = 1.0 / math.sqrt(TOKENS)
FACTOR = HSIZE ** (-0.5)
FAR = -1e30
BF = jnp.bfloat16
F32 = jnp.float32
LON = ("z", "y", "xh", "core")
ALL = LON + ("lat",)
SIZES = (8, 4, 2, 2, 2)
PEERS = ((0, 1), (1, 0), (1, 1))


def nn(a, b):
    return lax.dot_general(a, b, (((1,), (0,)), ((), ())), preferred_element_type=F32)


def nt(a, b):
    return lax.dot_general(a, b, (((1,), (1,)), ((), ())), preferred_element_type=F32)


def tn(a, b):
    return lax.dot_general(a, b, (((0,), (0,)), ((), ())), preferred_element_type=F32)


def window_rows(own, main, lat, diag, w):
    if w < WINS - 1:
        parts = [own[3 + 6 * w : 9 + 6 * w, 6:12], main[6 * w : 6 * w + 6]]
    else:
        parts = [own[21:24, 6:12], lat[0:3], main[18:21], diag[0:3]]
    return jnp.concatenate([p.astype(F32).reshape(-1, D) for p in parts], 0)


def halo_copies(block, main, lat, diag, sems):
    return [
        pltpu.make_async_copy(block.at[3:10, 0:6], main.at[0:7], sems.at[0]),
        pltpu.make_async_copy(block.at[10:17, 0:6], main.at[7:14], sems.at[1]),
        pltpu.make_async_copy(block.at[17:24, 0:6], main.at[14:21], sems.at[2]),
        pltpu.make_async_copy(block.at[0:3, 6:12], lat.at[0:3], sems.at[3]),
        pltpu.make_async_copy(block.at[0:3, 0:6], diag.at[0:3], sems.at[4]),
    ]


def tok_halo_kernel(land, tok, main, lat, diag, cells, sems):
    copies = halo_copies(tok, main, lat, diag, sems)
    for c in copies:
        c.start()
    by_row = jnp.concatenate([land[...].astype(F32), jnp.zeros((12, 104), F32)], 1)
    cells[...] = jnp.broadcast_to(by_row[:, None, :], (12, 2, 128)).astype(BF)
    more = [
        pltpu.make_async_copy(cells.at[0:6], main.at[21, :, :, 0:128], sems.at[5]),
        pltpu.make_async_copy(cells.at[6:12], lat.at[3, :, :, 0:128], sems.at[6]),
        pltpu.make_async_copy(cells.at[0:6], diag.at[3, :, :, 0:128], sems.at[7]),
    ]
    for c in more:
        c.start()
    for c in copies + more:
        c.wait()


def cot_halo_kernel(cot, wqkv_hbm, wout_hbm, main, lat, diag, wqkv, wout, sems):
    copies = halo_copies(cot, main, lat, diag, sems)
    for i in range(4):
        rows = slice(256 * i, 256 * i + 256)
        copies.append(pltpu.make_async_copy(wqkv_hbm.at[rows], wqkv.at[rows], sems.at[5 + i]))
    copies.append(pltpu.make_async_copy(wout_hbm, wout, sems.at[9]))
    for c in copies:
        c.start()
    for c in copies:
        c.wait()


def land_column(cells, first_row, rows):
    count = rows * 12
    token = lax.broadcasted_iota(jnp.int32, (count, 128), 0)
    lane = lax.broadcasted_iota(jnp.int32, (count, 128), 1)
    cell = lax.broadcasted_iota(jnp.int32, (count, 12), 0) % 12
    pick = (cell == lax.broadcasted_iota(jnp.int32, (count, 12), 1)).astype(F32)
    wide = nn(pick, cells)
    return jnp.sum(jnp.where(lane == token // 12 + first_row, wide, 0.0), 1, keepdims=True)


def forward_kernel(
    place, bias, tok, main, lat, diag, land, wqkv,
    nrm, inv_s, qkv, attn_s, att,
):
    for w in range(WINS):
        x = window_rows(tok, main, lat, diag, w)
        centred = x - jnp.mean(x, -1, keepdims=True)
        inverse = lax.rsqrt(jnp.mean(centred * centred, -1, keepdims=True) + 1e-05)
        rows = slice(WIN * w, WIN * w + WIN)
        inv_s[rows] = jnp.broadcast_to(inverse, (WIN, 128))
        nrm[rows] = (centred * inverse).astype(BF)
    for i in range(3):
        cols = slice(HD * i, HD * i + HD)
        r = nn(nrm[...], wqkv[:, cols])
        qkv[:, cols] = (r.astype(BF) * FACTOR).astype(BF) if i == 0 else r.astype(BF)

    by_row = jnp.concatenate([land[...].astype(F32), jnp.zeros((12, 104), F32)], 1)
    own_cells = jnp.broadcast_to(by_row[6:12][:, None, :], (6, 2, 128)).reshape(12, 128)
    main_cells, lat_cells, diag_cells = (
        r[r.shape[0] - 1, :, :, 0:128].astype(F32).reshape(12, 128) for r in (main, lat, diag)
    )
    first = lax.broadcasted_iota(jnp.int32, (WIN, SLAB), 1) < HSIZE
    zero = jnp.zeros((WIN, SLAB), BF)
    for w in range(WINS):
        rows = slice(WIN * w, WIN * w + WIN)
        if w < WINS - 1:
            parts = [land_column(own_cells, 3 + 6 * w, 6), land_column(main_cells, 3 + 6 * w, 6)]
            mask = None
        else:
            parts = [
                land_column(c, at, 3)
                for c, at in ((own_cells, 21), (lat_cells, 0), (main_cells, 21), (diag_cells, 0))
            ]
            k_at = lax.broadcasted_iota(jnp.int32, (WIN, WIN), 0) % HALF
            q_at = lax.broadcasted_iota(jnp.int32, (WIN, WIN), 1) % HALF
            apart = (k_at >= HALF // 2) != (q_at >= HALF // 2)
            mask = jnp.where(jnp.logical_and(apart, place[1] == 1), FAR, 0.0)
        land_key = jnp.broadcast_to(jnp.concatenate(parts, 0), (WIN, WIN))
        for s in range(HEADS // 2):
            q = qkv[rows, SLAB * s : SLAB * s + SLAB]
            k = qkv[rows, HD + SLAB * s : HD + SLAB * s + SLAB]
            v = qkv[rows, 2 * HD + SLAB * s : 2 * HD + SLAB * s + SLAB]
            both = jnp.concatenate([jnp.where(first, k, zero), jnp.where(first, zero, k)], 0)
            sc = nt(both, q).reshape(2, WIN, WIN)
            sc = jnp.stack([sc[e] + land_key * bias[2 * s + e] for e in range(2)])
            if mask is not None:
                sc = sc + mask[None]
            ex = jnp.exp(sc - jnp.max(sc, 1, keepdims=True))
            attn = ex * (1.0 / jnp.sum(ex, 1, keepdims=True))
            attn_s[w, s] = attn
            attn_b = attn.astype(BF)
            o = jnp.where(first, tn(attn_b[0], v), tn(attn_b[1], v))
            att[rows, SLAB * s : SLAB * s + SLAB] = o.astype(BF)


def backward_kernel(
    place, cot, main, lat, diag, nrm, qkv, attn_s, att, wout,
    keep, send, dqkv, cotb, datt,
):
    core = place[0]
    for w in range(WINS):
        cotb[WIN * w : WIN * w + WIN] = window_rows(cot, main, lat, diag, w).astype(BF)
    datt[...] = nt(cotb[...], wout[...]).astype(BF)

    first = lax.broadcasted_iota(jnp.int32, (WIN, SLAB), 1) < HSIZE
    zero = jnp.zeros((WIN, SLAB), BF)
    for w in range(WINS):
        rows = slice(WIN * w, WIN * w + WIN)
        for s in range(HEADS // 2):
            q_cols, k_cols, v_cols = (
                slice(HD * i + SLAB * s, HD * i + SLAB * s + SLAB) for i in range(3)
            )
            q, k, v = qkv[rows, q_cols], qkv[rows, k_cols], qkv[rows, v_cols]
            do = datt[rows, q_cols]
            attn = attn_s[w, s]
            both = jnp.concatenate([jnp.where(first, v, zero), jnp.where(first, zero, v)], 0)
            d_attn = nt(both, do).reshape(2, WIN, WIN)
            delta = jnp.sum(attn * d_attn, 1, keepdims=True)
            d_sc = (attn * (d_attn - delta)).astype(BF)
            d_v = nn(attn.astype(BF).reshape(2 * WIN, WIN), do)
            d_k = nn(d_sc.reshape(2 * WIN, WIN), q)
            d_q = jnp.where(first, tn(d_sc[0], k), tn(d_sc[1], k))
            dqkv[rows, q_cols] = (d_q * FACTOR).astype(BF)
            dqkv[rows, k_cols] = jnp.where(first, d_k[:WIN], d_k[WIN:]).astype(BF)
            dqkv[rows, v_cols] = jnp.where(first, d_v[:WIN], d_v[WIN:]).astype(BF)

    def put(r, i, lo):
        wide = r.shape[1]
        r = (r * GRAD_SCALE).reshape(2, 4, 2, 2, 8, wide)
        cols = slice(lo, lo + wide)
        for z in range(2):
            for y in range(4):
                even = r[z, y, :, 0].reshape(16, wide)
                odd = r[z, y, :, 1].reshape(16, wide)
                at = y * 8 + 2 * i + z
                keep[at, :, cols] = jnp.where(core == 0, even, odd)
                send[at, :, cols] = jnp.where(core == 0, odd, even).astype(BF)

    for i in range(4):
        feats = slice(256 * i, 256 * i + 256)
        put(tn(nrm[:, feats], dqkv[...]), i, 0)
        put(tn(cotb[:, feats], att[...]), i, 3 * HD)


def store_rows(r, own, main, lat, diag, w):
    r = r.astype(BF)
    if w < WINS - 1:
        own[3 + 6 * w : 9 + 6 * w, 6:12] = r[:HALF].reshape(6, 6, 2, D)
        main[6 * w : 6 * w + 6] = r[HALF:].reshape(6, 6, 2, D)
    else:
        own[21:24, 6:12] = r[:36].reshape(3, 6, 2, D)
        lat[...] = r[36:72].reshape(3, 6, 2, D)
        main[18:21] = r[72:108].reshape(3, 6, 2, D)
        diag[...] = r[108:].reshape(3, 6, 2, D)


def out_kernel(att, wout, own, main, lat, diag):
    for w in range(WINS):
        rows = slice(WIN * w, WIN * w + WIN)
        store_rows(nn(att[rows], wout[...]), own, main, lat, diag, w)


def token_kernel(dqkv, wqkv, nrm, inv_s, own, main, lat, diag):
    for w in range(WINS):
        rows = slice(WIN * w, WIN * w + WIN)
        d_normed = nt(dqkv[rows], wqkv[...])
        unit = nrm[rows].astype(F32)
        d_flat = inv_s[rows, 0:1] * (
            d_normed
            - jnp.mean(d_normed, -1, keepdims=True)
            - unit * jnp.mean(d_normed * unit, -1, keepdims=True)
        )
        store_rows(d_flat, own, main, lat, diag, w)


def core_kernel(place, keep, arrived, kept, s1, s2, s3):
    for n in range(32):
        at = place[2 + n]
        total = keep[at] + arrived[at].astype(F32)
        if n < 8:
            kept[n] = total
        else:
            (s1, s2, s3)[n // 8 - 1][n % 8] = total.astype(BF)


def middle_kernel(place, keep, a1, a2, a3, kept, s1, s2, s3):
    def total(i):
        at = pl.ds(2 * i, 2)
        return keep[at] + a1[at].astype(F32) + a2[at].astype(F32) + a3[at].astype(F32)

    mine = place[34]
    kept[...] = total(mine)
    for (dy, dz), ref in zip(PEERS, (s1, s2, s3)):
        ref[...] = total(mine ^ (2 * dy + dz)).astype(BF)


def late_kernel(place, keep, a1, a2, a3, kept, s1, s2, s3, work):
    total = keep[...] + a1[...].astype(F32) + a2[...].astype(F32) + a3[...].astype(F32)
    work[...] = total.reshape(2, 2, 8, 2 * D)
    z, x = place[35], place[36]
    kept[...] = work[z, x]
    for (dz, dx), ref in zip(PEERS, (s1, s2, s3)):
        r = work[z ^ dz, x ^ dx]
        ref[...] = jnp.concatenate([r[:, :D], r[:, D:]], 0).astype(BF)


def last_kernel(keep, a1, a2, a3, out):
    total = keep[...]
    for a in (a1, a2, a3):
        r = a[...].astype(F32)
        total = total + jnp.concatenate([r[:8], r[8:]], 1)
    out[...] = total


def finish_kernel(out_own, tok_own, o_main, t_main, lat, diag, out, tok, sems):
    copies = []
    for i, (ref, main) in enumerate(((out, o_main), (tok, t_main))):
        copies += [
            pltpu.make_async_copy(main, ref.at[3:24, 0:6], sems.at[i, 0]),
            pltpu.make_async_copy(lat.at[i], ref.at[0:3, 6:12], sems.at[i, 1]),
            pltpu.make_async_copy(diag.at[i], ref.at[0:3, 0:6], sems.at[i, 2]),
        ]
    for c in copies:
        c.start()
    for c in copies:
        c.wait()


VM = pl.BlockSpec(memory_space=pltpu.VMEM)
SM = pl.BlockSpec(memory_space=pltpu.SMEM)
ANY = pl.BlockSpec(memory_space=pl.ANY)


def shaped(dims, kind=BF):
    return jax.ShapeDtypeStruct(dims, kind)


def call(body, ins, outs, scratch=(), limit=16, flops=0, name=None, aliases=None, out_spec=VM):
    return pl.pallas_call(
        body,
        in_specs=ins,
        out_specs=out_spec if isinstance(out_spec, list) else [out_spec] * len(outs),
        out_shape=outs,
        scratch_shapes=list(scratch),
        input_output_aliases=aliases or {},
        compiler_params=pltpu.CompilerParams(vmem_limit_bytes=limit * 2**20),
        cost_estimate=pl.CostEstimate(flops=flops, bytes_accessed=8 * 2**20, transcendentals=0),
        name=name,
    )


def shift(block, axis, step):
    count = lax.axis_size(axis)
    return lax.ppermute(block, axis, [(i, (i + step) % count) for i in range(count)])


def shift_both(block, step):
    count = lax.axis_size(LON)
    route = [
        (i * 2 + b, ((i + step) % count) * 2 + 1 - b) for i in range(count) for b in range(2)
    ]
    return lax.ppermute(block, ALL, route)


def flipped(at, y_bits, z_bits, xh):
    z, y, x, core, lat = at
    y2 = (((y + core) % 4) ^ y_bits) - core
    z2 = (((z + core) % 8) ^ z_bits) - core
    return (z2 % 8, y2 % 4, x ^ xh, core, lat)


def exchange(block, y_bits, z_bits, xh=0):
    route = []
    for i, at in enumerate(np.ndindex(*SIZES)):
        route.append((i, int(np.ravel_multi_index(flipped(at, y_bits, z_bits, xh), SIZES))))
    return lax.ppermute(block, ALL, route)


def places():
    rows = []
    for z, y, xh, core, lat in np.ndindex(*SIZES):
        y_label, z_label = (y + core) % 4, (z + core) % 8
        row = [core, lat]
        for dy, dz in ((0, 0),) + PEERS:
            y0, z0 = (y_label & 1) ^ dy, (z_label & 1) ^ dz
            for y1, z1, z2 in np.ndindex(2, 2, 2):
                y_true = (2 * y1 + y0 - core) % 4
                z_true = (4 * z2 + 2 * z1 + z0 - core) % 8
                row.append(y_true * 8 + z_true)
        row += [(y_label >> 1) * 2 + ((z_label >> 1) & 1), z_label >> 2, xh]
        rows.append(row)
    return np.array(rows, np.int32)


def per_device(tokens, land_mask, land_bias, qkv_weight, out_weight, cotangent):
    place = lax.dynamic_index_in_dim(jnp.asarray(places()), lax.axis_index(ALL), 0, False)
    land = land_mask.T
    full, part, edge = (24, 12, 2, D), (21, 6, 2, D), (3, 6, 2, D)
    dma = pltpu.SemaphoreType.DMA

    main, lat, diag = call(
        tok_halo_kernel,
        [VM, ANY],
        [shaped((22, 6, 2, D)), shaped((4, 6, 2, D)), shaped((4, 6, 2, D))],
        scratch=[pltpu.VMEM((12, 2, 128), BF), dma((8,))],
        out_spec=ANY,
        limit=60,
        name="tok_halo",
    )(land, tokens)
    main, lat, diag = shift(main, LON, -1), shift(lat, "lat", -1), shift_both(diag, -1)
    cot_main, cot_lat, cot_diag, wqkv, wout = call(
        cot_halo_kernel,
        [ANY] * 3,
        [shaped(part), shaped(edge), shaped(edge), shaped((D, 3 * HD)), shaped((HD, D))],
        scratch=[dma((10,))],
        out_spec=[ANY] * 3 + [VM] * 2,
        limit=16,
        name="cot_halo",
    )(cotangent, qkv_weight, out_weight)
    main, lat, diag, cot_main, cot_lat, cot_diag = lax.optimization_barrier(
        (main, lat, diag, cot_main, cot_lat, cot_diag)
    )
    cot_main = shift(cot_main, LON, -1)
    cot_lat, cot_diag = shift(cot_lat, "lat", -1), shift_both(cot_diag, -1)

    nrm, inverse, qkv, attn, att = call(
        forward_kernel,
        [SM, SM] + [VM] * 6,
        [
            shaped((TOK, D)),
            shaped((TOK, 128), F32),
            shaped((TOK, 3 * HD)),
            shaped((WINS, HEADS // 2, 2, WIN, WIN), F32),
            shaped((TOK, HD)),
        ],
        limit=16,
        flops=4 * 10**9,
        name="forward",
    )(place, land_bias, tokens, main, lat, diag, land, wqkv)

    chunks = (32, 16, 2 * D)
    keep, send, dqkv = call(
        backward_kernel,
        [SM] + [VM] * 9,
        [shaped(chunks, F32), shaped(chunks), shaped((TOK, 3 * HD))],
        scratch=[pltpu.VMEM((TOK, D), BF), pltpu.VMEM((TOK, HD), BF)],
        limit=18,
        flops=4 * 10**9,
        name="backward",
    )(place, cotangent, cot_main, cot_lat, cot_diag, nrm, qkv, attn, att, wout)

    def staged(body, scratch, rows, operands, name, sent=None):
        kept, *sends = call(
            body,
            [SM] + [VM] * len(operands),
            [shaped(rows, F32)] + [shaped(sent or rows)] * 3,
            scratch=scratch,
            limit=16,
            name=name,
        )(place, *operands)
        return kept, sends

    arrived = shift(send, "core", 1)
    send, att = lax.optimization_barrier((send, att))
    out_own, out_main, out_lat, out_diag = call(
        out_kernel,
        [VM] * 2,
        [shaped(full), shaped(part), shaped(edge), shaped(edge)],
        limit=16,
        flops=10**9,
        name="out",
    )(att, wout)
    out_main, keep = lax.optimization_barrier((out_main, keep))
    kept, sends = staged(core_kernel, [], (8, 16, 2 * D), (keep, arrived), "sum_core")
    a = [exchange(s, dy, dz) for (dy, dz), s in zip(PEERS, sends)]
    dqkv, kept = lax.optimization_barrier((dqkv, kept))
    tok_own, tok_main, tok_lat, tok_diag = call(
        token_kernel,
        [VM] * 4,
        [shaped(full), shaped(part), shaped(edge), shaped(edge)],
        limit=16,
        flops=2 * 10**9,
        name="token_grad",
    )(dqkv, wqkv, nrm, inverse)
    lat = jnp.stack([out_lat, tok_lat])
    diag = jnp.stack([out_diag, tok_diag])
    kept, sends = staged(middle_kernel, [], (2, 16, 2 * D), [kept] + a, "sum_low")
    lat, diag, kept = lax.optimization_barrier((lat, diag, kept))
    a = [exchange(s, 2 * dy, 2 * dz) for (dy, dz), s in zip(PEERS, sends)]
    kept, sends = staged(
        late_kernel,
        [pltpu.VMEM((2, 2, 8, 2 * D), F32)],
        (8, 2 * D),
        [kept] + a,
        "sum_next",
        sent=(16, D),
    )
    a = [exchange(s, 0, 4 * dz, dx) for (dz, dx), s in zip(PEERS, sends)]
    lat, diag = shift(lat, "lat", 1), shift_both(diag, 1)
    lat, diag, kept = lax.optimization_barrier((lat, diag, kept))
    (mine,) = call(last_kernel, [VM] * 4, [shaped((8, 2 * D), F32)], name="sum_last")(kept, *a)
    total = mine + shift(mine, "lat", 1)

    block_out, grad_tokens = call(
        finish_kernel,
        [ANY] * 6,
        [shaped(full), shaped(full)],
        scratch=[dma((2, 3))],
        aliases={0: 0, 1: 1},
        out_spec=ANY,
        name="assemble",
    )(out_own, tok_own, shift(out_main, LON, 1), shift(tok_main, LON, 1), lat, diag)
    return (block_out, grad_tokens, total[:, : 3 * HD], total[:, 3 * HD :].T)


def solution(mesh):
    fine = Mesh(mesh.devices.reshape(SIZES), ALL)
    grid = P("lat", LON, None, None)
    in_specs = (grid, P("lat", LON), P(), P(), P(), grid)
    out_specs = (grid, grid, P(LON, None), P(None, LON))
    return jax.shard_map(
        per_device, mesh=fine, in_specs=in_specs, out_specs=out_specs, check_vma=False
    )
```

```python
import math

import jax
import jax.numpy as jnp
import numpy as np
from jax import lax
from jax.experimental import pallas as pl
from jax.experimental.pallas import tpu as pltpu
from jax.sharding import Mesh, PartitionSpec as P

D = 1024
HEADS = 8
HSIZE = 64
HD = 512
WIN = 144
HALF = 72
WINS = 4
TOK = 576
SLAB = 128
TOKENS = 147456
GRAD_SCALE = 1.0 / math.sqrt(TOKENS)
FACTOR = HSIZE ** (-0.5)
FAR = -1e30
BF = jnp.bfloat16
F32 = jnp.float32
LON = ("z", "y", "xh", "core")
ALL = LON + ("lat",)
SIZES = (8, 4, 2, 2, 2)
PEERS = ((0, 1), (1, 0), (1, 1))


def nn(a, b):
    return lax.dot_general(a, b, (((1,), (0,)), ((), ())), preferred_element_type=F32)


def nt(a, b):
    return lax.dot_general(a, b, (((1,), (1,)), ((), ())), preferred_element_type=F32)


def tn(a, b):
    return lax.dot_general(a, b, (((0,), (0,)), ((), ())), preferred_element_type=F32)


def window_rows(own, main, lat, diag, w):
    if w < WINS - 1:
        parts = [own[3 + 6 * w : 9 + 6 * w, 6:12], main[6 * w : 6 * w + 6]]
    else:
        parts = [own[21:24, 6:12], lat[0:3], main[18:21], diag[0:3]]
    return jnp.concatenate([p.astype(F32).reshape(-1, D) for p in parts], 0)


def halo_copies(block, main, lat, diag, sems):
    return [
        pltpu.make_async_copy(block.at[3:10, 0:6], main.at[0:7], sems.at[0]),
        pltpu.make_async_copy(block.at[10:17, 0:6], main.at[7:14], sems.at[1]),
        pltpu.make_async_copy(block.at[17:24, 0:6], main.at[14:21], sems.at[2]),
        pltpu.make_async_copy(block.at[0:3, 6:12], lat.at[0:3], sems.at[3]),
        pltpu.make_async_copy(block.at[0:3, 0:6], diag.at[0:3], sems.at[4]),
    ]


def tok_halo_kernel(land, tok, main, lat, diag, main_v, lat_v, diag_v, sems):
    copies = halo_copies(tok, main_v, lat_v, diag_v, sems.at[0])
    for c in copies:
        c.start()
    by_row = jnp.concatenate([land[...].astype(F32), jnp.zeros((12, D - 24), F32)], 1)
    cells = jnp.broadcast_to(by_row[:, None, :], (12, 2, D)).astype(BF)
    main_v[21] = cells[0:6]
    lat_v[3] = cells[6:12]
    diag_v[3] = cells[0:6]
    done = []
    for i, (rows, wide, ref) in enumerate(
        (((0, 7), main_v, main), ((7, 14), main_v, main), ((14, 22), main_v, main),
         ((0, 4), lat_v, lat), ((0, 4), diag_v, diag))
    ):
        copies[i].wait()
        rows = slice(*rows)
        done.append(pltpu.make_async_copy(wide.at[rows], ref.at[rows], sems.at[1, i]))
        done[-1].start()
    for c in done:
        c.wait()


def cot_halo_kernel(cot, wqkv_hbm, wout_hbm, main, lat, diag, wqkv, wout, sems):
    copies = halo_copies(cot, main, lat, diag, sems)
    for i in range(4):
        rows = slice(256 * i, 256 * i + 256)
        copies.append(pltpu.make_async_copy(wqkv_hbm.at[rows], wqkv.at[rows], sems.at[5 + i]))
    copies.append(pltpu.make_async_copy(wout_hbm, wout, sems.at[9]))
    for c in copies:
        c.start()
    for c in copies:
        c.wait()


def land_column(cells, first_row, rows):
    count = rows * 12
    token = lax.broadcasted_iota(jnp.int32, (count, 128), 0)
    lane = lax.broadcasted_iota(jnp.int32, (count, 128), 1)
    cell = lax.broadcasted_iota(jnp.int32, (count, 12), 0) % 12
    pick = (cell == lax.broadcasted_iota(jnp.int32, (count, 12), 1)).astype(F32)
    wide = nn(pick, cells)
    return jnp.sum(jnp.where(lane == token // 12 + first_row, wide, 0.0), 1, keepdims=True)


def forward_kernel(
    bias, tok, main, lat, diag, land, wqkv,
    nrm, inv_s, qkv, attn_s, att,
):
    for w in range(WINS):
        x = window_rows(tok, main, lat, diag, w)
        centred = x - jnp.mean(x, -1, keepdims=True)
        inverse = lax.rsqrt(jnp.mean(centred * centred, -1, keepdims=True) + 1e-05)
        rows = slice(WIN * w, WIN * w + WIN)
        inv_s[rows] = jnp.broadcast_to(inverse, (WIN, 128))
        nrm[rows] = (centred * inverse).astype(BF)
    for i in range(3):
        cols = slice(HD * i, HD * i + HD)
        r = nn(nrm[...], wqkv[:, cols])
        qkv[:, cols] = (r.astype(BF) * FACTOR).astype(BF) if i == 0 else r.astype(BF)

    by_row = jnp.concatenate([land[...].astype(F32), jnp.zeros((12, 104), F32)], 1)
    own_cells = jnp.broadcast_to(by_row[6:12][:, None, :], (6, 2, 128)).reshape(12, 128)
    main_cells, lat_cells, diag_cells = (
        r[r.shape[0] - 1, :, :, 0:128].astype(F32).reshape(12, 128) for r in (main, lat, diag)
    )
    first = lax.broadcasted_iota(jnp.int32, (WIN, SLAB), 1) < HSIZE
    zero = jnp.zeros((WIN, SLAB), BF)
    for w in range(WINS):
        rows = slice(WIN * w, WIN * w + WIN)
        if w < WINS - 1:
            parts = [land_column(own_cells, 3 + 6 * w, 6), land_column(main_cells, 3 + 6 * w, 6)]
            mask = None
        else:
            parts = [
                land_column(c, at, 3)
                for c, at in ((own_cells, 21), (lat_cells, 0), (main_cells, 21), (diag_cells, 0))
            ]
            k_at = lax.broadcasted_iota(jnp.int32, (WIN, WIN), 0) % HALF
            q_at = lax.broadcasted_iota(jnp.int32, (WIN, WIN), 1) % HALF
            apart = (k_at >= HALF // 2) != (q_at >= HALF // 2)
            mask = jnp.where(jnp.logical_and(apart, lax.axis_index("lat") == 1), FAR, 0.0)
        land_key = jnp.broadcast_to(jnp.concatenate(parts, 0), (WIN, WIN))
        for s in range(HEADS // 2):
            q = qkv[rows, SLAB * s : SLAB * s + SLAB]
            k = qkv[rows, HD + SLAB * s : HD + SLAB * s + SLAB]
            v = qkv[rows, 2 * HD + SLAB * s : 2 * HD + SLAB * s + SLAB]
            both = jnp.concatenate([jnp.where(first, k, zero), jnp.where(first, zero, k)], 0)
            sc = nt(both, q).reshape(2, WIN, WIN)
            sc = jnp.stack([sc[e] + land_key * bias[2 * s + e] for e in range(2)])
            if mask is not None:
                sc = sc + mask[None]
            ex = jnp.exp(sc - jnp.max(sc, 1, keepdims=True))
            attn = ex * (1.0 / jnp.sum(ex, 1, keepdims=True))
            attn_s[w, s] = attn
            attn_b = attn.astype(BF)
            o = jnp.where(first, tn(attn_b[0], v), tn(attn_b[1], v))
            att[rows, SLAB * s : SLAB * s + SLAB] = o.astype(BF)


def backward_kernel(
    cot, main, lat, diag, nrm, qkv, attn_s, att, wout,
    keep, send, dqkv, cotb, datt,
):
    core = lax.axis_index("core")
    for w in range(WINS):
        cotb[WIN * w : WIN * w + WIN] = window_rows(cot, main, lat, diag, w).astype(BF)
    datt[...] = nt(cotb[...], wout[...]).astype(BF)

    first = lax.broadcasted_iota(jnp.int32, (WIN, SLAB), 1) < HSIZE
    zero = jnp.zeros((WIN, SLAB), BF)
    for w in range(WINS):
        rows = slice(WIN * w, WIN * w + WIN)
        for s in range(HEADS // 2):
            q_cols, k_cols, v_cols = (
                slice(HD * i + SLAB * s, HD * i + SLAB * s + SLAB) for i in range(3)
            )
            q, k, v = qkv[rows, q_cols], qkv[rows, k_cols], qkv[rows, v_cols]
            do = datt[rows, q_cols]
            attn = attn_s[w, s]
            both = jnp.concatenate([jnp.where(first, v, zero), jnp.where(first, zero, v)], 0)
            d_attn = nt(both, do).reshape(2, WIN, WIN)
            delta = jnp.sum(attn * d_attn, 1, keepdims=True)
            d_sc = (attn * (d_attn - delta)).astype(BF)
            d_v = nn(attn.astype(BF).reshape(2 * WIN, WIN), do)
            d_k = nn(d_sc.reshape(2 * WIN, WIN), q)
            d_q = jnp.where(first, tn(d_sc[0], k), tn(d_sc[1], k))
            dqkv[rows, q_cols] = (d_q * FACTOR).astype(BF)
            dqkv[rows, k_cols] = jnp.where(first, d_k[:WIN], d_k[WIN:]).astype(BF)
            dqkv[rows, v_cols] = jnp.where(first, d_v[:WIN], d_v[WIN:]).astype(BF)

    def put(r, i, lo):
        wide = r.shape[1]
        r = (r * GRAD_SCALE).reshape(2, 4, 2, 2, 8, wide)
        cols = slice(lo, lo + wide)
        for z in range(2):
            for y in range(4):
                even = r[z, y, :, 0].reshape(16, wide)
                odd = r[z, y, :, 1].reshape(16, wide)
                at = y * 8 + 2 * i + z
                keep[at, :, cols] = jnp.where(core == 0, even, odd)
                send[at, :, cols] = jnp.where(core == 0, odd, even).astype(BF)

    for i in range(4):
        feats = slice(256 * i, 256 * i + 256)
        put(tn(nrm[:, feats], dqkv[...]), i, 0)
        put(tn(cotb[:, feats], att[...]), i, 3 * HD)


def store_rows(r, own, main, lat, diag, w):
    r = r.astype(BF)
    if w < WINS - 1:
        own[3 + 6 * w : 9 + 6 * w, 6:12] = r[:HALF].reshape(6, 6, 2, D)
        main[6 * w : 6 * w + 6] = r[HALF:].reshape(6, 6, 2, D)
    else:
        own[21:24, 6:12] = r[:36].reshape(3, 6, 2, D)
        lat[...] = r[36:72].reshape(3, 6, 2, D)
        main[18:21] = r[72:108].reshape(3, 6, 2, D)
        diag[...] = r[108:].reshape(3, 6, 2, D)


def out_kernel(att, wout, own, main, lat, diag):
    for w in range(WINS):
        rows = slice(WIN * w, WIN * w + WIN)
        store_rows(nn(att[rows], wout[...]), own, main, lat, diag, w)


def token_kernel(dqkv, wqkv, nrm, inv_s, out_lat, out_diag, own, main, lat, diag):
    lat[0] = out_lat[...]
    diag[0] = out_diag[...]
    for w in range(WINS):
        rows = slice(WIN * w, WIN * w + WIN)
        d_normed = nt(dqkv[rows], wqkv[...])
        unit = nrm[rows].astype(F32)
        d_flat = inv_s[rows, 0:1] * (
            d_normed
            - jnp.mean(d_normed, -1, keepdims=True)
            - unit * jnp.mean(d_normed * unit, -1, keepdims=True)
        )
        store_rows(d_flat, own, main, lat.at[1], diag.at[1], w)


def gray(label):
    return label ^ (label >> 1)


def labels():
    core = lax.axis_index("core")
    return gray((lax.axis_index("y") + core) & 3), (lax.axis_index("z") + core) & 7, core


def core_kernel(keep, arrived, kept, s1, s2, s3):
    y_label, z_label, core = labels()
    for (dy, dz), ref in zip(((0, 0),) + PEERS, (kept, s1, s2, s3)):
        y0, z0 = (y_label & 1) ^ dy, (z_label & 1) ^ dz
        for n, (y1, z1, z2) in enumerate(np.ndindex(2, 2, 2)):
            y = (gray(2 * y1 + y0) - core + 4) & 3
            z = (4 * z2 + 2 * z1 + z0 - core + 8) & 7
            at = y * 8 + z
            ref[n] = (keep[at] + arrived[at].astype(F32)).astype(ref.dtype)


def middle_kernel(keep, a1, a2, a3, kept, s1, s2, s3):
    def total(i):
        at = pl.ds(2 * i, 2)
        return keep[at] + a1[at].astype(F32) + a2[at].astype(F32) + a3[at].astype(F32)

    y_label, z_label, _ = labels()
    mine = (y_label >> 1) * 2 + ((z_label >> 1) & 1)
    kept[...] = total(mine)
    for (dy, dz), ref in zip(PEERS, (s1, s2, s3)):
        ref[...] = total(mine ^ (2 * dy + dz)).astype(BF)


def late_kernel(keep, a1, a2, a3, kept, s1, s2, s3, work):
    total = keep[...] + a1[...].astype(F32) + a2[...].astype(F32) + a3[...].astype(F32)
    work[...] = total.reshape(2, 2, 8, 2 * D)
    _, z_label, _ = labels()
    z, x = z_label >> 2, lax.axis_index("xh")
    kept[...] = work[z, x]
    for (dz, dx), ref in zip(PEERS, (s1, s2, s3)):
        r = work[z ^ dz, x ^ dx]
        ref[...] = jnp.concatenate([r[:, :D], r[:, D:]], 0).astype(BF)


def last_kernel(keep, a1, a2, a3, out):
    total = keep[...]
    for a in (a1, a2, a3):
        r = a[...].astype(F32)
        total = total + jnp.concatenate([r[:8], r[8:]], 1)
    out[...] = total


def split_kernel(mine, other, qkv, out):
    total = mine[...] + other[...]
    qkv[...] = total[:, : 3 * HD]
    out[...] = total[:, 3 * HD :]


def finish_kernel(out_own, tok_own, o_main, t_main, lat, diag, out, tok, sems):
    copies = []
    for i, (ref, main) in enumerate(((out, o_main), (tok, t_main))):
        copies += [
            pltpu.make_async_copy(main, ref.at[3:24, 0:6], sems.at[i, 0]),
            pltpu.make_async_copy(lat.at[i], ref.at[0:3, 6:12], sems.at[i, 1]),
            pltpu.make_async_copy(diag.at[i], ref.at[0:3, 0:6], sems.at[i, 2]),
        ]
    for c in copies:
        c.start()
    for c in copies:
        c.wait()


VM = pl.BlockSpec(memory_space=pltpu.VMEM)
SM = pl.BlockSpec(memory_space=pltpu.SMEM)
ANY = pl.BlockSpec(memory_space=pl.ANY)


def shaped(dims, kind=BF):
    return jax.ShapeDtypeStruct(dims, kind)


def call(body, ins, outs, scratch=(), limit=16, flops=0, name=None, aliases=None, out_spec=VM):
    return pl.pallas_call(
        body,
        in_specs=ins,
        out_specs=out_spec if isinstance(out_spec, list) else [out_spec] * len(outs),
        out_shape=outs,
        scratch_shapes=list(scratch),
        input_output_aliases=aliases or {},
        compiler_params=pltpu.CompilerParams(vmem_limit_bytes=limit * 2**20),
        cost_estimate=pl.CostEstimate(flops=flops, bytes_accessed=8 * 2**20, transcendentals=0),
        name=name,
    )


def shift(block, axis, step):
    count = lax.axis_size(axis)
    return lax.ppermute(block, axis, [(i, (i + step) % count) for i in range(count)])


def shift_both(block, step):
    count = lax.axis_size(LON)
    route = [
        (i * 2 + b, ((i + step) % count) * 2 + 1 - b) for i in range(count) for b in range(2)
    ]
    return lax.ppermute(block, ALL, route)


def flipped(at, y_bits, z_bits, xh):
    z, y, x, core, lat = at
    y_label = gray((y + core) % 4) ^ y_bits
    y2, z2 = gray(y_label), ((z + core) % 8) ^ z_bits
    return ((z2 - core) % 8, (y2 - core) % 4, x ^ xh, core, lat)


def exchange(block, y_bits, z_bits, xh=0):
    route = []
    for i, at in enumerate(np.ndindex(*SIZES)):
        route.append((i, int(np.ravel_multi_index(flipped(at, y_bits, z_bits, xh), SIZES))))
    return lax.ppermute(block, ALL, route)


def per_device(tokens, land_mask, land_bias, qkv_weight, out_weight, cotangent):
    land = land_mask.T
    full, part, edge = (24, 12, 2, D), (21, 6, 2, D), (3, 6, 2, D)
    dma = pltpu.SemaphoreType.DMA

    main, lat, diag = call(
        tok_halo_kernel,
        [VM, ANY],
        [shaped((22, 6, 2, D)), shaped((4, 6, 2, D)), shaped((4, 6, 2, D))],
        scratch=[
            pltpu.VMEM((22, 6, 2, D), BF),
            pltpu.VMEM((4, 6, 2, D), BF),
            pltpu.VMEM((4, 6, 2, D), BF),
            dma((2, 5)),
        ],
        out_spec=ANY,
        limit=60,
        name="tok_halo",
    )(land, tokens)
    main, lat, diag = shift(main, LON, -1), shift(lat, "lat", -1), shift_both(diag, -1)
    lat, diag, cotangent = lax.optimization_barrier((lat, diag, cotangent))
    cot_main, cot_lat, cot_diag, wqkv, wout = call(
        cot_halo_kernel,
        [ANY] * 3,
        [shaped(part), shaped(edge), shaped(edge), shaped((D, 3 * HD)), shaped((HD, D))],
        scratch=[dma((10,))],
        out_spec=[ANY] * 3 + [VM] * 2,
        limit=16,
        name="cot_halo",
    )(cotangent, qkv_weight, out_weight)
    cot_main = shift(cot_main, LON, -1)
    cot_lat, cot_diag = shift(cot_lat, "lat", -1), shift_both(cot_diag, -1)

    nrm, inverse, qkv, attn, att = call(
        forward_kernel,
        [SM] + [VM] * 6,
        [
            shaped((TOK, D)),
            shaped((TOK, 128), F32),
            shaped((TOK, 3 * HD)),
            shaped((WINS, HEADS // 2, 2, WIN, WIN), F32),
            shaped((TOK, HD)),
        ],
        limit=16,
        flops=4 * 10**9,
        name="forward",
    )(land_bias, tokens, main, lat, diag, land, wqkv)

    chunks = (32, 16, 2 * D)
    keep, send, dqkv = call(
        backward_kernel,
        [VM] * 9,
        [shaped(chunks, F32), shaped(chunks), shaped((TOK, 3 * HD))],
        scratch=[pltpu.VMEM((TOK, D), BF), pltpu.VMEM((TOK, HD), BF)],
        limit=18,
        flops=4 * 10**9,
        name="backward",
    )(cotangent, cot_main, cot_lat, cot_diag, nrm, qkv, attn, att, wout)

    def staged(body, scratch, rows, operands, name, sent=None):
        kept, *sends = call(
            body,
            [VM] * len(operands),
            [shaped(rows, F32)] + [shaped(sent or rows)] * 3,
            scratch=scratch,
            limit=16,
            name=name,
        )(*operands)
        return kept, sends

    arrived = shift(send, "core", 1)
    send, att = lax.optimization_barrier((send, att))
    out_own, out_main, out_lat, out_diag = call(
        out_kernel,
        [VM] * 2,
        [shaped(full), shaped(part), shaped(edge), shaped(edge)],
        limit=16,
        flops=10**9,
        name="out",
    )(att, wout)
    out_main, keep = lax.optimization_barrier((out_main, keep))
    kept, sends = staged(core_kernel, [], (8, 16, 2 * D), (keep, arrived), "sum_core")
    a = [exchange(s, dy, dz) for (dy, dz), s in zip(PEERS, sends)]
    dqkv, kept = lax.optimization_barrier((dqkv, kept))
    tok_own, tok_main, lat, diag = call(
        token_kernel,
        [VM] * 6,
        [shaped(full), shaped(part), shaped((2,) + edge), shaped((2,) + edge)],
        limit=16,
        flops=2 * 10**9,
        name="token_grad",
    )(dqkv, wqkv, nrm, inverse, out_lat, out_diag)
    lat, diag = shift(lat, "lat", 1), shift_both(diag, 1)
    lat, diag, kept = lax.optimization_barrier((lat, diag, kept))
    kept, sends = staged(middle_kernel, [], (2, 16, 2 * D), [kept] + a, "sum_low")
    a = [exchange(s, 2 * dy, 2 * dz) for (dy, dz), s in zip(PEERS, sends)]
    kept, sends = staged(
        late_kernel,
        [pltpu.VMEM((2, 2, 8, 2 * D), F32)],
        (8, 2 * D),
        [kept] + a,
        "sum_next",
        sent=(16, D),
    )
    a = [exchange(s, 0, 4 * dz, dx) for (dz, dx), s in zip(PEERS, sends)]
    (mine,) = call(last_kernel, [VM] * 4, [shaped((8, 2 * D), F32)], name="sum_last")(kept, *a)
    grad_qkv, grad_out = call(
        split_kernel,
        [VM] * 2,
        [shaped((8, 3 * HD), F32), shaped((8, HD), F32)],
        name="sum_lat",
    )(mine, shift(mine, "lat", 1))

    block_out, grad_tokens = call(
        finish_kernel,
        [ANY] * 6,
        [shaped(full), shaped(full)],
        scratch=[dma((2, 3))],
        aliases={0: 0, 1: 1},
        out_spec=ANY,
        name="assemble",
    )(out_own, tok_own, shift(out_main, LON, 1), shift(tok_main, LON, 1), lat, diag)
    return (block_out, grad_tokens, grad_qkv, grad_out.T)


def solution(mesh):
    fine = Mesh(mesh.devices.reshape(SIZES), ALL)
    grid = P("lat", LON, None, None)
    in_specs = (grid, P("lat", LON), P(), P(), P(), grid)
    out_specs = (grid, grid, P(LON, None), P(None, LON))
    return jax.shard_map(
        per_device, mesh=fine, in_specs=in_specs, out_specs=out_specs, check_vma=False
    )
```

```python
import math

import jax
import jax.numpy as jnp
import numpy as np
from jax import lax
from jax.experimental import pallas as pl
from jax.experimental.pallas import tpu as pltpu
from jax.sharding import Mesh, PartitionSpec as P

D = 1024
HEADS = 8
HSIZE = 64
HD = 512
WIN = 144
HALF = 72
WINS = 4
TOK = 576
SLAB = 128
TOKENS = 147456
GRAD_SCALE = 1.0 / math.sqrt(TOKENS)
FACTOR = HSIZE ** (-0.5)
FAR = -1e30
BF = jnp.bfloat16
F32 = jnp.float32
LON = ("z", "y", "xh", "core")
ALL = LON + ("lat",)
SIZES = (8, 4, 2, 2, 2)
PEERS = ((0, 1), (1, 0), (1, 1))


def nn(a, b):
    return lax.dot_general(a, b, (((1,), (0,)), ((), ())), preferred_element_type=F32)


def nt(a, b):
    return lax.dot_general(a, b, (((1,), (1,)), ((), ())), preferred_element_type=F32)


def tn(a, b):
    return lax.dot_general(a, b, (((0,), (0,)), ((), ())), preferred_element_type=F32)


def window_rows(own, main, lat, diag, w):
    if w < WINS - 1:
        parts = [own[3 + 6 * w : 9 + 6 * w, 6:12], main[6 * w : 6 * w + 6]]
    else:
        parts = [own[21:24, 6:12], lat[0:3], main[18:21], diag[0:3]]
    return jnp.concatenate([p.astype(F32).reshape(-1, D) for p in parts], 0)


def halo_copies(block, main, lat, diag, sems):
    return [
        pltpu.make_async_copy(block.at[3:10, 0:6], main.at[0:7], sems.at[0]),
        pltpu.make_async_copy(block.at[10:17, 0:6], main.at[7:14], sems.at[1]),
        pltpu.make_async_copy(block.at[17:24, 0:6], main.at[14:21], sems.at[2]),
        pltpu.make_async_copy(block.at[0:3, 6:12], lat.at[0:3], sems.at[3]),
        pltpu.make_async_copy(block.at[0:3, 0:6], diag.at[0:3], sems.at[4]),
    ]


def tok_halo_kernel(land, tok, main, lat, diag, main_v, lat_v, diag_v, sems):
    copies = halo_copies(tok, main_v, lat_v, diag_v, sems.at[0])
    for c in copies:
        c.start()
    by_row = jnp.concatenate([land[...].astype(F32), jnp.zeros((12, D - 24), F32)], 1)
    cells = jnp.broadcast_to(by_row[:, None, :], (12, 2, D)).astype(BF)
    main_v[21] = cells[0:6]
    lat_v[3] = cells[6:12]
    diag_v[3] = cells[0:6]
    done = []
    for i, (rows, wide, ref) in enumerate(
        (((0, 7), main_v, main), ((7, 14), main_v, main), ((14, 22), main_v, main),
         ((0, 4), lat_v, lat), ((0, 4), diag_v, diag))
    ):
        copies[i].wait()
        rows = slice(*rows)
        done.append(pltpu.make_async_copy(wide.at[rows], ref.at[rows], sems.at[1, i]))
        done[-1].start()
    for c in done:
        c.wait()


def cot_halo_kernel(cot, main, lat, diag, sems):
    copies = halo_copies(cot, main, lat, diag, sems)
    for c in copies:
        c.start()
    for c in copies:
        c.wait()


def weights_kernel(wqkv_hbm, wout_hbm, wqkv, wout, sems):
    copies = [pltpu.make_async_copy(wout_hbm, wout, sems.at[4])]
    for i in range(4):
        rows = slice(256 * i, 256 * i + 256)
        copies.append(pltpu.make_async_copy(wqkv_hbm.at[rows], wqkv.at[rows], sems.at[i]))
    for c in copies:
        c.start()
    for c in copies:
        c.wait()


def land_column(cells, first_row, rows):
    count = rows * 12
    token = lax.broadcasted_iota(jnp.int32, (count, 128), 0)
    lane = lax.broadcasted_iota(jnp.int32, (count, 128), 1)
    cell = lax.broadcasted_iota(jnp.int32, (count, 12), 0) % 12
    pick = (cell == lax.broadcasted_iota(jnp.int32, (count, 12), 1)).astype(F32)
    wide = nn(pick, cells)
    return jnp.sum(jnp.where(lane == token // 12 + first_row, wide, 0.0), 1, keepdims=True)


def forward_kernel(
    bias, tok, main, lat, diag, land, wqkv,
    nrm, inv_s, qkv, attn_s, att,
):
    for w in range(WINS):
        x = window_rows(tok, main, lat, diag, w)
        centred = x - jnp.mean(x, -1, keepdims=True)
        inverse = lax.rsqrt(jnp.mean(centred * centred, -1, keepdims=True) + 1e-05)
        rows = slice(WIN * w, WIN * w + WIN)
        inv_s[rows] = jnp.broadcast_to(inverse, (WIN, 128))
        nrm[rows] = (centred * inverse).astype(BF)
    for i in range(3):
        cols = slice(HD * i, HD * i + HD)
        r = nn(nrm[...], wqkv[:, cols])
        qkv[:, cols] = (r.astype(BF) * FACTOR).astype(BF) if i == 0 else r.astype(BF)

    by_row = jnp.concatenate([land[...].astype(F32), jnp.zeros((12, 104), F32)], 1)
    own_cells = jnp.broadcast_to(by_row[6:12][:, None, :], (6, 2, 128)).reshape(12, 128)
    main_cells, lat_cells, diag_cells = (
        r[r.shape[0] - 1, :, :, 0:128].astype(F32).reshape(12, 128) for r in (main, lat, diag)
    )
    first = lax.broadcasted_iota(jnp.int32, (WIN, SLAB), 1) < HSIZE
    zero = jnp.zeros((WIN, SLAB), BF)
    for w in range(WINS):
        rows = slice(WIN * w, WIN * w + WIN)
        if w < WINS - 1:
            parts = [land_column(own_cells, 3 + 6 * w, 6), land_column(main_cells, 3 + 6 * w, 6)]
            mask = None
        else:
            parts = [
                land_column(c, at, 3)
                for c, at in ((own_cells, 21), (lat_cells, 0), (main_cells, 21), (diag_cells, 0))
            ]
            k_at = lax.broadcasted_iota(jnp.int32, (WIN, WIN), 0) % HALF
            q_at = lax.broadcasted_iota(jnp.int32, (WIN, WIN), 1) % HALF
            apart = (k_at >= HALF // 2) != (q_at >= HALF // 2)
            mask = jnp.where(jnp.logical_and(apart, lax.axis_index("lat") == 1), FAR, 0.0)
        land_key = jnp.broadcast_to(jnp.concatenate(parts, 0), (WIN, WIN))
        for s in range(HEADS // 2):
            q = qkv[rows, SLAB * s : SLAB * s + SLAB]
            k = qkv[rows, HD + SLAB * s : HD + SLAB * s + SLAB]
            v = qkv[rows, 2 * HD + SLAB * s : 2 * HD + SLAB * s + SLAB]
            both = jnp.concatenate([jnp.where(first, k, zero), jnp.where(first, zero, k)], 0)
            sc = nt(both, q).reshape(2, WIN, WIN)
            sc = jnp.stack([sc[e] + land_key * bias[2 * s + e] for e in range(2)])
            if mask is not None:
                sc = sc + mask[None]
            ex = jnp.exp(sc - jnp.max(sc, 1, keepdims=True))
            attn = ex * (1.0 / jnp.sum(ex, 1, keepdims=True))
            attn_s[w, s] = attn
            attn_b = attn.astype(BF)
            o = jnp.where(first, tn(attn_b[0], v), tn(attn_b[1], v))
            att[rows, SLAB * s : SLAB * s + SLAB] = o.astype(BF)


def backward_kernel(
    cot, main, lat, diag, nrm, qkv, attn_s, att, wout,
    keep, send, dqkv, cotb, datt,
):
    core = lax.axis_index("core")
    for w in range(WINS):
        cotb[WIN * w : WIN * w + WIN] = window_rows(cot, main, lat, diag, w).astype(BF)
    datt[...] = nt(cotb[...], wout[...]).astype(BF)

    first = lax.broadcasted_iota(jnp.int32, (WIN, SLAB), 1) < HSIZE
    zero = jnp.zeros((WIN, SLAB), BF)
    for w in range(WINS):
        rows = slice(WIN * w, WIN * w + WIN)
        for s in range(HEADS // 2):
            q_cols, k_cols, v_cols = (
                slice(HD * i + SLAB * s, HD * i + SLAB * s + SLAB) for i in range(3)
            )
            q, k, v = qkv[rows, q_cols], qkv[rows, k_cols], qkv[rows, v_cols]
            do = datt[rows, q_cols]
            attn = attn_s[w, s]
            both = jnp.concatenate([jnp.where(first, v, zero), jnp.where(first, zero, v)], 0)
            d_attn = nt(both, do).reshape(2, WIN, WIN)
            delta = jnp.sum(attn * d_attn, 1, keepdims=True)
            d_sc = (attn * (d_attn - delta)).astype(BF)
            d_v = nn(attn.astype(BF).reshape(2 * WIN, WIN), do)
            d_k = nn(d_sc.reshape(2 * WIN, WIN), q)
            d_q = jnp.where(first, tn(d_sc[0], k), tn(d_sc[1], k))
            dqkv[rows, q_cols] = (d_q * FACTOR).astype(BF)
            dqkv[rows, k_cols] = jnp.where(first, d_k[:WIN], d_k[WIN:]).astype(BF)
            dqkv[rows, v_cols] = jnp.where(first, d_v[:WIN], d_v[WIN:]).astype(BF)

    def put(r, i, lo):
        wide = r.shape[1]
        r = (r * GRAD_SCALE).reshape(2, 4, 2, 2, 8, wide)
        cols = slice(lo, lo + wide)
        for z in range(2):
            for y in range(4):
                even = r[z, y, :, 0].reshape(16, wide)
                odd = r[z, y, :, 1].reshape(16, wide)
                at = y * 8 + 2 * i + z
                keep[at, :, cols] = jnp.where(core == 0, even, odd)
                send[at, :, cols] = jnp.where(core == 0, odd, even).astype(BF)

    for i in range(4):
        feats = slice(256 * i, 256 * i + 256)
        put(tn(nrm[:, feats], dqkv[...]), i, 0)
        put(tn(cotb[:, feats], att[...]), i, 3 * HD)


def store_rows(r, own, main, lat, diag, w):
    r = r.astype(BF)
    if w < WINS - 1:
        own[3 + 6 * w : 9 + 6 * w, 6:12] = r[:HALF].reshape(6, 6, 2, D)
        main[6 * w : 6 * w + 6] = r[HALF:].reshape(6, 6, 2, D)
    else:
        own[21:24, 6:12] = r[:36].reshape(3, 6, 2, D)
        lat[...] = r[36:72].reshape(3, 6, 2, D)
        main[18:21] = r[72:108].reshape(3, 6, 2, D)
        diag[...] = r[108:].reshape(3, 6, 2, D)


def out_kernel(att, wout, own, main, lat, diag):
    for w in range(WINS):
        rows = slice(WIN * w, WIN * w + WIN)
        store_rows(nn(att[rows], wout[...]), own, main, lat, diag, w)


def token_kernel(dqkv, wqkv, nrm, inv_s, out_lat, out_diag, own, main, lat, diag):
    lat[0] = out_lat[...]
    diag[0] = out_diag[...]
    for w in range(WINS):
        rows = slice(WIN * w, WIN * w + WIN)
        d_normed = nt(dqkv[rows], wqkv[...])
        unit = nrm[rows].astype(F32)
        d_flat = inv_s[rows, 0:1] * (
            d_normed
            - jnp.mean(d_normed, -1, keepdims=True)
            - unit * jnp.mean(d_normed * unit, -1, keepdims=True)
        )
        store_rows(d_flat, own, main, lat.at[1], diag.at[1], w)


def gray(label):
    return label ^ (label >> 1)


def labels():
    core = lax.axis_index("core")
    return gray((lax.axis_index("y") + core) & 3), (lax.axis_index("z") + core) & 7, core


def core_kernel(keep, arrived, kept, s1, s2, s3):
    y_label, z_label, core = labels()
    for (dy, dz), ref in zip(((0, 0),) + PEERS, (kept, s1, s2, s3)):
        y0, z0 = (y_label & 1) ^ dy, (z_label & 1) ^ dz
        for n, (y1, z1, z2) in enumerate(np.ndindex(2, 2, 2)):
            y = (gray(2 * y1 + y0) - core + 4) & 3
            z = (4 * z2 + 2 * z1 + z0 - core + 8) & 7
            at = y * 8 + z
            ref[n] = (keep[at] + arrived[at].astype(F32)).astype(ref.dtype)


def middle_kernel(keep, a1, a2, a3, kept, s1, s2, s3):
    def total(i):
        at = pl.ds(2 * i, 2)
        return keep[at] + a1[at].astype(F32) + a2[at].astype(F32) + a3[at].astype(F32)

    y_label, z_label, _ = labels()
    mine = (y_label >> 1) * 2 + ((z_label >> 1) & 1)
    kept[...] = total(mine)
    for (dy, dz), ref in zip(PEERS, (s1, s2, s3)):
        ref[...] = total(mine ^ (2 * dy + dz)).astype(BF)


def late_kernel(keep, a1, a2, a3, kept, s1, s2, s3, work):
    total = keep[...] + a1[...].astype(F32) + a2[...].astype(F32) + a3[...].astype(F32)
    work[...] = total.reshape(2, 2, 8, 2 * D)
    _, z_label, _ = labels()
    z, x = z_label >> 2, lax.axis_index("xh")
    kept[...] = work[z, x]
    for (dz, dx), ref in zip(PEERS, (s1, s2, s3)):
        r = work[z ^ dz, x ^ dx]
        ref[...] = jnp.concatenate([r[:, :D], r[:, D:]], 0).astype(BF)


def last_kernel(keep, a1, a2, a3, out):
    total = keep[...]
    for a in (a1, a2, a3):
        r = a[...].astype(F32)
        total = total + jnp.concatenate([r[:8], r[8:]], 1)
    out[...] = total


def split_kernel(mine, other, qkv, out):
    total = mine[...] + other[...]
    qkv[...] = total[:, : 3 * HD]
    out[...] = total[:, 3 * HD :]


def finish_kernel(out_own, tok_own, o_main, t_main, lat, diag, out, tok, sems):
    copies = []
    for i, (ref, main) in enumerate(((out, o_main), (tok, t_main))):
        copies += [
            pltpu.make_async_copy(main, ref.at[3:24, 0:6], sems.at[i, 0]),
            pltpu.make_async_copy(lat.at[i], ref.at[0:3, 6:12], sems.at[i, 1]),
            pltpu.make_async_copy(diag.at[i], ref.at[0:3, 0:6], sems.at[i, 2]),
        ]
    for c in copies:
        c.start()
    for c in copies:
        c.wait()


VM = pl.BlockSpec(memory_space=pltpu.VMEM)
SM = pl.BlockSpec(memory_space=pltpu.SMEM)
ANY = pl.BlockSpec(memory_space=pl.ANY)


def shaped(dims, kind=BF):
    return jax.ShapeDtypeStruct(dims, kind)


def call(body, ins, outs, scratch=(), limit=16, flops=0, name=None, aliases=None, out_spec=VM):
    return pl.pallas_call(
        body,
        in_specs=ins,
        out_specs=out_spec if isinstance(out_spec, list) else [out_spec] * len(outs),
        out_shape=outs,
        scratch_shapes=list(scratch),
        input_output_aliases=aliases or {},
        compiler_params=pltpu.CompilerParams(vmem_limit_bytes=limit * 2**20),
        cost_estimate=pl.CostEstimate(flops=0, bytes_accessed=1024, transcendentals=0),
        name=name,
    )


def shift(block, axis, step):
    count = lax.axis_size(axis)
    return lax.ppermute(block, axis, [(i, (i + step) % count) for i in range(count)])


def shift_both(block, step):
    count = lax.axis_size(LON)
    route = [
        (i * 2 + b, ((i + step) % count) * 2 + 1 - b) for i in range(count) for b in range(2)
    ]
    return lax.ppermute(block, ALL, route)


def flipped(at, y_bits, z_bits, xh):
    z, y, x, core, lat = at
    y_label = gray((y + core) % 4) ^ y_bits
    y2, z2 = gray(y_label), ((z + core) % 8) ^ z_bits
    return ((z2 - core) % 8, (y2 - core) % 4, x ^ xh, core, lat)


def exchange(block, y_bits, z_bits, xh=0):
    route = []
    for i, at in enumerate(np.ndindex(*SIZES)):
        route.append((i, int(np.ravel_multi_index(flipped(at, y_bits, z_bits, xh), SIZES))))
    return lax.ppermute(block, ALL, route)


def per_device(tokens, land_mask, land_bias, qkv_weight, out_weight, cotangent):
    land = land_mask.T
    full, part, edge = (24, 12, 2, D), (21, 6, 2, D), (3, 6, 2, D)
    dma = pltpu.SemaphoreType.DMA

    main, lat, diag = call(
        tok_halo_kernel,
        [VM, ANY],
        [shaped((22, 6, 2, D)), shaped((4, 6, 2, D)), shaped((4, 6, 2, D))],
        scratch=[
            pltpu.VMEM((22, 6, 2, D), BF),
            pltpu.VMEM((4, 6, 2, D), BF),
            pltpu.VMEM((4, 6, 2, D), BF),
            dma((2, 5)),
        ],
        out_spec=ANY,
        limit=60,
        name="tok_halo",
    )(land, tokens)
    main, qkv_weight, out_weight = lax.optimization_barrier((main, qkv_weight, out_weight))
    main, lat, diag = shift(main, LON, -1), shift(lat, "lat", -1), shift_both(diag, -1)
    wqkv, wout = call(
        weights_kernel,
        [ANY] * 2,
        [shaped((D, 3 * HD)), shaped((HD, D))],
        scratch=[dma((5,))],
        limit=16,
        name="weights",
    )(qkv_weight, out_weight)
    lat, diag, cotangent, wqkv = lax.optimization_barrier((lat, diag, cotangent, wqkv))
    cot_main, cot_lat, cot_diag = call(
        cot_halo_kernel,
        [ANY],
        [shaped(part), shaped(edge), shaped(edge)],
        scratch=[dma((5,))],
        out_spec=ANY,
        limit=16,
        name="cot_halo",
    )(cotangent)
    cot_main = shift(cot_main, LON, -1)
    cot_lat, cot_diag = shift(cot_lat, "lat", -1), shift_both(cot_diag, -1)

    nrm, inverse, qkv, attn, att = call(
        forward_kernel,
        [SM] + [VM] * 6,
        [
            shaped((TOK, D)),
            shaped((TOK, 128), F32),
            shaped((TOK, 3 * HD)),
            shaped((WINS, HEADS // 2, 2, WIN, WIN), F32),
            shaped((TOK, HD)),
        ],
        limit=16,
        flops=4 * 10**9,
        name="forward",
    )(land_bias, tokens, main, lat, diag, land, wqkv)

    chunks = (32, 16, 2 * D)
    keep, send, dqkv = call(
        backward_kernel,
        [VM] * 9,
        [shaped(chunks, F32), shaped(chunks), shaped((TOK, 3 * HD))],
        scratch=[pltpu.VMEM((TOK, D), BF), pltpu.VMEM((TOK, HD), BF)],
        limit=18,
        flops=4 * 10**9,
        name="backward",
    )(cotangent, cot_main, cot_lat, cot_diag, nrm, qkv, attn, att, wout)

    def staged(body, scratch, rows, operands, name, sent=None):
        kept, *sends = call(
            body,
            [VM] * len(operands),
            [shaped(rows, F32)] + [shaped(sent or rows)] * 3,
            scratch=scratch,
            limit=16,
            name=name,
        )(*operands)
        return kept, sends

    arrived = shift(send, "core", 1)
    send, att = lax.optimization_barrier((send, att))
    out_own, out_main, out_lat, out_diag = call(
        out_kernel,
        [VM] * 2,
        [shaped(full), shaped(part), shaped(edge), shaped(edge)],
        limit=16,
        flops=10**9,
        name="out",
    )(att, wout)
    out_lat, keep = lax.optimization_barrier((out_lat, keep))
    out_main = shift(out_main, LON, 1)
    kept, sends = staged(core_kernel, [], (8, 16, 2 * D), (keep, arrived), "sum_core")
    a = [exchange(s, dy, dz) for (dy, dz), s in zip(PEERS, sends)]
    dqkv, kept, out_main = lax.optimization_barrier((dqkv, kept, out_main))
    tok_own, tok_main, lat, diag = call(
        token_kernel,
        [VM] * 6,
        [shaped(full), shaped(part), shaped((2,) + edge), shaped((2,) + edge)],
        limit=16,
        flops=2 * 10**9,
        name="token_grad",
    )(dqkv, wqkv, nrm, inverse, out_lat, out_diag)
    lat, diag = shift(lat, "lat", 1), shift_both(diag, 1)
    lat, diag, kept = lax.optimization_barrier((lat, diag, kept))
    kept, sends = staged(middle_kernel, [], (2, 16, 2 * D), [kept] + a, "sum_low")
    a = [exchange(s, 2 * dy, 2 * dz) for (dy, dz), s in zip(PEERS, sends)]
    kept, sends = staged(
        late_kernel,
        [pltpu.VMEM((2, 2, 8, 2 * D), F32)],
        (8, 2 * D),
        [kept] + a,
        "sum_next",
        sent=(16, D),
    )
    a = [exchange(s, 0, 4 * dz, dx) for (dz, dx), s in zip(PEERS, sends)]
    (mine,) = call(last_kernel, [VM] * 4, [shaped((8, 2 * D), F32)], name="sum_last")(kept, *a)
    grad_qkv, grad_out = call(
        split_kernel,
        [VM] * 2,
        [shaped((8, 3 * HD), F32), shaped((8, HD), F32)],
        name="sum_lat",
    )(mine, shift(mine, "lat", 1))

    block_out, grad_tokens = call(
        finish_kernel,
        [ANY] * 6,
        [shaped(full), shaped(full)],
        scratch=[dma((2, 3))],
        aliases={0: 0, 1: 1},
        out_spec=ANY,
        name="assemble",
    )(out_own, tok_own, out_main, shift(tok_main, LON, 1), lat, diag)
    return (block_out, grad_tokens, grad_qkv, grad_out.T)


def solution(mesh):
    fine = Mesh(mesh.devices.reshape(SIZES), ALL)
    grid = P("lat", LON, None, None)
    in_specs = (grid, P("lat", LON), P(), P(), P(), grid)
    out_specs = (grid, grid, P(LON, None), P(None, LON))
    return jax.shard_map(
        per_device, mesh=fine, in_specs=in_specs, out_specs=out_specs, check_vma=False
    )
```

```python
import math

import jax
import jax.numpy as jnp
import numpy as np
from jax import lax
from jax.experimental import pallas as pl
from jax.experimental.pallas import tpu as pltpu
from jax.sharding import Mesh, PartitionSpec as P

D = 1024
HEADS = 8
HSIZE = 64
HD = 512
WIN = 144
HALF = 72
WINS = 4
TOK = 576
SLAB = 128
TOKENS = 147456
GRAD_SCALE = 1.0 / math.sqrt(TOKENS)
FACTOR = HSIZE ** (-0.5)
FAR = -1e30
BF = jnp.bfloat16
F32 = jnp.float32
LON = ("z", "y", "xh", "core")
ALL = LON + ("lat",)
SIZES = (8, 4, 2, 2, 2)
PEERS = ((0, 1), (1, 0), (1, 1))


def nn(a, b):
    return lax.dot_general(a, b, (((1,), (0,)), ((), ())), preferred_element_type=F32)


def nt(a, b):
    return lax.dot_general(a, b, (((1,), (1,)), ((), ())), preferred_element_type=F32)


def tn(a, b):
    return lax.dot_general(a, b, (((0,), (0,)), ((), ())), preferred_element_type=F32)


def window_rows(own, main, lat, diag, w):
    if w < WINS - 1:
        parts = [own[3 + 6 * w : 9 + 6 * w, 6:12], main[6 * w : 6 * w + 6]]
    else:
        parts = [own[21:24, 6:12], lat[0:3], main[18:21], diag[0:3]]
    return jnp.concatenate([p.astype(F32).reshape(-1, D) for p in parts], 0)


def halo_copies(block, main, lat, diag, sems):
    return [
        pltpu.make_async_copy(block.at[3:10, 0:6], main.at[0:7], sems.at[0]),
        pltpu.make_async_copy(block.at[10:17, 0:6], main.at[7:14], sems.at[1]),
        pltpu.make_async_copy(block.at[17:24, 0:6], main.at[14:21], sems.at[2]),
        pltpu.make_async_copy(block.at[0:3, 6:12], lat.at[0:3], sems.at[3]),
        pltpu.make_async_copy(block.at[0:3, 0:6], diag.at[0:3], sems.at[4]),
    ]


def tok_halo_kernel(land, tok, main, lat, diag, main_v, lat_v, diag_v, sems):
    copies = halo_copies(tok, main_v, lat_v, diag_v, sems.at[0])
    for c in copies:
        c.start()
    by_row = jnp.concatenate([land[...].astype(F32), jnp.zeros((12, D - 24), F32)], 1)
    cells = jnp.broadcast_to(by_row[:, None, :], (12, 2, D)).astype(BF)
    main_v[21] = cells[0:6]
    lat_v[3] = cells[6:12]
    diag_v[3] = cells[0:6]
    done = []
    for i, (rows, wide, ref) in enumerate(
        (((0, 7), main_v, main), ((7, 14), main_v, main), ((14, 22), main_v, main),
         ((0, 4), lat_v, lat), ((0, 4), diag_v, diag))
    ):
        copies[i].wait()
        rows = slice(*rows)
        done.append(pltpu.make_async_copy(wide.at[rows], ref.at[rows], sems.at[1, i]))
        done[-1].start()
    for c in done:
        c.wait()


def cot_halo_kernel(cot, main, lat, diag, sems):
    copies = halo_copies(cot, main, lat, diag, sems)
    for c in copies:
        c.start()
    for c in copies:
        c.wait()


def weights_kernel(wqkv_hbm, wout_hbm, wqkv, wout, sems):
    copies = [pltpu.make_async_copy(wout_hbm, wout, sems.at[4])]
    for i in range(4):
        rows = slice(256 * i, 256 * i + 256)
        copies.append(pltpu.make_async_copy(wqkv_hbm.at[rows], wqkv.at[rows], sems.at[i]))
    for c in copies:
        c.start()
    for c in copies:
        c.wait()


def land_column(cells, first_row, rows):
    count = rows * 12
    token = lax.broadcasted_iota(jnp.int32, (count, 128), 0)
    lane = lax.broadcasted_iota(jnp.int32, (count, 128), 1)
    cell = lax.broadcasted_iota(jnp.int32, (count, 12), 0) % 12
    pick = (cell == lax.broadcasted_iota(jnp.int32, (count, 12), 1)).astype(F32)
    wide = nn(pick, cells)
    return jnp.sum(jnp.where(lane == token // 12 + first_row, wide, 0.0), 1, keepdims=True)


def forward_kernel(
    bias, tok, main, lat, diag, land, wqkv,
    nrm, inv_s, qkv, attn_s, att,
):
    for w in range(WINS):
        x = window_rows(tok, main, lat, diag, w)
        centred = x - jnp.mean(x, -1, keepdims=True)
        inverse = lax.rsqrt(jnp.mean(centred * centred, -1, keepdims=True) + 1e-05)
        rows = slice(WIN * w, WIN * w + WIN)
        inv_s[rows] = jnp.broadcast_to(inverse, (WIN, 128))
        nrm[rows] = (centred * inverse).astype(BF)
    for i in range(3):
        cols = slice(HD * i, HD * i + HD)
        r = nn(nrm[...], wqkv[:, cols])
        qkv[:, cols] = (r.astype(BF) * FACTOR).astype(BF) if i == 0 else r.astype(BF)

    by_row = jnp.concatenate([land[...].astype(F32), jnp.zeros((12, 104), F32)], 1)
    own_cells = jnp.broadcast_to(by_row[6:12][:, None, :], (6, 2, 128)).reshape(12, 128)
    main_cells, lat_cells, diag_cells = (
        r[r.shape[0] - 1, :, :, 0:128].astype(F32).reshape(12, 128) for r in (main, lat, diag)
    )
    first = lax.broadcasted_iota(jnp.int32, (WIN, SLAB), 1) < HSIZE
    zero = jnp.zeros((WIN, SLAB), BF)
    for w in range(WINS):
        rows = slice(WIN * w, WIN * w + WIN)
        if w < WINS - 1:
            parts = [land_column(own_cells, 3 + 6 * w, 6), land_column(main_cells, 3 + 6 * w, 6)]
            mask = None
        else:
            parts = [
                land_column(c, at, 3)
                for c, at in ((own_cells, 21), (lat_cells, 0), (main_cells, 21), (diag_cells, 0))
            ]
            k_at = lax.broadcasted_iota(jnp.int32, (WIN, WIN), 0) % HALF
            q_at = lax.broadcasted_iota(jnp.int32, (WIN, WIN), 1) % HALF
            apart = (k_at >= HALF // 2) != (q_at >= HALF // 2)
            mask = jnp.where(jnp.logical_and(apart, lax.axis_index("lat") == 1), FAR, 0.0)
        land_key = jnp.broadcast_to(jnp.concatenate(parts, 0), (WIN, WIN))
        for s in range(HEADS // 2):
            q = qkv[rows, SLAB * s : SLAB * s + SLAB]
            k = qkv[rows, HD + SLAB * s : HD + SLAB * s + SLAB]
            v = qkv[rows, 2 * HD + SLAB * s : 2 * HD + SLAB * s + SLAB]
            both = jnp.concatenate([jnp.where(first, k, zero), jnp.where(first, zero, k)], 0)
            sc = nt(both, q).reshape(2, WIN, WIN)
            sc = jnp.stack([sc[e] + land_key * bias[2 * s + e] for e in range(2)])
            if mask is not None:
                sc = sc + mask[None]
            ex = jnp.exp(sc - jnp.max(sc, 1, keepdims=True))
            attn = ex * (1.0 / jnp.sum(ex, 1, keepdims=True))
            attn_s[w, s] = attn
            attn_b = attn.astype(BF)
            o = jnp.where(first, tn(attn_b[0], v), tn(attn_b[1], v))
            att[rows, SLAB * s : SLAB * s + SLAB] = o.astype(BF)


def backward_kernel(
    cot, main, lat, diag, nrm, qkv, attn_s, att, wout,
    keep, send, dqkv, cotb, datt,
):
    core = lax.axis_index("core")
    for w in range(WINS):
        cotb[WIN * w : WIN * w + WIN] = window_rows(cot, main, lat, diag, w).astype(BF)
    datt[...] = nt(cotb[...], wout[...]).astype(BF)

    first = lax.broadcasted_iota(jnp.int32, (WIN, SLAB), 1) < HSIZE
    zero = jnp.zeros((WIN, SLAB), BF)
    for w in range(WINS):
        rows = slice(WIN * w, WIN * w + WIN)
        for s in range(HEADS // 2):
            q_cols, k_cols, v_cols = (
                slice(HD * i + SLAB * s, HD * i + SLAB * s + SLAB) for i in range(3)
            )
            q, k, v = qkv[rows, q_cols], qkv[rows, k_cols], qkv[rows, v_cols]
            do = datt[rows, q_cols]
            attn = attn_s[w, s]
            both = jnp.concatenate([jnp.where(first, v, zero), jnp.where(first, zero, v)], 0)
            d_attn = nt(both, do).reshape(2, WIN, WIN)
            delta = jnp.sum(attn * d_attn, 1, keepdims=True)
            d_sc = (attn * (d_attn - delta)).astype(BF)
            d_v = nn(attn.astype(BF).reshape(2 * WIN, WIN), do)
            d_k = nn(d_sc.reshape(2 * WIN, WIN), q)
            d_q = jnp.where(first, tn(d_sc[0], k), tn(d_sc[1], k))
            dqkv[rows, q_cols] = (d_q * FACTOR).astype(BF)
            dqkv[rows, k_cols] = jnp.where(first, d_k[:WIN], d_k[WIN:]).astype(BF)
            dqkv[rows, v_cols] = jnp.where(first, d_v[:WIN], d_v[WIN:]).astype(BF)

    def put(r, i, lo):
        wide = r.shape[1]
        r = (r * GRAD_SCALE).reshape(2, 4, 2, 2, 8, wide)
        cols = slice(lo, lo + wide)
        for z in range(2):
            for y in range(4):
                even = r[z, y, :, 0].reshape(16, wide)
                odd = r[z, y, :, 1].reshape(16, wide)
                at = y * 8 + 2 * i + z
                keep[at, :, cols] = jnp.where(core == 0, even, odd)
                send[at, :, cols] = jnp.where(core == 0, odd, even).astype(BF)

    for i in range(4):
        feats = slice(256 * i, 256 * i + 256)
        put(tn(nrm[:, feats], dqkv[...]), i, 0)
        put(tn(cotb[:, feats], att[...]), i, 3 * HD)


def store_rows(r, own, main, lat, w):
    r = r.astype(BF)
    if w < WINS - 1:
        own[3 + 6 * w : 9 + 6 * w, 6:12] = r[:HALF].reshape(6, 6, 2, D)
        main[6 * w : 6 * w + 6] = r[HALF:].reshape(6, 6, 2, D)
    else:
        own[21:24, 6:12] = r[:36].reshape(3, 6, 2, D)
        lat[...] = r[36:72].reshape(3, 6, 2, D)
        main[18:21] = r[72:108].reshape(3, 6, 2, D)
        main[21:24] = r[108:].reshape(3, 6, 2, D)


def out_kernel(att, wout, own, main, lat):
    for w in range(WINS):
        rows = slice(WIN * w, WIN * w + WIN)
        store_rows(nn(att[rows], wout[...]), own, main, lat, w)


def token_kernel(dqkv, wqkv, nrm, inv_s, own, main, lat):
    for w in range(WINS):
        rows = slice(WIN * w, WIN * w + WIN)
        d_normed = nt(dqkv[rows], wqkv[...])
        unit = nrm[rows].astype(F32)
        d_flat = inv_s[rows, 0:1] * (
            d_normed
            - jnp.mean(d_normed, -1, keepdims=True)
            - unit * jnp.mean(d_normed * unit, -1, keepdims=True)
        )
        store_rows(d_flat, own, main, lat, w)


def gray(label):
    return label ^ (label >> 1)


def labels():
    core = lax.axis_index("core")
    return gray((lax.axis_index("y") + core) & 3), (lax.axis_index("z") + core) & 7, core


def core_kernel(keep, arrived, kept, s1, s2, s3):
    y_label, z_label, core = labels()
    for (dy, dz), ref in zip(((0, 0),) + PEERS, (kept, s1, s2, s3)):
        y0, z0 = (y_label & 1) ^ dy, (z_label & 1) ^ dz
        for n, (y1, z1, z2) in enumerate(np.ndindex(2, 2, 2)):
            y = (gray(2 * y1 + y0) - core + 4) & 3
            z = (4 * z2 + 2 * z1 + z0 - core + 8) & 7
            at = y * 8 + z
            ref[n] = (keep[at] + arrived[at].astype(F32)).astype(ref.dtype)


def middle_kernel(keep, a1, a2, a3, kept, s1, s2, s3):
    def total(i):
        at = pl.ds(2 * i, 2)
        return keep[at] + a1[at].astype(F32) + a2[at].astype(F32) + a3[at].astype(F32)

    y_label, z_label, _ = labels()
    mine = (y_label >> 1) * 2 + ((z_label >> 1) & 1)
    kept[...] = total(mine)
    for (dy, dz), ref in zip(PEERS, (s1, s2, s3)):
        ref[...] = total(mine ^ (2 * dy + dz)).astype(BF)


def late_kernel(keep, a1, a2, a3, kept, send, work):
    work[...] = keep[...] + a1[...].astype(F32) + a2[...].astype(F32) + a3[...].astype(F32)
    _, z_label, _ = labels()
    z = z_label >> 2
    kept[...] = work[z]
    send[...] = work[z ^ 1].astype(BF)


def ring_kernel(keep, arrived, kept, send, work):
    total = keep[...] + arrived[...].astype(F32)
    work[...] = total.reshape(2, 8, 2 * D)
    x = lax.axis_index("xh")
    for ref, at in ((kept, x), (send, x ^ 1)):
        r = work[at]
        ref[...] = jnp.concatenate([r[:, :D], r[:, D:]], 0).astype(BF)


def last_kernel(keep, a1, a2, a3, qkv, out):
    wide = [r[...].astype(F32) for r in (keep, a1, a2, a3)]
    total = (wide[0] + wide[1]) + (wide[2] + wide[3])
    qkv[...] = jnp.concatenate([total[:8], total[8:, :HD]], 1)
    out[...] = total[8:, HD:]


def gather_kernel(out_own, tok_own, o_main, t_main, o_lat, t_lat, out, tok, lat, sems):
    copies = []
    for i, (ref, main, edge) in enumerate(((out, o_main, o_lat), (tok, t_main, t_lat))):
        copies += [
            pltpu.make_async_copy(main.at[0:21], ref.at[3:24, 0:6], sems.at[i, 0]),
            pltpu.make_async_copy(main.at[21:24], lat.at[i, :, 0:6], sems.at[i, 1]),
            pltpu.make_async_copy(edge, lat.at[i, :, 6:12], sems.at[i, 2]),
        ]
    for c in copies:
        c.start()
    for c in copies:
        c.wait()


def finish_kernel(out_part, tok_part, lat, out, tok, sems):
    copies = [
        pltpu.make_async_copy(lat.at[i], ref.at[0:3], sems.at[i])
        for i, ref in enumerate((out, tok))
    ]
    for c in copies:
        c.start()
    for c in copies:
        c.wait()


VM = pl.BlockSpec(memory_space=pltpu.VMEM)
SM = pl.BlockSpec(memory_space=pltpu.SMEM)
ANY = pl.BlockSpec(memory_space=pl.ANY)


def shaped(dims, kind=BF):
    return jax.ShapeDtypeStruct(dims, kind)


def call(body, ins, outs, scratch=(), limit=16, flops=0, name=None, aliases=None, out_spec=VM, moved=8):
    return pl.pallas_call(
        body,
        in_specs=ins,
        out_specs=out_spec if isinstance(out_spec, list) else [out_spec] * len(outs),
        out_shape=outs,
        scratch_shapes=list(scratch),
        input_output_aliases=aliases or {},
        compiler_params=pltpu.CompilerParams(vmem_limit_bytes=limit * 2**20),
        cost_estimate=pl.CostEstimate(flops=0, bytes_accessed=moved * 2**20, transcendentals=0),
        name=name,
    )


def shift(block, axis, step):
    count = lax.axis_size(axis)
    return lax.ppermute(block, axis, [(i, (i + step) % count) for i in range(count)])


def shift_both(block, step):
    count = lax.axis_size(LON)
    route = [
        (i * 2 + b, ((i + step) % count) * 2 + 1 - b) for i in range(count) for b in range(2)
    ]
    return lax.ppermute(block, ALL, route)


def flipped(at, y_bits, z_bits, xh):
    z, y, x, core, lat = at
    y_label = gray((y + core) % 4) ^ y_bits
    y2, z2 = gray(y_label), ((z + core) % 8) ^ z_bits
    return ((z2 - core) % 8, (y2 - core) % 4, x ^ xh, core, lat)


def shift_both_x(block):
    return lax.ppermute(block, ("xh", "lat"), [(i, 3 - i) for i in range(4)])


def exchange(block, y_bits, z_bits, xh=0):
    route = []
    for i, at in enumerate(np.ndindex(*SIZES)):
        route.append((i, int(np.ravel_multi_index(flipped(at, y_bits, z_bits, xh), SIZES))))
    return lax.ppermute(block, ALL, route)


def per_device(tokens, land_mask, land_bias, qkv_weight, out_weight, cotangent):
    land = land_mask.T
    full, part, edge = (24, 12, 2, D), (21, 6, 2, D), (3, 6, 2, D)
    dma = pltpu.SemaphoreType.DMA

    main, lat, diag = call(
        tok_halo_kernel,
        [VM, ANY],
        [shaped((22, 6, 2, D)), shaped((4, 6, 2, D)), shaped((4, 6, 2, D))],
        scratch=[
            pltpu.VMEM((22, 6, 2, D), BF),
            pltpu.VMEM((4, 6, 2, D), BF),
            pltpu.VMEM((4, 6, 2, D), BF),
            dma((2, 5)),
        ],
        out_spec=ANY,
        limit=60,
        name="tok_halo",
    )(land, tokens)
    main, qkv_weight, out_weight = lax.optimization_barrier((main, qkv_weight, out_weight))
    main, lat, diag = shift(main, LON, -1), shift(lat, "lat", -1), shift_both(diag, -1)
    wqkv, wout = call(
        weights_kernel,
        [ANY] * 2,
        [shaped((D, 3 * HD)), shaped((HD, D))],
        scratch=[dma((5,))],
        limit=16,
        name="weights",
    )(qkv_weight, out_weight)
    lat, diag, cotangent, wqkv = lax.optimization_barrier((lat, diag, cotangent, wqkv))
    cot_main, cot_lat, cot_diag = call(
        cot_halo_kernel,
        [ANY],
        [shaped(part), shaped(edge), shaped(edge)],
        scratch=[dma((5,))],
        out_spec=ANY,
        limit=16,
        name="cot_halo",
    )(cotangent)
    cot_main = shift(cot_main, LON, -1)
    cot_lat, cot_diag = shift(cot_lat, "lat", -1), shift_both(cot_diag, -1)

    nrm, inverse, qkv, attn, att = call(
        forward_kernel,
        [SM] + [VM] * 6,
        [
            shaped((TOK, D)),
            shaped((TOK, 128), F32),
            shaped((TOK, 3 * HD)),
            shaped((WINS, HEADS // 2, 2, WIN, WIN), F32),
            shaped((TOK, HD)),
        ],
        limit=16,
        flops=4 * 10**9,
        name="forward",
    )(land_bias, tokens, main, lat, diag, land, wqkv)

    chunks = (32, 16, 2 * D)
    keep, send, dqkv = call(
        backward_kernel,
        [VM] * 9,
        [shaped(chunks, F32), shaped(chunks), shaped((TOK, 3 * HD))],
        scratch=[pltpu.VMEM((TOK, D), BF), pltpu.VMEM((TOK, HD), BF)],
        limit=18,
        flops=4 * 10**9,
        name="backward",
    )(cotangent, cot_main, cot_lat, cot_diag, nrm, qkv, attn, att, wout)

    def summed(body, operands, rows, sent, sends, name, scratch=(), kind=F32, moved=8):
        kept, *rest = call(
            body,
            [VM] * len(operands),
            [shaped(rows, kind)] + [shaped(sent)] * sends,
            scratch=scratch,
            limit=16,
            name=name,
            moved=moved,
        )(*operands)
        return kept, rest

    arrived = shift(send, "core", 1)
    whole = (24, 6, 2, D)
    send, att = lax.optimization_barrier((send, att))
    out_own, out_main, out_lat = call(
        out_kernel,
        [VM] * 2,
        [shaped(full), shaped(whole), shaped(edge)],
        limit=16,
        flops=10**9,
        name="out",
    )(att, wout)
    out_lat, keep = lax.optimization_barrier((out_lat, keep))
    out_main = shift(out_main, LON, 1)
    eighth, small = (8, 16, 2 * D), (2, 16, 2 * D)
    kept, sends = summed(core_kernel, (keep, arrived), eighth, eighth, 3, "sum_core")
    a = [exchange(s, dy, dz) for (dy, dz), s in zip(PEERS, sends)]
    dqkv, kept = lax.optimization_barrier((dqkv, kept))
    tok_own, tok_main, tok_lat = call(
        token_kernel,
        [VM] * 4,
        [shaped(full), shaped(whole), shaped(edge)],
        limit=16,
        flops=2 * 10**9,
        name="token_grad",
    )(dqkv, wqkv, nrm, inverse)
    tok_main = shift(tok_main, LON, 1)
    out_main, kept = lax.optimization_barrier((out_main, kept))
    kept, sends = summed(middle_kernel, [kept] + a, small, small, 3, "sum_low")
    a = [exchange(s, 2 * dy, 2 * dz) for (dy, dz), s in zip(PEERS, sends)]
    kept, (s,) = summed(
        late_kernel, [kept] + a, small[1:], small[1:], 1, "sum_next", [pltpu.VMEM(small, F32)]
    )
    out_own, kept = lax.optimization_barrier((out_own, kept))
    block_out, grad_tokens, lat = call(
        gather_kernel,
        [ANY] * 6,
        [shaped(full), shaped(full), shaped((2, 3, 12, 2, D))],
        scratch=[dma((2, 3))],
        aliases={0: 0, 1: 1},
        out_spec=ANY,
        name="gather",
    )(out_own, tok_own, out_main, tok_main, out_lat, tok_lat)
    kept, (s,) = summed(
        ring_kernel,
        (kept, exchange(s, 0, 4)),
        (16, D),
        (16, D),
        1,
        "sum_z",
        [pltpu.VMEM((2, 8, 2 * D), F32)],
        BF,
        64,
    )
    a = [shift(kept, "lat", 1), shift(s, "xh", 1), shift_both_x(s)]
    grad_qkv, grad_out = call(
        last_kernel,
        [VM] * 4,
        [shaped((8, 3 * HD), F32), shaped((8, HD), F32)],
        name="sum_x",
    )(kept, *a)
    block_out, grad_tokens = call(
        finish_kernel,
        [ANY] * 3,
        [shaped(full), shaped(full)],
        scratch=[dma((2,))],
        aliases={0: 0, 1: 1},
        out_spec=ANY,
        name="assemble",
    )(block_out, grad_tokens, shift(lat, "lat", 1))
    return (block_out, grad_tokens, grad_qkv, grad_out.T)


def solution(mesh):
    fine = Mesh(mesh.devices.reshape(SIZES), ALL)
    grid = P("lat", LON, None, None)
    in_specs = (grid, P("lat", LON), P(), P(), P(), grid)
    out_specs = (grid, grid, P(LON, None), P(None, LON))
    return jax.shard_map(
        per_device, mesh=fine, in_specs=in_specs, out_specs=out_specs, check_vma=False
    )
```

```python
import math

import jax
import jax.numpy as jnp
import numpy as np
from jax import lax
from jax.experimental import pallas as pl
from jax.experimental.pallas import tpu as pltpu
from jax.sharding import Mesh, PartitionSpec as P

D = 1024
HEADS = 8
HSIZE = 64
HD = 512
WIN = 144
HALF = 72
WINS = 4
TOK = 576
SLAB = 128
TOKENS = 147456
GRAD_SCALE = 1.0 / math.sqrt(TOKENS)
FACTOR = HSIZE ** (-0.5)
FAR = -1e30
BF = jnp.bfloat16
F32 = jnp.float32
LON = ("z", "y", "xh", "core")
ALL = LON + ("lat",)
SIZES = (8, 4, 2, 2, 2)
PEERS = ((0, 1), (1, 0), (1, 1))


def nn(a, b):
    return lax.dot_general(a, b, (((1,), (0,)), ((), ())), preferred_element_type=F32)


def nt(a, b):
    return lax.dot_general(a, b, (((1,), (1,)), ((), ())), preferred_element_type=F32)


def tn(a, b):
    return lax.dot_general(a, b, (((0,), (0,)), ((), ())), preferred_element_type=F32)


def window_rows(own, main, lat, diag, w):
    if w < WINS - 1:
        parts = [own[3 + 6 * w : 9 + 6 * w, 6:12], main[6 * w : 6 * w + 6]]
    else:
        parts = [own[21:24, 6:12], lat[0:3], main[18:21], diag[0:3]]
    return jnp.concatenate([p.astype(F32).reshape(-1, D) for p in parts], 0)


def halo_copies(block, main, lat, diag, sems):
    return [
        pltpu.make_async_copy(block.at[3:10, 0:6], main.at[0:7], sems.at[0]),
        pltpu.make_async_copy(block.at[10:17, 0:6], main.at[7:14], sems.at[1]),
        pltpu.make_async_copy(block.at[17:24, 0:6], main.at[14:21], sems.at[2]),
        pltpu.make_async_copy(block.at[0:3, 6:12], lat.at[0:3], sems.at[3]),
        pltpu.make_async_copy(block.at[0:3, 0:6], diag.at[0:3], sems.at[4]),
    ]


def tok_halo_kernel(land, tok, main, lat, diag, main_v, lat_v, diag_v, sems):
    copies = halo_copies(tok, main_v, lat_v, diag_v, sems.at[0])
    for c in copies:
        c.start()
    by_row = jnp.concatenate([land[...].astype(F32), jnp.zeros((12, D - 24), F32)], 1)
    cells = jnp.broadcast_to(by_row[:, None, :], (12, 2, D)).astype(BF)
    main_v[21] = cells[0:6]
    lat_v[3] = cells[6:12]
    diag_v[3] = cells[0:6]
    done = []
    for i, (rows, wide, ref) in enumerate(
        (((0, 7), main_v, main), ((7, 14), main_v, main), ((14, 22), main_v, main),
         ((0, 4), lat_v, lat), ((0, 4), diag_v, diag))
    ):
        copies[i].wait()
        rows = slice(*rows)
        done.append(pltpu.make_async_copy(wide.at[rows], ref.at[rows], sems.at[1, i]))
        done[-1].start()
    for c in done:
        c.wait()


def cot_halo_kernel(cot, main, lat, diag, sems):
    copies = halo_copies(cot, main, lat, diag, sems)
    for c in copies:
        c.start()
    for c in copies:
        c.wait()


def weights_kernel(wqkv_hbm, wout_hbm, wqkv, wout, sems):
    copies = [pltpu.make_async_copy(wout_hbm, wout, sems.at[4])]
    for i in range(4):
        rows = slice(256 * i, 256 * i + 256)
        copies.append(pltpu.make_async_copy(wqkv_hbm.at[rows], wqkv.at[rows], sems.at[i]))
    for c in copies:
        c.start()
    for c in copies:
        c.wait()


def land_column(cells, first_row, rows):
    count = rows * 12
    token = lax.broadcasted_iota(jnp.int32, (count, 128), 0)
    lane = lax.broadcasted_iota(jnp.int32, (count, 128), 1)
    cell = lax.broadcasted_iota(jnp.int32, (count, 12), 0) % 12
    pick = (cell == lax.broadcasted_iota(jnp.int32, (count, 12), 1)).astype(F32)
    wide = nn(pick, cells)
    return jnp.sum(jnp.where(lane == token // 12 + first_row, wide, 0.0), 1, keepdims=True)


def forward_kernel(
    bias, tok, main, lat, diag, land, wqkv,
    nrm, inv_s, qkv, attn_s, att,
):
    for w in range(WINS):
        x = window_rows(tok, main, lat, diag, w)
        centred = x - jnp.mean(x, -1, keepdims=True)
        inverse = lax.rsqrt(jnp.mean(centred * centred, -1, keepdims=True) + 1e-05)
        rows = slice(WIN * w, WIN * w + WIN)
        inv_s[rows] = jnp.broadcast_to(inverse, (WIN, 128))
        nrm[rows] = (centred * inverse).astype(BF)
    for i in range(3):
        cols = slice(HD * i, HD * i + HD)
        r = nn(nrm[...], wqkv[:, cols])
        qkv[:, cols] = (r.astype(BF) * FACTOR).astype(BF) if i == 0 else r.astype(BF)

    by_row = jnp.concatenate([land[...].astype(F32), jnp.zeros((12, 104), F32)], 1)
    own_cells = jnp.broadcast_to(by_row[6:12][:, None, :], (6, 2, 128)).reshape(12, 128)
    main_cells, lat_cells, diag_cells = (
        r[r.shape[0] - 1, :, :, 0:128].astype(F32).reshape(12, 128) for r in (main, lat, diag)
    )
    first = lax.broadcasted_iota(jnp.int32, (WIN, SLAB), 1) < HSIZE
    zero = jnp.zeros((WIN, SLAB), BF)
    for w in range(WINS):
        rows = slice(WIN * w, WIN * w + WIN)
        if w < WINS - 1:
            parts = [land_column(own_cells, 3 + 6 * w, 6), land_column(main_cells, 3 + 6 * w, 6)]
            mask = None
        else:
            parts = [
                land_column(c, at, 3)
                for c, at in ((own_cells, 21), (lat_cells, 0), (main_cells, 21), (diag_cells, 0))
            ]
            k_at = lax.broadcasted_iota(jnp.int32, (WIN, WIN), 0) % HALF
            q_at = lax.broadcasted_iota(jnp.int32, (WIN, WIN), 1) % HALF
            apart = (k_at >= HALF // 2) != (q_at >= HALF // 2)
            mask = jnp.where(jnp.logical_and(apart, lax.axis_index("lat") == 1), FAR, 0.0)
        land_key = jnp.broadcast_to(jnp.concatenate(parts, 0), (WIN, WIN))
        for s in range(HEADS // 2):
            q = qkv[rows, SLAB * s : SLAB * s + SLAB]
            k = qkv[rows, HD + SLAB * s : HD + SLAB * s + SLAB]
            v = qkv[rows, 2 * HD + SLAB * s : 2 * HD + SLAB * s + SLAB]
            both = jnp.concatenate([jnp.where(first, k, zero), jnp.where(first, zero, k)], 0)
            sc = nt(both, q).reshape(2, WIN, WIN)
            sc = jnp.stack([sc[e] + land_key * bias[2 * s + e] for e in range(2)])
            if mask is not None:
                sc = sc + mask[None]
            ex = jnp.exp(sc - jnp.max(sc, 1, keepdims=True))
            attn = ex * (1.0 / jnp.sum(ex, 1, keepdims=True))
            attn_s[w, s] = attn
            attn_b = attn.astype(BF)
            o = jnp.where(first, tn(attn_b[0], v), tn(attn_b[1], v))
            att[rows, SLAB * s : SLAB * s + SLAB] = o.astype(BF)


def backward_kernel(
    cot, main, lat, diag, nrm, qkv, attn_s, att, wout,
    keep, send, dqkv, cotb, datt,
):
    core = lax.axis_index("core")
    for w in range(WINS):
        cotb[WIN * w : WIN * w + WIN] = window_rows(cot, main, lat, diag, w).astype(BF)
    datt[...] = nt(cotb[...], wout[...]).astype(BF)

    first = lax.broadcasted_iota(jnp.int32, (WIN, SLAB), 1) < HSIZE
    zero = jnp.zeros((WIN, SLAB), BF)
    for w in range(WINS):
        rows = slice(WIN * w, WIN * w + WIN)
        for s in range(HEADS // 2):
            q_cols, k_cols, v_cols = (
                slice(HD * i + SLAB * s, HD * i + SLAB * s + SLAB) for i in range(3)
            )
            q, k, v = qkv[rows, q_cols], qkv[rows, k_cols], qkv[rows, v_cols]
            do = datt[rows, q_cols]
            attn = attn_s[w, s]
            both = jnp.concatenate([jnp.where(first, v, zero), jnp.where(first, zero, v)], 0)
            d_attn = nt(both, do).reshape(2, WIN, WIN)
            delta = jnp.sum(attn * d_attn, 1, keepdims=True)
            d_sc = (attn * (d_attn - delta)).astype(BF)
            d_v = nn(attn.astype(BF).reshape(2 * WIN, WIN), do)
            d_k = nn(d_sc.reshape(2 * WIN, WIN), q)
            d_q = jnp.where(first, tn(d_sc[0], k), tn(d_sc[1], k))
            dqkv[rows, q_cols] = (d_q * FACTOR).astype(BF)
            dqkv[rows, k_cols] = jnp.where(first, d_k[:WIN], d_k[WIN:]).astype(BF)
            dqkv[rows, v_cols] = jnp.where(first, d_v[:WIN], d_v[WIN:]).astype(BF)

    def put(r, i, lo):
        wide = r.shape[1]
        r = (r * GRAD_SCALE).reshape(2, 4, 2, 2, 8, wide)
        cols = slice(lo, lo + wide)
        for z in range(2):
            for y in range(4):
                even = r[z, y, :, 0].reshape(16, wide)
                odd = r[z, y, :, 1].reshape(16, wide)
                at = y * 8 + 2 * i + z
                keep[at, :, cols] = jnp.where(core == 0, even, odd)
                send[at, :, cols] = jnp.where(core == 0, odd, even).astype(BF)

    for i in range(4):
        feats = slice(256 * i, 256 * i + 256)
        put(tn(nrm[:, feats], dqkv[...]), i, 0)
        put(tn(cotb[:, feats], att[...]), i, 3 * HD)


def store_rows(r, own, main, lat, w):
    r = r.astype(BF)
    if w < WINS - 1:
        own[3 + 6 * w : 9 + 6 * w, 6:12] = r[:HALF].reshape(6, 6, 2, D)
        main[6 * w : 6 * w + 6] = r[HALF:].reshape(6, 6, 2, D)
    else:
        own[21:24, 6:12] = r[:36].reshape(3, 6, 2, D)
        lat[...] = r[36:72].reshape(3, 6, 2, D)
        main[18:21] = r[72:108].reshape(3, 6, 2, D)
        main[21:24] = r[108:].reshape(3, 6, 2, D)


def out_kernel(att, wout, own, main, lat):
    for w in range(WINS):
        rows = slice(WIN * w, WIN * w + WIN)
        store_rows(nn(att[rows], wout[...]), own, main, lat, w)


def token_kernel(dqkv, wqkv, nrm, inv_s, own, main, lat):
    for w in range(WINS):
        rows = slice(WIN * w, WIN * w + WIN)
        d_normed = nt(dqkv[rows], wqkv[...])
        unit = nrm[rows].astype(F32)
        d_flat = inv_s[rows, 0:1] * (
            d_normed
            - jnp.mean(d_normed, -1, keepdims=True)
            - unit * jnp.mean(d_normed * unit, -1, keepdims=True)
        )
        store_rows(d_flat, own, main, lat, w)


def gray(label):
    return label ^ (label >> 1)


def labels():
    core = lax.axis_index("core")
    return gray((lax.axis_index("y") + core) & 3), (lax.axis_index("z") + core) & 7, core


def core_kernel(keep, arrived, kept, s1, s2, s3):
    y_label, z_label, core = labels()
    for (dy, dz), ref in zip(((0, 0),) + PEERS, (kept, s1, s2, s3)):
        y0, z0 = (y_label & 1) ^ dy, (z_label & 1) ^ dz
        for n, (z2, z1, y1) in enumerate(np.ndindex(2, 2, 2)):
            y = (gray(2 * y1 + y0) - core + 4) & 3
            z = (4 * z2 + 2 * z1 + z0 - core + 8) & 7
            at = y * 8 + z
            ref[n] = (keep[at] + arrived[at].astype(F32)).astype(ref.dtype)


def middle_kernel(keep, a1, a2, a3, kept, s1, s2, s3):
    def total(i):
        at = pl.ds(2 * i, 2)
        return keep[at] + a1[at].astype(F32) + a2[at].astype(F32) + a3[at].astype(F32)

    _, z_label, _ = labels()
    mine = z_label >> 1
    kept[...] = total(mine)
    for n, ref in enumerate((s1, s2, s3)):
        ref[...] = total(mine ^ (n + 1)).astype(BF)


def late_kernel(keep, a1, a2, a3, kept, send, work):
    work[...] = keep[...] + a1[...].astype(F32) + a2[...].astype(F32) + a3[...].astype(F32)
    y_label, _, _ = labels()
    y = y_label >> 1
    kept[...] = work[y]
    send[...] = work[y ^ 1].astype(BF)


def ring_kernel(keep, arrived, kept, send, work):
    total = keep[...] + arrived[...].astype(F32)
    work[...] = total.reshape(2, 8, 2 * D)
    x = lax.axis_index("xh")
    for ref, at in ((kept, x), (send, x ^ 1)):
        r = work[at]
        ref[...] = jnp.concatenate([r[:, :D], r[:, D:]], 0).astype(BF)


def last_kernel(keep, a1, a2, a3, qkv, out):
    wide = [r[...].astype(F32) for r in (keep, a1, a2, a3)]
    total = (wide[0] + wide[1]) + (wide[2] + wide[3])
    qkv[...] = jnp.concatenate([total[:8], total[8:, :HD]], 1)
    out[...] = total[8:, HD:]


def gather_kernel(out_own, tok_own, o_main, t_main, o_lat, t_lat, out, tok, lat, sems):
    copies = []
    for i, (ref, main, edge) in enumerate(((out, o_main, o_lat), (tok, t_main, t_lat))):
        copies += [
            pltpu.make_async_copy(main.at[0:21], ref.at[3:24, 0:6], sems.at[i, 0]),
            pltpu.make_async_copy(main.at[21:24], lat.at[i, :, 0:6], sems.at[i, 1]),
            pltpu.make_async_copy(edge, lat.at[i, :, 6:12], sems.at[i, 2]),
        ]
    for c in copies:
        c.start()
    for c in copies:
        c.wait()


def finish_kernel(out_part, tok_part, lat, out, tok, sems):
    copies = [
        pltpu.make_async_copy(lat.at[i], ref.at[0:3], sems.at[i])
        for i, ref in enumerate((out, tok))
    ]
    for c in copies:
        c.start()
    for c in copies:
        c.wait()


VM = pl.BlockSpec(memory_space=pltpu.VMEM)
SM = pl.BlockSpec(memory_space=pltpu.SMEM)
ANY = pl.BlockSpec(memory_space=pl.ANY)


def shaped(dims, kind=BF):
    return jax.ShapeDtypeStruct(dims, kind)


def call(body, ins, outs, scratch=(), limit=16, flops=0, name=None, aliases=None, out_spec=VM, moved=8):
    return pl.pallas_call(
        body,
        in_specs=ins,
        out_specs=out_spec if isinstance(out_spec, list) else [out_spec] * len(outs),
        out_shape=outs,
        scratch_shapes=list(scratch),
        input_output_aliases=aliases or {},
        compiler_params=pltpu.CompilerParams(vmem_limit_bytes=limit * 2**20),
        cost_estimate=pl.CostEstimate(flops=0, bytes_accessed=moved * 2**20, transcendentals=0),
        name=name,
    )


def shift(block, axis, step):
    count = lax.axis_size(axis)
    return lax.ppermute(block, axis, [(i, (i + step) % count) for i in range(count)])


def shift_both(block, step):
    count = lax.axis_size(LON)
    route = [
        (i * 2 + b, ((i + step) % count) * 2 + 1 - b) for i in range(count) for b in range(2)
    ]
    return lax.ppermute(block, ALL, route)


def flipped(at, y_bits, z_bits, xh):
    z, y, x, core, lat = at
    y_label = gray((y + core) % 4) ^ y_bits
    y2, z2 = gray(y_label), ((z + core) % 8) ^ z_bits
    return ((z2 - core) % 8, (y2 - core) % 4, x ^ xh, core, lat)


def shift_both_x(block):
    return lax.ppermute(block, ("xh", "lat"), [(i, 3 - i) for i in range(4)])


def exchange(block, y_bits, z_bits, xh=0):
    route = []
    for i, at in enumerate(np.ndindex(*SIZES)):
        route.append((i, int(np.ravel_multi_index(flipped(at, y_bits, z_bits, xh), SIZES))))
    return lax.ppermute(block, ALL, route)


def per_device(tokens, land_mask, land_bias, qkv_weight, out_weight, cotangent):
    land = land_mask.T
    full, part, edge = (24, 12, 2, D), (21, 6, 2, D), (3, 6, 2, D)
    dma = pltpu.SemaphoreType.DMA

    main, lat, diag = call(
        tok_halo_kernel,
        [VM, ANY],
        [shaped((22, 6, 2, D)), shaped((4, 6, 2, D)), shaped((4, 6, 2, D))],
        scratch=[
            pltpu.VMEM((22, 6, 2, D), BF),
            pltpu.VMEM((4, 6, 2, D), BF),
            pltpu.VMEM((4, 6, 2, D), BF),
            dma((2, 5)),
        ],
        out_spec=ANY,
        limit=60,
        name="tok_halo",
    )(land, tokens)
    main, qkv_weight, out_weight = lax.optimization_barrier((main, qkv_weight, out_weight))
    main, lat, diag = shift(main, LON, -1), shift(lat, "lat", -1), shift_both(diag, -1)
    wqkv, wout = call(
        weights_kernel,
        [ANY] * 2,
        [shaped((D, 3 * HD)), shaped((HD, D))],
        scratch=[dma((5,))],
        limit=16,
        name="weights",
    )(qkv_weight, out_weight)
    lat, diag, cotangent, wqkv = lax.optimization_barrier((lat, diag, cotangent, wqkv))
    cot_main, cot_lat, cot_diag = call(
        cot_halo_kernel,
        [ANY],
        [shaped(part), shaped(edge), shaped(edge)],
        scratch=[dma((5,))],
        out_spec=ANY,
        limit=16,
        name="cot_halo",
    )(cotangent)
    cot_main = shift(cot_main, LON, -1)
    cot_lat, cot_diag = shift(cot_lat, "lat", -1), shift_both(cot_diag, -1)

    nrm, inverse, qkv, attn, att = call(
        forward_kernel,
        [SM] + [VM] * 6,
        [
            shaped((TOK, D)),
            shaped((TOK, 128), F32),
            shaped((TOK, 3 * HD)),
            shaped((WINS, HEADS // 2, 2, WIN, WIN), F32),
            shaped((TOK, HD)),
        ],
        limit=16,
        flops=4 * 10**9,
        name="forward",
    )(land_bias, tokens, main, lat, diag, land, wqkv)

    chunks = (32, 16, 2 * D)
    keep, send, dqkv = call(
        backward_kernel,
        [VM] * 9,
        [shaped(chunks, F32), shaped(chunks), shaped((TOK, 3 * HD))],
        scratch=[pltpu.VMEM((TOK, D), BF), pltpu.VMEM((TOK, HD), BF)],
        limit=18,
        flops=4 * 10**9,
        name="backward",
    )(cotangent, cot_main, cot_lat, cot_diag, nrm, qkv, attn, att, wout)

    def summed(body, operands, rows, sent, sends, name, scratch=(), kind=F32, moved=8):
        kept, *rest = call(
            body,
            [VM] * len(operands),
            [shaped(rows, kind)] + [shaped(sent)] * sends,
            scratch=scratch,
            limit=16,
            name=name,
            moved=moved,
        )(*operands)
        return kept, rest

    arrived = shift(send, "core", 1)
    whole = (24, 6, 2, D)
    send, att = lax.optimization_barrier((send, att))
    out_own, out_main, out_lat = call(
        out_kernel,
        [VM] * 2,
        [shaped(full), shaped(whole), shaped(edge)],
        limit=16,
        flops=10**9,
        name="out",
    )(att, wout)
    out_lat, keep = lax.optimization_barrier((out_lat, keep))
    out_main = shift(out_main, LON, 1)
    eighth, small = (8, 16, 2 * D), (2, 16, 2 * D)
    kept, sends = summed(core_kernel, (keep, arrived), eighth, eighth, 3, "sum_core")
    a = [exchange(s, dy, dz) for (dy, dz), s in zip(PEERS, sends)]
    dqkv, kept = lax.optimization_barrier((dqkv, kept))
    tok_own, tok_main, tok_lat = call(
        token_kernel,
        [VM] * 4,
        [shaped(full), shaped(whole), shaped(edge)],
        limit=16,
        flops=2 * 10**9,
        name="token_grad",
    )(dqkv, wqkv, nrm, inverse)
    out_main, kept = lax.optimization_barrier((out_main, kept))
    kept, sends = summed(middle_kernel, [kept] + a, small, small, 3, "sum_low")
    tok_main, kept = lax.optimization_barrier((tok_main, kept))
    tok_main = shift(tok_main, LON, 1)
    a = [exchange(s, 0, 2 * n + 2) for n, s in enumerate(sends)]
    kept, (s,) = summed(
        late_kernel, [kept] + a, small[1:], small[1:], 1, "sum_next", [pltpu.VMEM(small, F32)]
    )
    kept, (s,) = summed(
        ring_kernel,
        (kept, exchange(s, 2, 0)),
        (16, D),
        (16, D),
        1,
        "sum_y",
        [pltpu.VMEM((2, 8, 2 * D), F32)],
        BF,
        64,
    )
    out_own, kept = lax.optimization_barrier((out_own, kept))
    block_out, grad_tokens, lat = call(
        gather_kernel,
        [ANY] * 6,
        [shaped(full), shaped(full), shaped((2, 3, 12, 2, D))],
        scratch=[dma((2, 3))],
        aliases={0: 0, 1: 1},
        out_spec=ANY,
        name="gather",
    )(out_own, tok_own, out_main, tok_main, out_lat, tok_lat)
    a = [shift(kept, "lat", 1), shift(s, "xh", 1), shift_both_x(s)]
    grad_qkv, grad_out = call(
        last_kernel,
        [VM] * 4,
        [shaped((8, 3 * HD), F32), shaped((8, HD), F32)],
        name="sum_x",
    )(kept, *a)
    block_out, grad_tokens = call(
        finish_kernel,
        [ANY] * 3,
        [shaped(full), shaped(full)],
        scratch=[dma((2,))],
        aliases={0: 0, 1: 1},
        out_spec=ANY,
        name="assemble",
    )(block_out, grad_tokens, shift(lat, "lat", 1))
    return (block_out, grad_tokens, grad_qkv, grad_out.T)


def solution(mesh):
    fine = Mesh(mesh.devices.reshape(SIZES), ALL)
    grid = P("lat", LON, None, None)
    in_specs = (grid, P("lat", LON), P(), P(), P(), grid)
    out_specs = (grid, grid, P(LON, None), P(None, LON))
    return jax.shard_map(
        per_device, mesh=fine, in_specs=in_specs, out_specs=out_specs, check_vma=False
    )
```

```python
import math

import jax
import jax.numpy as jnp
import numpy as np
from jax import lax
from jax.experimental import pallas as pl
from jax.experimental.pallas import tpu as pltpu
from jax.sharding import Mesh, PartitionSpec as P

D = 1024
HEADS = 8
HSIZE = 64
HD = 512
WIN = 144
HALF = 72
WINS = 4
TOK = 576
SLAB = 128
TOKENS = 147456
GRAD_SCALE = 1.0 / math.sqrt(TOKENS)
FACTOR = HSIZE ** (-0.5)
FAR = -1e30
BF = jnp.bfloat16
F32 = jnp.float32
LON = ("z", "y", "xh", "core")
ALL = LON + ("lat",)
SIZES = (8, 4, 2, 2, 2)
PEERS = ((0, 1), (1, 0), (1, 1))


def nn(a, b):
    return lax.dot_general(a, b, (((1,), (0,)), ((), ())), preferred_element_type=F32)


def nt(a, b):
    return lax.dot_general(a, b, (((1,), (1,)), ((), ())), preferred_element_type=F32)


def tn(a, b):
    return lax.dot_general(a, b, (((0,), (0,)), ((), ())), preferred_element_type=F32)


def window_rows(own, main, lat, diag, w):
    if w < WINS - 1:
        parts = [own[3 + 6 * w : 9 + 6 * w, 6:12], main[6 * w : 6 * w + 6]]
    else:
        parts = [own[21:24, 6:12], lat[0:3], main[18:21], diag[0:3]]
    return jnp.concatenate([p.astype(F32).reshape(-1, D) for p in parts], 0)


def halo_copies(block, main, lat, diag, sems):
    return [
        pltpu.make_async_copy(block.at[3:10, 0:6], main.at[0:7], sems.at[0]),
        pltpu.make_async_copy(block.at[10:17, 0:6], main.at[7:14], sems.at[1]),
        pltpu.make_async_copy(block.at[17:24, 0:6], main.at[14:21], sems.at[2]),
        pltpu.make_async_copy(block.at[0:3, 6:12], lat.at[0:3], sems.at[3]),
        pltpu.make_async_copy(block.at[0:3, 0:6], diag.at[0:3], sems.at[4]),
    ]


def tok_halo_kernel(land, tok, main, lat, diag, main_v, lat_v, diag_v, sems):
    copies = halo_copies(tok, main_v, lat_v, diag_v, sems.at[0])
    for c in copies:
        c.start()
    by_row = jnp.concatenate([land[...].astype(F32), jnp.zeros((12, D - 24), F32)], 1)
    cells = jnp.broadcast_to(by_row[:, None, :], (12, 2, D)).astype(BF)
    main_v[21] = cells[0:6]
    lat_v[3] = cells[6:12]
    diag_v[3] = cells[0:6]
    done = []
    for i, (rows, wide, ref) in enumerate(
        (((0, 7), main_v, main), ((7, 14), main_v, main), ((14, 22), main_v, main),
         ((0, 4), lat_v, lat), ((0, 4), diag_v, diag))
    ):
        copies[i].wait()
        rows = slice(*rows)
        done.append(pltpu.make_async_copy(wide.at[rows], ref.at[rows], sems.at[1, i]))
        done[-1].start()
    for c in done:
        c.wait()


def cot_halo_kernel(cot, main, lat, diag, sems):
    copies = halo_copies(cot, main, lat, diag, sems)
    for c in copies:
        c.start()
    for c in copies:
        c.wait()


def weights_kernel(wqkv_hbm, wout_hbm, wqkv, wout, sems):
    copies = [pltpu.make_async_copy(wout_hbm, wout, sems.at[4])]
    for i in range(4):
        rows = slice(256 * i, 256 * i + 256)
        copies.append(pltpu.make_async_copy(wqkv_hbm.at[rows], wqkv.at[rows], sems.at[i]))
    for c in copies:
        c.start()
    for c in copies:
        c.wait()


def land_column(cells, first_row, rows):
    count = rows * 12
    token = lax.broadcasted_iota(jnp.int32, (count, 128), 0)
    lane = lax.broadcasted_iota(jnp.int32, (count, 128), 1)
    cell = lax.broadcasted_iota(jnp.int32, (count, 12), 0) % 12
    pick = (cell == lax.broadcasted_iota(jnp.int32, (count, 12), 1)).astype(F32)
    wide = nn(pick, cells)
    return jnp.sum(jnp.where(lane == token // 12 + first_row, wide, 0.0), 1, keepdims=True)


def forward_kernel(
    bias, tok, main, lat, diag, land, wqkv,
    nrm, inv_s, qkv, attn_s, att, att_left,
):
    for w in range(WINS):
        x = window_rows(tok, main, lat, diag, w)
        centred = x - jnp.mean(x, -1, keepdims=True)
        inverse = lax.rsqrt(jnp.mean(centred * centred, -1, keepdims=True) + 1e-05)
        rows = slice(WIN * w, WIN * w + WIN)
        inv_s[rows] = jnp.broadcast_to(inverse, (WIN, 128))
        nrm[rows] = (centred * inverse).astype(BF)
    for i in range(3):
        cols = slice(HD * i, HD * i + HD)
        r = nn(nrm[...], wqkv[:, cols])
        qkv[:, cols] = (r.astype(BF) * FACTOR).astype(BF) if i == 0 else r.astype(BF)

    by_row = jnp.concatenate([land[...].astype(F32), jnp.zeros((12, 104), F32)], 1)
    own_cells = jnp.broadcast_to(by_row[6:12][:, None, :], (6, 2, 128)).reshape(12, 128)
    main_cells, lat_cells, diag_cells = (
        r[r.shape[0] - 1, :, :, 0:128].astype(F32).reshape(12, 128) for r in (main, lat, diag)
    )
    first = lax.broadcasted_iota(jnp.int32, (WIN, SLAB), 1) < HSIZE
    zero = jnp.zeros((WIN, SLAB), BF)
    for w in range(WINS):
        rows = slice(WIN * w, WIN * w + WIN)
        if w < WINS - 1:
            parts = [land_column(own_cells, 3 + 6 * w, 6), land_column(main_cells, 3 + 6 * w, 6)]
            mask = None
        else:
            parts = [
                land_column(c, at, 3)
                for c, at in ((own_cells, 21), (lat_cells, 0), (main_cells, 21), (diag_cells, 0))
            ]
            k_at = lax.broadcasted_iota(jnp.int32, (WIN, WIN), 0) % HALF
            q_at = lax.broadcasted_iota(jnp.int32, (WIN, WIN), 1) % HALF
            apart = (k_at >= HALF // 2) != (q_at >= HALF // 2)
            mask = jnp.where(jnp.logical_and(apart, lax.axis_index("lat") == 1), FAR, 0.0)
        land_key = jnp.broadcast_to(jnp.concatenate(parts, 0), (WIN, WIN))
        for s in range(HEADS // 2):
            q = qkv[rows, SLAB * s : SLAB * s + SLAB]
            k = qkv[rows, HD + SLAB * s : HD + SLAB * s + SLAB]
            v = qkv[rows, 2 * HD + SLAB * s : 2 * HD + SLAB * s + SLAB]
            both = jnp.concatenate([jnp.where(first, k, zero), jnp.where(first, zero, k)], 0)
            sc = nt(both, q).reshape(2, WIN, WIN)
            sc = jnp.stack([sc[e] + land_key * bias[2 * s + e] for e in range(2)])
            if mask is not None:
                sc = sc + mask[None]
            ex = jnp.exp(sc - jnp.max(sc, 1, keepdims=True))
            attn = ex * (1.0 / jnp.sum(ex, 1, keepdims=True))
            attn_s[w, s] = attn
            attn_b = attn.astype(BF)
            o = jnp.where(first, tn(attn_b[0], v), tn(attn_b[1], v))
            att[rows, SLAB * s : SLAB * s + SLAB] = o.astype(BF)
            att_left[w, :, SLAB * s : SLAB * s + SLAB] = o[HALF:].astype(BF)


def backward_kernel(
    cot, main, lat, diag, nrm, qkv, attn_s, att, wout,
    keep, send, dqkv, cotb, datt,
):
    core = lax.axis_index("core")
    for w in range(WINS):
        cotb[WIN * w : WIN * w + WIN] = window_rows(cot, main, lat, diag, w).astype(BF)
    datt[...] = nt(cotb[...], wout[...]).astype(BF)

    first = lax.broadcasted_iota(jnp.int32, (WIN, SLAB), 1) < HSIZE
    zero = jnp.zeros((WIN, SLAB), BF)
    for w in range(WINS):
        rows = slice(WIN * w, WIN * w + WIN)
        for s in range(HEADS // 2):
            q_cols, k_cols, v_cols = (
                slice(HD * i + SLAB * s, HD * i + SLAB * s + SLAB) for i in range(3)
            )
            q, k, v = qkv[rows, q_cols], qkv[rows, k_cols], qkv[rows, v_cols]
            do = datt[rows, q_cols]
            attn = attn_s[w, s]
            both = jnp.concatenate([jnp.where(first, v, zero), jnp.where(first, zero, v)], 0)
            d_attn = nt(both, do).reshape(2, WIN, WIN)
            delta = jnp.sum(attn * d_attn, 1, keepdims=True)
            d_sc = (attn * (d_attn - delta)).astype(BF)
            d_v = nn(attn.astype(BF).reshape(2 * WIN, WIN), do)
            d_k = nn(d_sc.reshape(2 * WIN, WIN), q)
            d_q = jnp.where(first, tn(d_sc[0], k), tn(d_sc[1], k))
            dqkv[rows, q_cols] = (d_q * FACTOR).astype(BF)
            dqkv[rows, k_cols] = jnp.where(first, d_k[:WIN], d_k[WIN:]).astype(BF)
            dqkv[rows, v_cols] = jnp.where(first, d_v[:WIN], d_v[WIN:]).astype(BF)

    def put(r, i, lo):
        wide = r.shape[1]
        r = (r * GRAD_SCALE).reshape(2, 4, 2, 2, 8, wide)
        cols = slice(lo, lo + wide)
        for z in range(2):
            for y in range(4):
                even = r[z, y, :, 0].reshape(16, wide)
                odd = r[z, y, :, 1].reshape(16, wide)
                at = y * 8 + 2 * i + z
                keep[at, :, cols] = jnp.where(core == 0, even, odd)
                send[at, :, cols] = jnp.where(core == 0, odd, even).astype(BF)

    for i in range(4):
        feats = slice(256 * i, 256 * i + 256)
        put(tn(nrm[:, feats], dqkv[...]), i, 0)
        put(tn(cotb[:, feats], att[...]), i, 3 * HD)


def store_rows(r, own, main, lat, w):
    r = r.astype(BF)
    if w < WINS - 1:
        own[3 + 6 * w : 9 + 6 * w, 6:12] = r[:HALF].reshape(6, 6, 2, D)
        main[6 * w : 6 * w + 6] = r[HALF:].reshape(6, 6, 2, D)
    else:
        own[21:24, 6:12] = r[:36].reshape(3, 6, 2, D)
        lat[...] = r[36:72].reshape(3, 6, 2, D)
        main[18:21] = r[72:108].reshape(3, 6, 2, D)
        main[21:24] = r[108:].reshape(3, 6, 2, D)


def out_kernel(att, wout, own, lat):
    for w in range(WINS):
        r = nn(att[WIN * w : WIN * w + 80], wout[...]).astype(BF)
        if w < WINS - 1:
            own[3 + 6 * w : 9 + 6 * w, 6:12] = r[:HALF].reshape(6, 6, 2, D)
        else:
            own[21:24, 6:12] = r[:36].reshape(3, 6, 2, D)
            lat[...] = r[36:72].reshape(3, 6, 2, D)


def home_kernel(att_left, wout, main):
    for w in range(WINS):
        main[6 * w : 6 * w + 6] = nn(att_left[w], wout[...]).astype(BF).reshape(6, 6, 2, D)


def token_kernel(dqkv, wqkv, nrm, inv_s, own, main, lat):
    for w in range(WINS):
        rows = slice(WIN * w, WIN * w + WIN)
        d_normed = nt(dqkv[rows], wqkv[...])
        unit = nrm[rows].astype(F32)
        d_flat = inv_s[rows, 0:1] * (
            d_normed
            - jnp.mean(d_normed, -1, keepdims=True)
            - unit * jnp.mean(d_normed * unit, -1, keepdims=True)
        )
        store_rows(d_flat, own, main, lat, w)


def gray(label):
    return label ^ (label >> 1)


def labels():
    core = lax.axis_index("core")
    return gray((lax.axis_index("y") + core) & 3), (lax.axis_index("z") + core) & 7, core


def core_kernel(keep, arrived, kept, s1, s2, s3):
    y_label, z_label, core = labels()
    for (dy, dz), ref in zip(((0, 0),) + PEERS, (kept, s1, s2, s3)):
        y0, z0 = (y_label & 1) ^ dy, (z_label & 1) ^ dz
        for n, (z2, z1, y1) in enumerate(np.ndindex(2, 2, 2)):
            y = (gray(2 * y1 + y0) - core + 4) & 3
            z = (4 * z2 + 2 * z1 + z0 - core + 8) & 7
            at = y * 8 + z
            ref[n] = (keep[at] + arrived[at].astype(F32)).astype(ref.dtype)


def middle_kernel(keep, a1, a2, a3, kept, s1, s2, s3):
    def total(i):
        at = pl.ds(2 * i, 2)
        return keep[at] + a1[at].astype(F32) + a2[at].astype(F32) + a3[at].astype(F32)

    _, z_label, _ = labels()
    mine = z_label >> 1
    kept[...] = total(mine)
    for n, ref in enumerate((s1, s2, s3)):
        ref[...] = total(mine ^ (n + 1)).astype(BF)


def late_kernel(keep, a1, a2, a3, kept, send, work):
    work[...] = keep[...] + a1[...].astype(F32) + a2[...].astype(F32) + a3[...].astype(F32)
    y_label, _, _ = labels()
    y = y_label >> 1
    kept[...] = work[y]
    send[...] = work[y ^ 1].astype(BF)


def ring_kernel(keep, arrived, kept, send, work):
    total = keep[...] + arrived[...].astype(F32)
    work[...] = total.reshape(2, 8, 2 * D)
    x = lax.axis_index("xh")
    for ref, at in ((kept, x), (send, x ^ 1)):
        r = work[at]
        ref[...] = jnp.concatenate([r[:, :D], r[:, D:]], 0).astype(BF)


def last_kernel(keep, a1, a2, a3, qkv, out):
    wide = [r[...].astype(F32) for r in (keep, a1, a2, a3)]
    total = (wide[0] + wide[1]) + (wide[2] + wide[3])
    qkv[...] = jnp.concatenate([total[:8], total[8:, :HD]], 1)
    out[...] = total[8:, HD:]


def gather_kernel(out_own, tok_own, o_main, t_main, o_lat, t_lat, out, tok, lat, sems):
    copies = []
    for i, (ref, main, edge) in enumerate(((out, o_main, o_lat), (tok, t_main, t_lat))):
        copies += [
            pltpu.make_async_copy(main.at[0:21], ref.at[3:24, 0:6], sems.at[i, 0]),
            pltpu.make_async_copy(main.at[21:24], lat.at[i, :, 0:6], sems.at[i, 1]),
            pltpu.make_async_copy(edge, lat.at[i, :, 6:12], sems.at[i, 2]),
        ]
    for c in copies:
        c.start()
    for c in copies:
        c.wait()


def finish_kernel(out_part, tok_part, lat, out, tok, sems):
    copies = [
        pltpu.make_async_copy(lat.at[i], ref.at[0:3], sems.at[i])
        for i, ref in enumerate((out, tok))
    ]
    for c in copies:
        c.start()
    for c in copies:
        c.wait()


VM = pl.BlockSpec(memory_space=pltpu.VMEM)
SM = pl.BlockSpec(memory_space=pltpu.SMEM)
ANY = pl.BlockSpec(memory_space=pl.ANY)


def shaped(dims, kind=BF):
    return jax.ShapeDtypeStruct(dims, kind)


def call(body, ins, outs, scratch=(), limit=16, flops=0, name=None, aliases=None, out_spec=VM, moved=8):
    return pl.pallas_call(
        body,
        in_specs=ins,
        out_specs=out_spec if isinstance(out_spec, list) else [out_spec] * len(outs),
        out_shape=outs,
        scratch_shapes=list(scratch),
        input_output_aliases=aliases or {},
        compiler_params=pltpu.CompilerParams(vmem_limit_bytes=limit * 2**20),
        cost_estimate=pl.CostEstimate(flops=0, bytes_accessed=moved * 2**20, transcendentals=0),
        name=name,
    )


def shift(block, axis, step):
    count = lax.axis_size(axis)
    return lax.ppermute(block, axis, [(i, (i + step) % count) for i in range(count)])


def shift_both(block, step):
    count = lax.axis_size(LON)
    route = [
        (i * 2 + b, ((i + step) % count) * 2 + 1 - b) for i in range(count) for b in range(2)
    ]
    return lax.ppermute(block, ALL, route)


def flipped(at, y_bits, z_bits, xh):
    z, y, x, core, lat = at
    y_label = gray((y + core) % 4) ^ y_bits
    y2, z2 = gray(y_label), ((z + core) % 8) ^ z_bits
    return ((z2 - core) % 8, (y2 - core) % 4, x ^ xh, core, lat)


def shift_both_x(block):
    return lax.ppermute(block, ("xh", "lat"), [(i, 3 - i) for i in range(4)])


def exchange(block, y_bits, z_bits, xh=0):
    route = []
    for i, at in enumerate(np.ndindex(*SIZES)):
        route.append((i, int(np.ravel_multi_index(flipped(at, y_bits, z_bits, xh), SIZES))))
    return lax.ppermute(block, ALL, route)


def per_device(tokens, land_mask, land_bias, qkv_weight, out_weight, cotangent):
    land = land_mask.T
    full, part, edge = (24, 12, 2, D), (21, 6, 2, D), (3, 6, 2, D)
    dma = pltpu.SemaphoreType.DMA

    main, lat, diag = call(
        tok_halo_kernel,
        [VM, ANY],
        [shaped((22, 6, 2, D)), shaped((4, 6, 2, D)), shaped((4, 6, 2, D))],
        scratch=[
            pltpu.VMEM((22, 6, 2, D), BF),
            pltpu.VMEM((4, 6, 2, D), BF),
            pltpu.VMEM((4, 6, 2, D), BF),
            dma((2, 5)),
        ],
        out_spec=ANY,
        limit=60,
        name="tok_halo",
    )(land, tokens)
    main, qkv_weight, out_weight = lax.optimization_barrier((main, qkv_weight, out_weight))
    main, lat, diag = shift(main, LON, -1), shift(lat, "lat", -1), shift_both(diag, -1)
    wqkv, wout = call(
        weights_kernel,
        [ANY] * 2,
        [shaped((D, 3 * HD)), shaped((HD, D))],
        scratch=[dma((5,))],
        limit=16,
        name="weights",
    )(qkv_weight, out_weight)
    lat, diag, cotangent, wqkv = lax.optimization_barrier((lat, diag, cotangent, wqkv))
    cot_main, cot_lat, cot_diag = call(
        cot_halo_kernel,
        [ANY],
        [shaped(part), shaped(edge), shaped(edge)],
        scratch=[dma((5,))],
        out_spec=ANY,
        limit=16,
        name="cot_halo",
    )(cotangent)
    cot_main = shift(cot_main, LON, -1)
    cot_lat, cot_diag = shift(cot_lat, "lat", -1), shift_both(cot_diag, -1)

    nrm, inverse, qkv, attn, att, att_left = call(
        forward_kernel,
        [SM] + [VM] * 6,
        [
            shaped((TOK, D)),
            shaped((TOK, 128), F32),
            shaped((TOK, 3 * HD)),
            shaped((WINS, HEADS // 2, 2, WIN, WIN), F32),
            shaped((TOK, HD)),
            shaped((WINS, HALF, HD)),
        ],
        limit=16,
        flops=4 * 10**9,
        name="forward",
    )(land_bias, tokens, main, lat, diag, land, wqkv)

    chunks = (32, 16, 2 * D)
    keep, send, dqkv = call(
        backward_kernel,
        [VM] * 9,
        [shaped(chunks, F32), shaped(chunks), shaped((TOK, 3 * HD))],
        scratch=[pltpu.VMEM((TOK, D), BF), pltpu.VMEM((TOK, HD), BF)],
        limit=18,
        flops=4 * 10**9,
        name="backward",
    )(cotangent, cot_main, cot_lat, cot_diag, nrm, qkv, attn, att, wout)

    def summed(body, operands, rows, sent, sends, name, scratch=(), kind=F32, moved=8):
        kept, *rest = call(
            body,
            [VM] * len(operands),
            [shaped(rows, kind)] + [shaped(sent)] * sends,
            scratch=scratch,
            limit=16,
            name=name,
            moved=moved,
        )(*operands)
        return kept, rest

    arrived = shift(send, "core", 1)
    whole = (24, 6, 2, D)
    send, att = lax.optimization_barrier((send, att))
    att_left = shift(att_left, LON, 1)
    out_own, out_lat = call(
        out_kernel,
        [VM] * 2,
        [shaped(full), shaped(edge)],
        limit=16,
        flops=10**9,
        name="out",
    )(att, wout)
    out_lat, keep = lax.optimization_barrier((out_lat, keep))
    eighth, small = (8, 16, 2 * D), (2, 16, 2 * D)
    kept, sends = summed(core_kernel, (keep, arrived), eighth, eighth, 3, "sum_core")
    a = [exchange(s, dy, dz) for (dy, dz), s in zip(PEERS, sends)]
    dqkv, kept, att_left = lax.optimization_barrier((dqkv, kept, att_left))
    tok_own, tok_main, tok_lat = call(
        token_kernel,
        [VM] * 4,
        [shaped(full), shaped(whole), shaped(edge)],
        limit=16,
        flops=2 * 10**9,
        name="token_grad",
    )(dqkv, wqkv, nrm, inverse)
    tok_main = shift(tok_main, LON, 1)
    (out_main,) = call(
        home_kernel, [VM] * 2, [shaped(whole)], limit=16, flops=10**9, name="out_left"
    )(att_left, wout)
    out_main, kept = lax.optimization_barrier((out_main, kept))
    kept, sends = summed(middle_kernel, [kept] + a, small, small, 3, "sum_low")
    a = [exchange(s, 0, 2 * n + 2) for n, s in enumerate(sends)]
    kept, (s,) = summed(
        late_kernel, [kept] + a, small[1:], small[1:], 1, "sum_next", [pltpu.VMEM(small, F32)]
    )
    out_own, kept = lax.optimization_barrier((out_own, kept))
    block_out, grad_tokens, lat = call(
        gather_kernel,
        [ANY] * 6,
        [shaped(full), shaped(full), shaped((2, 3, 12, 2, D))],
        scratch=[dma((2, 3))],
        aliases={0: 0, 1: 1},
        out_spec=ANY,
        name="gather",
    )(out_own, tok_own, out_main, tok_main, out_lat, tok_lat)
    kept, (s,) = summed(
        ring_kernel,
        (kept, exchange(s, 2, 0)),
        (16, D),
        (16, D),
        1,
        "sum_y",
        [pltpu.VMEM((2, 8, 2 * D), F32)],
        BF,
        64,
    )
    a = [shift(kept, "lat", 1), shift(s, "xh", 1), shift_both_x(s)]
    grad_qkv, grad_out = call(
        last_kernel,
        [VM] * 4,
        [shaped((8, 3 * HD), F32), shaped((8, HD), F32)],
        name="sum_x",
    )(kept, *a)
    block_out, grad_tokens = call(
        finish_kernel,
        [ANY] * 3,
        [shaped(full), shaped(full)],
        scratch=[dma((2,))],
        aliases={0: 0, 1: 1},
        out_spec=ANY,
        name="assemble",
    )(block_out, grad_tokens, shift(lat, "lat", 1))
    return (block_out, grad_tokens, grad_qkv, grad_out.T)


def solution(mesh):
    fine = Mesh(mesh.devices.reshape(SIZES), ALL)
    grid = P("lat", LON, None, None)
    in_specs = (grid, P("lat", LON), P(), P(), P(), grid)
    out_specs = (grid, grid, P(LON, None), P(None, LON))
    return jax.shard_map(
        per_device, mesh=fine, in_specs=in_specs, out_specs=out_specs, check_vma=False
    )
```

```python
import math

import jax
import jax.numpy as jnp
import numpy as np
from jax import lax
from jax.experimental import pallas as pl
from jax.experimental.pallas import tpu as pltpu
from jax.sharding import Mesh, PartitionSpec as P

D = 1024
HEADS = 8
HSIZE = 64
HD = 512
WIN = 144
HALF = 72
WINS = 4
TOK = 576
SLAB = 128
TOKENS = 147456
GRAD_SCALE = 1.0 / math.sqrt(TOKENS)
FACTOR = HSIZE ** (-0.5)
FAR = -1e30
BF = jnp.bfloat16
F32 = jnp.float32
LON = ("z", "y", "xh", "core")
ALL = LON + ("lat",)
SIZES = (8, 4, 2, 2, 2)
PEERS = ((0, 1), (1, 0), (1, 1))


def nn(a, b):
    return lax.dot_general(a, b, (((1,), (0,)), ((), ())), preferred_element_type=F32)


def nt(a, b):
    return lax.dot_general(a, b, (((1,), (1,)), ((), ())), preferred_element_type=F32)


def tn(a, b):
    return lax.dot_general(a, b, (((0,), (0,)), ((), ())), preferred_element_type=F32)


def window_rows(own, main, lat, diag, w):
    if w < WINS - 1:
        parts = [own[3 + 6 * w : 9 + 6 * w, 6:12], main[6 * w : 6 * w + 6]]
    else:
        parts = [own[21:24, 6:12], lat[0:3], main[18:21], diag[0:3]]
    return jnp.concatenate([p.astype(F32).reshape(-1, D) for p in parts], 0)


def halo_copies(block, main, lat, diag, sems):
    return [
        pltpu.make_async_copy(block.at[3:10, 0:6], main.at[0:7], sems.at[0]),
        pltpu.make_async_copy(block.at[10:17, 0:6], main.at[7:14], sems.at[1]),
        pltpu.make_async_copy(block.at[17:24, 0:6], main.at[14:21], sems.at[2]),
        pltpu.make_async_copy(block.at[0:3, 6:12], lat.at[0:3], sems.at[3]),
        pltpu.make_async_copy(block.at[0:3, 0:6], diag.at[0:3], sems.at[4]),
    ]


def tok_halo_kernel(land, tok, main, lat, diag, main_v, lat_v, diag_v, sems):
    copies = halo_copies(tok, main_v, lat_v, diag_v, sems.at[0])
    for c in copies:
        c.start()
    by_row = jnp.concatenate([land[...].astype(F32), jnp.zeros((12, D - 24), F32)], 1)
    cells = jnp.broadcast_to(by_row[:, None, :], (12, 2, D)).astype(BF)
    main_v[21] = cells[0:6]
    lat_v[3] = cells[6:12]
    diag_v[3] = cells[0:6]
    done = []
    for i, (rows, wide, ref) in enumerate(
        (((0, 7), main_v, main), ((7, 14), main_v, main), ((14, 22), main_v, main),
         ((0, 4), lat_v, lat), ((0, 4), diag_v, diag))
    ):
        copies[i].wait()
        rows = slice(*rows)
        done.append(pltpu.make_async_copy(wide.at[rows], ref.at[rows], sems.at[1, i]))
        done[-1].start()
    for c in done:
        c.wait()


def cot_halo_kernel(cot, main, lat, diag, sems):
    copies = halo_copies(cot, main, lat, diag, sems)
    for c in copies:
        c.start()
    for c in copies:
        c.wait()


def weights_kernel(wqkv_hbm, wout_hbm, wqkv, wout, sems):
    copies = [pltpu.make_async_copy(wout_hbm, wout, sems.at[4])]
    for i in range(4):
        rows = slice(256 * i, 256 * i + 256)
        copies.append(pltpu.make_async_copy(wqkv_hbm.at[rows], wqkv.at[rows], sems.at[i]))
    for c in copies:
        c.start()
    for c in copies:
        c.wait()


def land_column(cells, first_row, rows):
    count = rows * 12
    token = lax.broadcasted_iota(jnp.int32, (count, 128), 0)
    lane = lax.broadcasted_iota(jnp.int32, (count, 128), 1)
    cell = lax.broadcasted_iota(jnp.int32, (count, 12), 0) % 12
    pick = (cell == lax.broadcasted_iota(jnp.int32, (count, 12), 1)).astype(F32)
    wide = nn(pick, cells)
    return jnp.sum(jnp.where(lane == token // 12 + first_row, wide, 0.0), 1, keepdims=True)


def forward_kernel(
    bias, tok, main, lat, diag, land, wqkv,
    nrm, inv_s, qkv, attn_s, att, att_left,
):
    for w in range(WINS):
        x = window_rows(tok, main, lat, diag, w)
        centred = x - jnp.mean(x, -1, keepdims=True)
        inverse = lax.rsqrt(jnp.mean(centred * centred, -1, keepdims=True) + 1e-05)
        rows = slice(WIN * w, WIN * w + WIN)
        inv_s[rows] = jnp.broadcast_to(inverse, (WIN, 128))
        nrm[rows] = (centred * inverse).astype(BF)
    for i in range(3):
        cols = slice(HD * i, HD * i + HD)
        r = nn(nrm[...], wqkv[:, cols])
        qkv[:, cols] = (r.astype(BF) * FACTOR).astype(BF) if i == 0 else r.astype(BF)

    by_row = jnp.concatenate([land[...].astype(F32), jnp.zeros((12, 104), F32)], 1)
    own_cells = jnp.broadcast_to(by_row[6:12][:, None, :], (6, 2, 128)).reshape(12, 128)
    main_cells, lat_cells, diag_cells = (
        r[r.shape[0] - 1, :, :, 0:128].astype(F32).reshape(12, 128) for r in (main, lat, diag)
    )
    first = lax.broadcasted_iota(jnp.int32, (WIN, SLAB), 1) < HSIZE
    zero = jnp.zeros((WIN, SLAB), BF)
    for w in range(WINS):
        rows = slice(WIN * w, WIN * w + WIN)
        if w < WINS - 1:
            parts = [land_column(own_cells, 3 + 6 * w, 6), land_column(main_cells, 3 + 6 * w, 6)]
            mask = None
        else:
            parts = [
                land_column(c, at, 3)
                for c, at in ((own_cells, 21), (lat_cells, 0), (main_cells, 21), (diag_cells, 0))
            ]
            k_at = lax.broadcasted_iota(jnp.int32, (WIN, WIN), 0) % HALF
            q_at = lax.broadcasted_iota(jnp.int32, (WIN, WIN), 1) % HALF
            apart = (k_at >= HALF // 2) != (q_at >= HALF // 2)
            mask = jnp.where(jnp.logical_and(apart, lax.axis_index("lat") == 1), FAR, 0.0)
        land_key = jnp.broadcast_to(jnp.concatenate(parts, 0), (WIN, WIN))
        for s in range(HEADS // 2):
            q = qkv[rows, SLAB * s : SLAB * s + SLAB]
            k = qkv[rows, HD + SLAB * s : HD + SLAB * s + SLAB]
            v = qkv[rows, 2 * HD + SLAB * s : 2 * HD + SLAB * s + SLAB]
            both = jnp.concatenate([jnp.where(first, k, zero), jnp.where(first, zero, k)], 0)
            sc = nt(both, q).reshape(2, WIN, WIN)
            sc = jnp.stack([sc[e] + land_key * bias[2 * s + e] for e in range(2)])
            if mask is not None:
                sc = sc + mask[None]
            ex = jnp.exp(sc - jnp.max(sc, 1, keepdims=True))
            attn = ex * (1.0 / jnp.sum(ex, 1, keepdims=True))
            attn_s[w, s] = attn
            attn_b = attn.astype(BF)
            o = jnp.where(first, tn(attn_b[0], v), tn(attn_b[1], v))
            att[rows, SLAB * s : SLAB * s + SLAB] = o.astype(BF)
            att_left[w, :, SLAB * s : SLAB * s + SLAB] = o[HALF:].astype(BF)


def backward_kernel(
    cot, main, lat, diag, nrm, qkv, attn_s, att, wout,
    keep, send, dqkv, cotb, datt,
):
    core = lax.axis_index("core")
    for w in range(WINS):
        cotb[WIN * w : WIN * w + WIN] = window_rows(cot, main, lat, diag, w).astype(BF)
    datt[...] = nt(cotb[...], wout[...]).astype(BF)

    first = lax.broadcasted_iota(jnp.int32, (WIN, SLAB), 1) < HSIZE
    zero = jnp.zeros((WIN, SLAB), BF)
    for w in range(WINS):
        rows = slice(WIN * w, WIN * w + WIN)
        for s in range(HEADS // 2):
            q_cols, k_cols, v_cols = (
                slice(HD * i + SLAB * s, HD * i + SLAB * s + SLAB) for i in range(3)
            )
            q, k, v = qkv[rows, q_cols], qkv[rows, k_cols], qkv[rows, v_cols]
            do = datt[rows, q_cols]
            attn = attn_s[w, s]
            both = jnp.concatenate([jnp.where(first, v, zero), jnp.where(first, zero, v)], 0)
            d_attn = nt(both, do).reshape(2, WIN, WIN)
            delta = jnp.sum(attn * d_attn, 1, keepdims=True)
            d_sc = (attn * (d_attn - delta)).astype(BF)
            d_v = nn(attn.astype(BF).reshape(2 * WIN, WIN), do)
            d_k = nn(d_sc.reshape(2 * WIN, WIN), q)
            d_q = jnp.where(first, tn(d_sc[0], k), tn(d_sc[1], k))
            dqkv[rows, q_cols] = (d_q * FACTOR).astype(BF)
            dqkv[rows, k_cols] = jnp.where(first, d_k[:WIN], d_k[WIN:]).astype(BF)
            dqkv[rows, v_cols] = jnp.where(first, d_v[:WIN], d_v[WIN:]).astype(BF)

    def put(r, i, lo):
        wide = r.shape[1]
        r = (r * GRAD_SCALE).reshape(2, 4, 2, 2, 8, wide)
        cols = slice(lo, lo + wide)
        for z in range(2):
            for y in range(4):
                even = r[z, y, :, 0].reshape(16, wide)
                odd = r[z, y, :, 1].reshape(16, wide)
                at = y * 8 + 2 * i + z
                keep[at, :, cols] = jnp.where(core == 0, even, odd)
                send[at, :, cols] = jnp.where(core == 0, odd, even).astype(BF)

    for i in range(4):
        feats = slice(256 * i, 256 * i + 256)
        put(tn(nrm[:, feats], dqkv[...]), i, 0)
        put(tn(cotb[:, feats], att[...]), i, 3 * HD)


def store_rows(r, own, main, lat, w):
    r = r.astype(BF)
    if w < WINS - 1:
        own[3 + 6 * w : 9 + 6 * w, 6:12] = r[:HALF].reshape(6, 6, 2, D)
        main[6 * w : 6 * w + 6] = r[HALF:].reshape(6, 6, 2, D)
    else:
        own[21:24, 6:12] = r[:36].reshape(3, 6, 2, D)
        lat[...] = r[36:72].reshape(3, 6, 2, D)
        main[18:21] = r[72:108].reshape(3, 6, 2, D)
        main[21:24] = r[108:].reshape(3, 6, 2, D)


def out_kernel(att, wout, own, lat):
    for w in range(WINS):
        r = nn(att[WIN * w : WIN * w + 80], wout[...]).astype(BF)
        if w < WINS - 1:
            own[3 + 6 * w : 9 + 6 * w, 6:12] = r[:HALF].reshape(6, 6, 2, D)
        else:
            own[21:24, 6:12] = r[:36].reshape(3, 6, 2, D)
            lat[...] = r[36:72].reshape(3, 6, 2, D)


def home_kernel(att_left, wout, main):
    for w in range(WINS):
        main[6 * w : 6 * w + 6] = nn(att_left[w], wout[...]).astype(BF).reshape(6, 6, 2, D)


def token_kernel(dqkv, wqkv, nrm, inv_s, own, main, lat):
    for w in range(WINS):
        rows = slice(WIN * w, WIN * w + WIN)
        d_normed = nt(dqkv[rows], wqkv[...])
        unit = nrm[rows].astype(F32)
        d_flat = inv_s[rows, 0:1] * (
            d_normed
            - jnp.mean(d_normed, -1, keepdims=True)
            - unit * jnp.mean(d_normed * unit, -1, keepdims=True)
        )
        store_rows(d_flat, own, main, lat, w)


def gray(label):
    return label ^ (label >> 1)


def paired(z):
    return 2 * gray(z >> 1) + (z & 1)


def labels():
    core = lax.axis_index("core")
    y = gray((lax.axis_index("y") + core) & 3)
    return y, paired((lax.axis_index("z") + core) & 7), core


def core_kernel(keep, arrived, kept, s1, s2, s3):
    y_label, z_label, core = labels()
    for (dy, dz), ref in zip(((0, 0),) + PEERS, (kept, s1, s2, s3)):
        y0, z0 = (y_label & 1) ^ dy, (z_label & 1) ^ dz
        for n, (y1, z1, z2) in enumerate(np.ndindex(2, 2, 2)):
            y = (gray(2 * y1 + y0) - core + 4) & 3
            z = (paired(4 * z2 + 2 * z1 + z0) - core + 8) & 7
            at = y * 8 + z
            ref[n] = (keep[at] + arrived[at].astype(F32)).astype(ref.dtype)


def middle_kernel(keep, a1, a2, a3, kept, s1, s2, s3):
    def total(i):
        at = pl.ds(2 * i, 2)
        return keep[at] + a1[at].astype(F32) + a2[at].astype(F32) + a3[at].astype(F32)

    y_label, z_label, _ = labels()
    mine = (y_label >> 1) * 2 + ((z_label >> 1) & 1)
    kept[...] = total(mine)
    for n, ref in enumerate((s1, s2, s3)):
        ref[...] = total(mine ^ (n + 1)).astype(BF)


def late_kernel(keep, a1, a2, a3, kept, send, work):
    work[...] = keep[...] + a1[...].astype(F32) + a2[...].astype(F32) + a3[...].astype(F32)
    _, z_label, _ = labels()
    z = z_label >> 2
    kept[...] = work[z]
    send[...] = work[z ^ 1].astype(BF)


def ring_kernel(keep, arrived, kept, send, work):
    total = keep[...] + arrived[...].astype(F32)
    work[...] = total.reshape(2, 8, 2 * D)
    x = lax.axis_index("xh")
    for ref, at in ((kept, x), (send, x ^ 1)):
        r = work[at]
        ref[...] = jnp.concatenate([r[:, :D], r[:, D:]], 0).astype(BF)


def last_kernel(keep, a1, a2, a3, qkv, out):
    wide = [r[...].astype(F32) for r in (keep, a1, a2, a3)]
    total = (wide[0] + wide[1]) + (wide[2] + wide[3])
    qkv[...] = jnp.concatenate([total[:8], total[8:, :HD]], 1)
    out[...] = total[8:, HD:]


def gather_kernel(out_own, tok_own, o_main, t_main, o_lat, t_lat, out, tok, lat, sems):
    copies = []
    for i, (ref, main, edge) in enumerate(((out, o_main, o_lat), (tok, t_main, t_lat))):
        copies += [
            pltpu.make_async_copy(main.at[0:21], ref.at[3:24, 0:6], sems.at[i, 0]),
            pltpu.make_async_copy(main.at[21:24], lat.at[i, :, 0:6], sems.at[i, 1]),
            pltpu.make_async_copy(edge, lat.at[i, :, 6:12], sems.at[i, 2]),
        ]
    for c in copies:
        c.start()
    for c in copies:
        c.wait()


def finish_kernel(out_part, tok_part, lat, out, tok, sems):
    copies = [
        pltpu.make_async_copy(lat.at[i], ref.at[0:3], sems.at[i])
        for i, ref in enumerate((out, tok))
    ]
    for c in copies:
        c.start()
    for c in copies:
        c.wait()


VM = pl.BlockSpec(memory_space=pltpu.VMEM)
SM = pl.BlockSpec(memory_space=pltpu.SMEM)
ANY = pl.BlockSpec(memory_space=pl.ANY)


def shaped(dims, kind=BF):
    return jax.ShapeDtypeStruct(dims, kind)


def call(body, ins, outs, scratch=(), limit=16, flops=0, name=None, aliases=None, out_spec=VM, moved=8):
    return pl.pallas_call(
        body,
        in_specs=ins,
        out_specs=out_spec if isinstance(out_spec, list) else [out_spec] * len(outs),
        out_shape=outs,
        scratch_shapes=list(scratch),
        input_output_aliases=aliases or {},
        compiler_params=pltpu.CompilerParams(vmem_limit_bytes=limit * 2**20),
        cost_estimate=pl.CostEstimate(flops=0, bytes_accessed=moved * 2**20, transcendentals=0),
        name=name,
    )


def shift(block, axis, step):
    count = lax.axis_size(axis)
    return lax.ppermute(block, axis, [(i, (i + step) % count) for i in range(count)])


def shift_both(block, step):
    count = lax.axis_size(LON)
    route = [
        (i * 2 + b, ((i + step) % count) * 2 + 1 - b) for i in range(count) for b in range(2)
    ]
    return lax.ppermute(block, ALL, route)


def flipped(at, y_bits, z_bits, xh):
    z, y, x, core, lat = at
    y_label = gray((y + core) % 4) ^ y_bits
    y2, z2 = gray(y_label), paired(paired((z + core) % 8) ^ z_bits)
    return ((z2 - core) % 8, (y2 - core) % 4, x ^ xh, core, lat)


def shift_both_x(block):
    return lax.ppermute(block, ("xh", "lat"), [(i, 3 - i) for i in range(4)])


def exchange(block, y_bits, z_bits, xh=0):
    route = []
    for i, at in enumerate(np.ndindex(*SIZES)):
        route.append((i, int(np.ravel_multi_index(flipped(at, y_bits, z_bits, xh), SIZES))))
    return lax.ppermute(block, ALL, route)


def per_device(tokens, land_mask, land_bias, qkv_weight, out_weight, cotangent):
    land = land_mask.T
    full, part, edge = (24, 12, 2, D), (21, 6, 2, D), (3, 6, 2, D)
    dma = pltpu.SemaphoreType.DMA

    main, lat, diag = call(
        tok_halo_kernel,
        [VM, ANY],
        [shaped((22, 6, 2, D)), shaped((4, 6, 2, D)), shaped((4, 6, 2, D))],
        scratch=[
            pltpu.VMEM((22, 6, 2, D), BF),
            pltpu.VMEM((4, 6, 2, D), BF),
            pltpu.VMEM((4, 6, 2, D), BF),
            dma((2, 5)),
        ],
        out_spec=ANY,
        limit=60,
        name="tok_halo",
    )(land, tokens)
    main, qkv_weight, out_weight = lax.optimization_barrier((main, qkv_weight, out_weight))
    main, lat, diag = shift(main, LON, -1), shift(lat, "lat", -1), shift_both(diag, -1)
    wqkv, wout = call(
        weights_kernel,
        [ANY] * 2,
        [shaped((D, 3 * HD)), shaped((HD, D))],
        scratch=[dma((5,))],
        limit=16,
        name="weights",
    )(qkv_weight, out_weight)
    lat, diag, cotangent, wqkv = lax.optimization_barrier((lat, diag, cotangent, wqkv))
    cot_main, cot_lat, cot_diag = call(
        cot_halo_kernel,
        [ANY],
        [shaped(part), shaped(edge), shaped(edge)],
        scratch=[dma((5,))],
        out_spec=ANY,
        limit=16,
        name="cot_halo",
    )(cotangent)
    cot_main = shift(cot_main, LON, -1)
    cot_lat, cot_diag = shift(cot_lat, "lat", -1), shift_both(cot_diag, -1)

    nrm, inverse, qkv, attn, att, att_left = call(
        forward_kernel,
        [SM] + [VM] * 6,
        [
            shaped((TOK, D)),
            shaped((TOK, 128), F32),
            shaped((TOK, 3 * HD)),
            shaped((WINS, HEADS // 2, 2, WIN, WIN), F32),
            shaped((TOK, HD)),
            shaped((WINS, HALF, HD)),
        ],
        limit=16,
        flops=4 * 10**9,
        name="forward",
    )(land_bias, tokens, main, lat, diag, land, wqkv)

    chunks = (32, 16, 2 * D)
    keep, send, dqkv = call(
        backward_kernel,
        [VM] * 9,
        [shaped(chunks, F32), shaped(chunks), shaped((TOK, 3 * HD))],
        scratch=[pltpu.VMEM((TOK, D), BF), pltpu.VMEM((TOK, HD), BF)],
        limit=18,
        flops=4 * 10**9,
        name="backward",
    )(cotangent, cot_main, cot_lat, cot_diag, nrm, qkv, attn, att, wout)

    def summed(body, operands, rows, sent, sends, name, scratch=(), kind=F32, moved=8):
        kept, *rest = call(
            body,
            [VM] * len(operands),
            [shaped(rows, kind)] + [shaped(sent)] * sends,
            scratch=scratch,
            limit=16,
            name=name,
            moved=moved,
        )(*operands)
        return kept, rest

    arrived = shift(send, "core", 1)
    whole = (24, 6, 2, D)
    send, att = lax.optimization_barrier((send, att))
    att_left = shift(att_left, LON, 1)
    out_own, out_lat = call(
        out_kernel,
        [VM] * 2,
        [shaped(full), shaped(edge)],
        limit=16,
        flops=10**9,
        name="out",
    )(att, wout)
    out_lat, keep = lax.optimization_barrier((out_lat, keep))
    eighth, small = (8, 16, 2 * D), (2, 16, 2 * D)
    kept, sends = summed(core_kernel, (keep, arrived), eighth, eighth, 3, "sum_core")
    a = [exchange(s, dy, dz) for (dy, dz), s in zip(PEERS, sends)]
    dqkv, kept, att_left = lax.optimization_barrier((dqkv, kept, att_left))
    tok_own, tok_main, tok_lat = call(
        token_kernel,
        [VM] * 4,
        [shaped(full), shaped(whole), shaped(edge)],
        limit=16,
        flops=2 * 10**9,
        name="token_grad",
    )(dqkv, wqkv, nrm, inverse)
    tok_main = shift(tok_main, LON, 1)
    (out_main,) = call(
        home_kernel, [VM] * 2, [shaped(whole)], limit=16, flops=10**9, name="out_left"
    )(att_left, wout)
    out_main, kept = lax.optimization_barrier((out_main, kept))
    kept, sends = summed(middle_kernel, [kept] + a, small, small, 3, "sum_low")
    a = [exchange(s, 2 * dy, 2 * dz) for (dy, dz), s in zip(PEERS, sends)]
    kept, (s,) = summed(
        late_kernel, [kept] + a, small[1:], small[1:], 1, "sum_next", [pltpu.VMEM(small, F32)]
    )
    out_own, kept = lax.optimization_barrier((out_own, kept))
    block_out, grad_tokens, lat = call(
        gather_kernel,
        [ANY] * 6,
        [shaped(full), shaped(full), shaped((2, 3, 12, 2, D))],
        scratch=[dma((2, 3))],
        aliases={0: 0, 1: 1},
        out_spec=ANY,
        name="gather",
    )(out_own, tok_own, out_main, tok_main, out_lat, tok_lat)
    kept, (s,) = summed(
        ring_kernel,
        (kept, exchange(s, 0, 4)),
        (16, D),
        (16, D),
        1,
        "sum_z",
        [pltpu.VMEM((2, 8, 2 * D), F32)],
        BF,
        64,
    )
    a = [shift(kept, "lat", 1), shift(s, "xh", 1), shift_both_x(s)]
    grad_qkv, grad_out = call(
        last_kernel,
        [VM] * 4,
        [shaped((8, 3 * HD), F32), shaped((8, HD), F32)],
        name="sum_x",
    )(kept, *a)
    block_out, grad_tokens = call(
        finish_kernel,
        [ANY] * 3,
        [shaped(full), shaped(full)],
        scratch=[dma((2,))],
        aliases={0: 0, 1: 1},
        out_spec=ANY,
        name="assemble",
    )(block_out, grad_tokens, shift(lat, "lat", 1))
    return (block_out, grad_tokens, grad_qkv, grad_out.T)


def solution(mesh):
    fine = Mesh(mesh.devices.reshape(SIZES), ALL)
    grid = P("lat", LON, None, None)
    in_specs = (grid, P("lat", LON), P(), P(), P(), grid)
    out_specs = (grid, grid, P(LON, None), P(None, LON))
    return jax.shard_map(
        per_device, mesh=fine, in_specs=in_specs, out_specs=out_specs, check_vma=False
    )
```

```python
import math

import jax
import jax.numpy as jnp
import numpy as np
from jax import lax
from jax.experimental import pallas as pl
from jax.experimental.pallas import tpu as pltpu
from jax.sharding import Mesh, PartitionSpec as P

D = 1024
HEADS = 8
HSIZE = 64
HD = 512
WIN = 144
HALF = 72
WINS = 4
TOK = 576
SLAB = 128
TOKENS = 147456
GRAD_SCALE = 1.0 / math.sqrt(TOKENS)
FACTOR = HSIZE ** (-0.5)
FAR = -1e30
BF = jnp.bfloat16
F32 = jnp.float32
LON = ("z", "y", "xh", "core")
ALL = LON + ("lat",)
SIZES = (8, 4, 2, 2, 2)
PEERS = ((0, 1), (1, 0), (1, 1))


def nn(a, b):
    return lax.dot_general(a, b, (((1,), (0,)), ((), ())), preferred_element_type=F32)


def nt(a, b):
    return lax.dot_general(a, b, (((1,), (1,)), ((), ())), preferred_element_type=F32)


def tn(a, b):
    return lax.dot_general(a, b, (((0,), (0,)), ((), ())), preferred_element_type=F32)


def window_rows(own, main, lat, diag, w):
    if w < WINS - 1:
        parts = [own[3 + 6 * w : 9 + 6 * w, 6:12], main[6 * w : 6 * w + 6]]
    else:
        parts = [own[21:24, 6:12], lat[0:3], main[18:21], diag[0:3]]
    return jnp.concatenate([p.astype(F32).reshape(-1, D) for p in parts], 0)


def halo_copies(block, main, lat, diag, sems):
    copies = [
        pltpu.make_async_copy(block.at[3 + r : 6 + r, 0:6], main.at[r : r + 3], sems.at[r // 3])
        for r in range(0, 21, 3)
    ]
    copies.append(pltpu.make_async_copy(block.at[0:3, 6:12], lat.at[0:3], sems.at[7]))
    copies.append(pltpu.make_async_copy(block.at[0:3, 0:6], diag.at[0:3], sems.at[8]))
    return copies


def tok_halo_kernel(land, tok, main, lat, diag, main_v, lat_v, diag_v, sems):
    copies = halo_copies(tok, main_v, lat_v, diag_v, sems.at[0])
    for c in copies:
        c.start()
    by_row = jnp.concatenate([land[...].astype(F32), jnp.zeros((12, D - 24), F32)], 1)
    cells = jnp.broadcast_to(by_row[:, None, :], (12, 2, D)).astype(BF)
    main_v[21] = cells[0:6]
    lat_v[3] = cells[6:12]
    diag_v[3] = cells[0:6]
    parts = [(main_v, main, r, r + 3) for r in range(0, 18, 3)]
    parts += [(main_v, main, 18, 22), (lat_v, lat, 0, 4), (diag_v, diag, 0, 4)]
    done = []
    for i, (wide, ref, lo, hi) in enumerate(parts):
        copies[i].wait()
        done.append(pltpu.make_async_copy(wide.at[lo:hi], ref.at[lo:hi], sems.at[1, i]))
        done[-1].start()
    for c in done:
        c.wait()


def cot_halo_kernel(cot, main, lat, diag, sems):
    copies = halo_copies(cot, main, lat, diag, sems)
    for c in copies:
        c.start()
    for c in copies:
        c.wait()


def weights_kernel(wqkv_hbm, wout_hbm, wqkv, wout, sems):
    copies = [pltpu.make_async_copy(wout_hbm, wout, sems.at[4])]
    for i in range(4):
        rows = slice(256 * i, 256 * i + 256)
        copies.append(pltpu.make_async_copy(wqkv_hbm.at[rows], wqkv.at[rows], sems.at[i]))
    for c in copies:
        c.start()
    for c in copies:
        c.wait()


def land_column(cells, first_row, rows):
    count = rows * 12
    token = lax.broadcasted_iota(jnp.int32, (count, 128), 0)
    lane = lax.broadcasted_iota(jnp.int32, (count, 128), 1)
    cell = lax.broadcasted_iota(jnp.int32, (count, 12), 0) % 12
    pick = (cell == lax.broadcasted_iota(jnp.int32, (count, 12), 1)).astype(F32)
    wide = nn(pick, cells)
    return jnp.sum(jnp.where(lane == token // 12 + first_row, wide, 0.0), 1, keepdims=True)


def forward_kernel(
    bias, tok, main, lat, diag, land, wqkv,
    nrm, inv_s, qkv, attn_s, att, att_left,
):
    for w in range(WINS):
        x = window_rows(tok, main, lat, diag, w)
        centred = x - jnp.mean(x, -1, keepdims=True)
        inverse = lax.rsqrt(jnp.mean(centred * centred, -1, keepdims=True) + 1e-05)
        rows = slice(WIN * w, WIN * w + WIN)
        inv_s[rows] = jnp.broadcast_to(inverse, (WIN, 128))
        nrm[rows] = (centred * inverse).astype(BF)
    for i in range(3):
        cols = slice(HD * i, HD * i + HD)
        r = nn(nrm[...], wqkv[:, cols])
        qkv[:, cols] = (r.astype(BF) * FACTOR).astype(BF) if i == 0 else r.astype(BF)

    by_row = jnp.concatenate([land[...].astype(F32), jnp.zeros((12, 104), F32)], 1)
    own_cells = jnp.broadcast_to(by_row[6:12][:, None, :], (6, 2, 128)).reshape(12, 128)
    main_cells, lat_cells, diag_cells = (
        r[r.shape[0] - 1, :, :, 0:128].astype(F32).reshape(12, 128) for r in (main, lat, diag)
    )
    first = lax.broadcasted_iota(jnp.int32, (WIN, SLAB), 1) < HSIZE
    zero = jnp.zeros((WIN, SLAB), BF)
    for w in range(WINS):
        rows = slice(WIN * w, WIN * w + WIN)
        if w < WINS - 1:
            parts = [land_column(own_cells, 3 + 6 * w, 6), land_column(main_cells, 3 + 6 * w, 6)]
            mask = None
        else:
            parts = [
                land_column(c, at, 3)
                for c, at in ((own_cells, 21), (lat_cells, 0), (main_cells, 21), (diag_cells, 0))
            ]
            k_at = lax.broadcasted_iota(jnp.int32, (WIN, WIN), 0) % HALF
            q_at = lax.broadcasted_iota(jnp.int32, (WIN, WIN), 1) % HALF
            apart = (k_at >= HALF // 2) != (q_at >= HALF // 2)
            mask = jnp.where(jnp.logical_and(apart, lax.axis_index("lat") == 1), FAR, 0.0)
        land_key = jnp.broadcast_to(jnp.concatenate(parts, 0), (WIN, WIN))
        for s in range(HEADS // 2):
            q = qkv[rows, SLAB * s : SLAB * s + SLAB]
            k = qkv[rows, HD + SLAB * s : HD + SLAB * s + SLAB]
            v = qkv[rows, 2 * HD + SLAB * s : 2 * HD + SLAB * s + SLAB]
            both = jnp.concatenate([jnp.where(first, k, zero), jnp.where(first, zero, k)], 0)
            sc = nt(both, q).reshape(2, WIN, WIN)
            sc = jnp.stack([sc[e] + land_key * bias[2 * s + e] for e in range(2)])
            if mask is not None:
                sc = sc + mask[None]
            ex = jnp.exp(sc - jnp.max(sc, 1, keepdims=True))
            attn = ex * (1.0 / jnp.sum(ex, 1, keepdims=True))
            attn_s[w, s] = attn
            attn_b = attn.astype(BF)
            o = jnp.where(first, tn(attn_b[0], v), tn(attn_b[1], v))
            att[rows, SLAB * s : SLAB * s + SLAB] = o.astype(BF)
            att_left[w, :, SLAB * s : SLAB * s + SLAB] = o[HALF:].astype(BF)


def backward_kernel(
    cot, main, lat, diag, nrm, qkv, attn_s, att, wout,
    keep, send, dqkv, cotb, datt,
):
    core = lax.axis_index("core")
    for w in range(WINS):
        cotb[WIN * w : WIN * w + WIN] = window_rows(cot, main, lat, diag, w).astype(BF)
    datt[...] = nt(cotb[...], wout[...]).astype(BF)

    first = lax.broadcasted_iota(jnp.int32, (WIN, SLAB), 1) < HSIZE
    zero = jnp.zeros((WIN, SLAB), BF)
    for w in range(WINS):
        rows = slice(WIN * w, WIN * w + WIN)
        for s in range(HEADS // 2):
            q_cols, k_cols, v_cols = (
                slice(HD * i + SLAB * s, HD * i + SLAB * s + SLAB) for i in range(3)
            )
            q, k, v = qkv[rows, q_cols], qkv[rows, k_cols], qkv[rows, v_cols]
            do = datt[rows, q_cols]
            attn = attn_s[w, s]
            both = jnp.concatenate([jnp.where(first, v, zero), jnp.where(first, zero, v)], 0)
            d_attn = nt(both, do).reshape(2, WIN, WIN)
            delta = jnp.sum(attn * d_attn, 1, keepdims=True)
            d_sc = (attn * (d_attn - delta)).astype(BF)
            d_v = nn(attn.astype(BF).reshape(2 * WIN, WIN), do)
            d_k = nn(d_sc.reshape(2 * WIN, WIN), q)
            d_q = jnp.where(first, tn(d_sc[0], k), tn(d_sc[1], k))
            dqkv[rows, q_cols] = (d_q * FACTOR).astype(BF)
            dqkv[rows, k_cols] = jnp.where(first, d_k[:WIN], d_k[WIN:]).astype(BF)
            dqkv[rows, v_cols] = jnp.where(first, d_v[:WIN], d_v[WIN:]).astype(BF)

    def put(r, i, lo):
        wide = r.shape[1]
        r = (r * GRAD_SCALE).reshape(2, 4, 2, 2, 8, wide)
        cols = slice(lo, lo + wide)
        for z in range(2):
            for y in range(4):
                even = r[z, y, :, 0].reshape(16, wide)
                odd = r[z, y, :, 1].reshape(16, wide)
                at = y * 8 + 2 * i + z
                keep[at, :, cols] = jnp.where(core == 0, even, odd)
                send[at, :, cols] = jnp.where(core == 0, odd, even).astype(BF)

    for i in range(4):
        feats = slice(256 * i, 256 * i + 256)
        put(tn(nrm[:, feats], dqkv[...]), i, 0)
        put(tn(cotb[:, feats], att[...]), i, 3 * HD)


def store_rows(r, own, main, lat, w):
    r = r.astype(BF)
    if w < WINS - 1:
        own[3 + 6 * w : 9 + 6 * w, 6:12] = r[:HALF].reshape(6, 6, 2, D)
        main[6 * w : 6 * w + 6] = r[HALF:].reshape(6, 6, 2, D)
    else:
        own[21:24, 6:12] = r[:36].reshape(3, 6, 2, D)
        lat[...] = r[36:72].reshape(3, 6, 2, D)
        main[18:21] = r[72:108].reshape(3, 6, 2, D)
        main[21:24] = r[108:].reshape(3, 6, 2, D)


def out_kernel(att, wout, own, lat):
    for w in range(WINS):
        r = nn(att[WIN * w : WIN * w + 80], wout[...]).astype(BF)
        if w < WINS - 1:
            own[3 + 6 * w : 9 + 6 * w, 6:12] = r[:HALF].reshape(6, 6, 2, D)
        else:
            own[21:24, 6:12] = r[:36].reshape(3, 6, 2, D)
            lat[...] = r[36:72].reshape(3, 6, 2, D)


def home_kernel(att_left, wout, main):
    for w in range(WINS):
        main[6 * w : 6 * w + 6] = nn(att_left[w], wout[...]).astype(BF).reshape(6, 6, 2, D)


def token_kernel(dqkv, wqkv, nrm, inv_s, own, main, lat):
    for w in range(WINS):
        rows = slice(WIN * w, WIN * w + WIN)
        d_normed = nt(dqkv[rows], wqkv[...])
        unit = nrm[rows].astype(F32)
        d_flat = inv_s[rows, 0:1] * (
            d_normed
            - jnp.mean(d_normed, -1, keepdims=True)
            - unit * jnp.mean(d_normed * unit, -1, keepdims=True)
        )
        store_rows(d_flat, own, main, lat, w)


def gray(label):
    return label ^ (label >> 1)


def paired(z):
    return 2 * gray(z >> 1) + (z & 1)


def labels():
    core = lax.axis_index("core")
    y = gray((lax.axis_index("y") + core) & 3)
    return y, paired((lax.axis_index("z") + core) & 7), core


def core_kernel(keep, arrived, kept, s1, s2, s3):
    y_label, z_label, core = labels()
    for (dy, dz), ref in zip(((0, 0),) + PEERS, (kept, s1, s2, s3)):
        y0, z0 = (y_label & 1) ^ dy, (z_label & 1) ^ dz
        for n, (y1, z1, z2) in enumerate(np.ndindex(2, 2, 2)):
            y = (gray(2 * y1 + y0) - core + 4) & 3
            z = (paired(4 * z2 + 2 * z1 + z0) - core + 8) & 7
            at = y * 8 + z
            ref[n] = (keep[at] + arrived[at].astype(F32)).astype(ref.dtype)


def middle_kernel(keep, a1, a2, a3, kept, s1, s2, s3):
    def total(i):
        at = pl.ds(2 * i, 2)
        return keep[at] + a1[at].astype(F32) + a2[at].astype(F32) + a3[at].astype(F32)

    y_label, z_label, _ = labels()
    mine = (y_label >> 1) * 2 + ((z_label >> 1) & 1)
    kept[...] = total(mine)
    for n, ref in enumerate((s1, s2, s3)):
        ref[...] = total(mine ^ (n + 1)).astype(BF)


def late_kernel(keep, a1, a2, a3, kept, send, work):
    work[...] = keep[...] + a1[...].astype(F32) + a2[...].astype(F32) + a3[...].astype(F32)
    _, z_label, _ = labels()
    z = z_label >> 2
    kept[...] = work[z]
    send[...] = work[z ^ 1].astype(BF)


def ring_kernel(keep, arrived, kept, send, work):
    total = keep[...] + arrived[...].astype(F32)
    work[...] = total.reshape(2, 8, 2 * D)
    x = lax.axis_index("xh")
    for ref, at in ((kept, x), (send, x ^ 1)):
        r = work[at]
        ref[...] = jnp.concatenate([r[:, :D], r[:, D:]], 0).astype(BF)


def last_kernel(keep, a1, a2, a3, qkv, out):
    wide = [r[...].astype(F32) for r in (keep, a1, a2, a3)]
    total = (wide[0] + wide[1]) + (wide[2] + wide[3])
    qkv[...] = jnp.concatenate([total[:8], total[8:, :HD]], 1)
    out[...] = total[8:, HD:]


def gather_kernel(out_own, tok_own, o_main, t_main, o_lat, t_lat, out, tok, lat, sems):
    copies = []
    for i, (ref, main, edge) in enumerate(((out, o_main, o_lat), (tok, t_main, t_lat))):
        copies += [
            pltpu.make_async_copy(main.at[0:21], ref.at[3:24, 0:6], sems.at[i, 0]),
            pltpu.make_async_copy(main.at[21:24], lat.at[i, :, 0:6], sems.at[i, 1]),
            pltpu.make_async_copy(edge, lat.at[i, :, 6:12], sems.at[i, 2]),
        ]
    for c in copies:
        c.start()
    for c in copies:
        c.wait()


def finish_kernel(out_part, tok_part, lat, out, tok, sems):
    copies = [
        pltpu.make_async_copy(lat.at[i], ref.at[0:3], sems.at[i])
        for i, ref in enumerate((out, tok))
    ]
    for c in copies:
        c.start()
    for c in copies:
        c.wait()


VM = pl.BlockSpec(memory_space=pltpu.VMEM)
SM = pl.BlockSpec(memory_space=pltpu.SMEM)
ANY = pl.BlockSpec(memory_space=pl.ANY)


def shaped(dims, kind=BF):
    return jax.ShapeDtypeStruct(dims, kind)


def call(body, ins, outs, scratch=(), limit=16, flops=0, name=None, aliases=None, out_spec=VM, moved=8):
    return pl.pallas_call(
        body,
        in_specs=ins,
        out_specs=out_spec if isinstance(out_spec, list) else [out_spec] * len(outs),
        out_shape=outs,
        scratch_shapes=list(scratch),
        input_output_aliases=aliases or {},
        compiler_params=pltpu.CompilerParams(vmem_limit_bytes=limit * 2**20),
        cost_estimate=pl.CostEstimate(flops=0, bytes_accessed=moved * 2**20, transcendentals=0),
        name=name,
    )


def shift(block, axis, step):
    count = lax.axis_size(axis)
    return lax.ppermute(block, axis, [(i, (i + step) % count) for i in range(count)])


def shift_both(block, step):
    count = lax.axis_size(LON)
    route = [
        (i * 2 + b, ((i + step) % count) * 2 + 1 - b) for i in range(count) for b in range(2)
    ]
    return lax.ppermute(block, ALL, route)


def flipped(at, y_bits, z_bits, xh):
    z, y, x, core, lat = at
    y_label = gray((y + core) % 4) ^ y_bits
    y2, z2 = gray(y_label), paired(paired((z + core) % 8) ^ z_bits)
    return ((z2 - core) % 8, (y2 - core) % 4, x ^ xh, core, lat)


def shift_both_x(block):
    return lax.ppermute(block, ("xh", "lat"), [(i, 3 - i) for i in range(4)])


def exchange(block, y_bits, z_bits, xh=0):
    route = []
    for i, at in enumerate(np.ndindex(*SIZES)):
        route.append((i, int(np.ravel_multi_index(flipped(at, y_bits, z_bits, xh), SIZES))))
    return lax.ppermute(block, ALL, route)


def per_device(tokens, land_mask, land_bias, qkv_weight, out_weight, cotangent):
    land = land_mask.T
    full, part, edge = (24, 12, 2, D), (21, 6, 2, D), (3, 6, 2, D)
    dma = pltpu.SemaphoreType.DMA

    main, lat, diag = call(
        tok_halo_kernel,
        [VM, ANY],
        [shaped((22, 6, 2, D)), shaped((4, 6, 2, D)), shaped((4, 6, 2, D))],
        scratch=[
            pltpu.VMEM((22, 6, 2, D), BF),
            pltpu.VMEM((4, 6, 2, D), BF),
            pltpu.VMEM((4, 6, 2, D), BF),
            dma((2, 9)),
        ],
        out_spec=ANY,
        limit=60,
        name="tok_halo",
    )(land, tokens)
    main, qkv_weight, out_weight = lax.optimization_barrier((main, qkv_weight, out_weight))
    main, lat, diag = shift(main, LON, -1), shift(lat, "lat", -1), shift_both(diag, -1)
    wqkv, wout = call(
        weights_kernel,
        [ANY] * 2,
        [shaped((D, 3 * HD)), shaped((HD, D))],
        scratch=[dma((5,))],
        limit=16,
        name="weights",
    )(qkv_weight, out_weight)
    lat, diag, cotangent, wqkv = lax.optimization_barrier((lat, diag, cotangent, wqkv))
    cot_main, cot_lat, cot_diag = call(
        cot_halo_kernel,
        [ANY],
        [shaped(part), shaped(edge), shaped(edge)],
        scratch=[dma((9,))],
        out_spec=ANY,
        limit=16,
        name="cot_halo",
    )(cotangent)
    cot_main = shift(cot_main, LON, -1)
    cot_lat, cot_diag = shift(cot_lat, "lat", -1), shift_both(cot_diag, -1)

    nrm, inverse, qkv, attn, att, att_left = call(
        forward_kernel,
        [SM] + [VM] * 6,
        [
            shaped((TOK, D)),
            shaped((TOK, 128), F32),
            shaped((TOK, 3 * HD)),
            shaped((WINS, HEADS // 2, 2, WIN, WIN), F32),
            shaped((TOK, HD)),
            shaped((WINS, HALF, HD)),
        ],
        limit=16,
        flops=4 * 10**9,
        name="forward",
    )(land_bias, tokens, main, lat, diag, land, wqkv)

    chunks = (32, 16, 2 * D)
    keep, send, dqkv = call(
        backward_kernel,
        [VM] * 9,
        [shaped(chunks, F32), shaped(chunks), shaped((TOK, 3 * HD))],
        scratch=[pltpu.VMEM((TOK, D), BF), pltpu.VMEM((TOK, HD), BF)],
        limit=18,
        flops=4 * 10**9,
        name="backward",
    )(cotangent, cot_main, cot_lat, cot_diag, nrm, qkv, attn, att, wout)

    def summed(body, operands, rows, sent, sends, name, scratch=(), kind=F32, moved=8):
        kept, *rest = call(
            body,
            [VM] * len(operands),
            [shaped(rows, kind)] + [shaped(sent)] * sends,
            scratch=scratch,
            limit=16,
            name=name,
            moved=moved,
        )(*operands)
        return kept, rest

    arrived = shift(send, "core", 1)
    whole = (24, 6, 2, D)
    send, att = lax.optimization_barrier((send, att))
    att_left = shift(att_left, LON, 1)
    out_own, out_lat = call(
        out_kernel,
        [VM] * 2,
        [shaped(full), shaped(edge)],
        limit=16,
        flops=10**9,
        name="out",
    )(att, wout)
    out_lat, keep = lax.optimization_barrier((out_lat, keep))
    eighth, small = (8, 16, 2 * D), (2, 16, 2 * D)
    kept, sends = summed(core_kernel, (keep, arrived), eighth, eighth, 3, "sum_core")
    a = [exchange(s, dy, dz) for (dy, dz), s in zip(PEERS, sends)]
    dqkv, kept, att_left = lax.optimization_barrier((dqkv, kept, att_left))
    tok_own, tok_main, tok_lat = call(
        token_kernel,
        [VM] * 4,
        [shaped(full), shaped(whole), shaped(edge)],
        limit=16,
        flops=2 * 10**9,
        name="token_grad",
    )(dqkv, wqkv, nrm, inverse)
    tok_main = shift(tok_main, LON, 1)
    (out_main,) = call(
        home_kernel, [VM] * 2, [shaped(whole)], limit=16, flops=10**9, name="out_left"
    )(att_left, wout)
    out_main, kept = lax.optimization_barrier((out_main, kept))
    kept, sends = summed(middle_kernel, [kept] + a, small, small, 3, "sum_low")
    a = [exchange(s, 2 * dy, 2 * dz) for (dy, dz), s in zip(PEERS, sends)]
    kept, (s,) = summed(
        late_kernel, [kept] + a, small[1:], small[1:], 1, "sum_next", [pltpu.VMEM(small, F32)]
    )
    out_own, kept = lax.optimization_barrier((out_own, kept))
    block_out, grad_tokens, lat = call(
        gather_kernel,
        [ANY] * 6,
        [shaped(full), shaped(full), shaped((2, 3, 12, 2, D))],
        scratch=[dma((2, 3))],
        aliases={0: 0, 1: 1},
        out_spec=ANY,
        name="gather",
    )(out_own, tok_own, out_main, tok_main, out_lat, tok_lat)
    kept, (s,) = summed(
        ring_kernel,
        (kept, exchange(s, 0, 4)),
        (16, D),
        (16, D),
        1,
        "sum_z",
        [pltpu.VMEM((2, 8, 2 * D), F32)],
        BF,
        64,
    )
    a = [shift(kept, "lat", 1), shift(s, "xh", 1), shift_both_x(s)]
    block_out, grad_tokens = call(
        finish_kernel,
        [ANY] * 3,
        [shaped(full), shaped(full)],
        scratch=[dma((2,))],
        aliases={0: 0, 1: 1},
        out_spec=ANY,
        name="assemble",
    )(block_out, grad_tokens, shift(lat, "lat", 1))
    block_out, kept = lax.optimization_barrier((block_out, kept))
    grad_qkv, grad_out = call(
        last_kernel,
        [VM] * 4,
        [shaped((8, 3 * HD), F32), shaped((8, HD), F32)],
        name="sum_x",
    )(kept, *a)
    return (block_out, grad_tokens, grad_qkv, grad_out.T)


def solution(mesh):
    fine = Mesh(mesh.devices.reshape(SIZES), ALL)
    grid = P("lat", LON, None, None)
    in_specs = (grid, P("lat", LON), P(), P(), P(), grid)
    out_specs = (grid, grid, P(LON, None), P(None, LON))
    return jax.shard_map(
        per_device, mesh=fine, in_specs=in_specs, out_specs=out_specs, check_vma=False
    )
```

```python
import math

import jax
import jax.numpy as jnp
import numpy as np
from jax import lax
from jax.experimental import pallas as pl
from jax.experimental.pallas import tpu as pltpu
from jax.sharding import Mesh, PartitionSpec as P

D = 1024
HEADS = 8
HSIZE = 64
HD = 512
WIN = 144
HALF = 72
WINS = 4
TOK = 576
SLAB = 128
TOKENS = 147456
GRAD_SCALE = 1.0 / math.sqrt(TOKENS)
FACTOR = HSIZE ** (-0.5)
FAR = -1e30
BF = jnp.bfloat16
F32 = jnp.float32
LON = ("z", "y", "xh", "core")
ALL = LON + ("lat",)
SIZES = (8, 4, 2, 2, 2)
PEERS = ((0, 1), (1, 0), (1, 1))


def nn(a, b):
    return lax.dot_general(a, b, (((1,), (0,)), ((), ())), preferred_element_type=F32)


def nt(a, b):
    return lax.dot_general(a, b, (((1,), (1,)), ((), ())), preferred_element_type=F32)


def tn(a, b):
    return lax.dot_general(a, b, (((0,), (0,)), ((), ())), preferred_element_type=F32)


def window_rows(own, main, lat, diag, w):
    if w < WINS - 1:
        parts = [own[3 + 6 * w : 9 + 6 * w, 6:12], main[6 * w : 6 * w + 6]]
    else:
        parts = [own[21:24, 6:12], lat[0:3], main[18:21], diag[0:3]]
    return jnp.concatenate([p.astype(F32).reshape(-1, D) for p in parts], 0)


def halo_copies(block, main, lat, diag, sems):
    return [
        pltpu.make_async_copy(block.at[3:10, 0:6], main.at[0:7], sems.at[0]),
        pltpu.make_async_copy(block.at[10:17, 0:6], main.at[7:14], sems.at[1]),
        pltpu.make_async_copy(block.at[17:24, 0:6], main.at[14:21], sems.at[2]),
        pltpu.make_async_copy(block.at[0:3, 6:12], lat.at[0:3], sems.at[3]),
        pltpu.make_async_copy(block.at[0:3, 0:6], diag.at[0:3], sems.at[4]),
    ]


def tok_halo_kernel(land, tok, main, lat, diag, main_v, lat_v, diag_v, sems):
    copies = halo_copies(tok, main_v, lat_v, diag_v, sems.at[0])
    for c in copies:
        c.start()
    by_row = jnp.concatenate([land[...].astype(F32), jnp.zeros((12, D - 24), F32)], 1)
    cells = jnp.broadcast_to(by_row[:, None, :], (12, 2, D)).astype(BF)
    main_v[21] = cells[0:6]
    lat_v[3] = cells[6:12]
    diag_v[3] = cells[0:6]
    done = []
    for i, (rows, wide, ref) in enumerate(
        (((0, 7), main_v, main), ((7, 14), main_v, main), ((14, 22), main_v, main),
         ((0, 4), lat_v, lat), ((0, 4), diag_v, diag))
    ):
        copies[i].wait()
        rows = slice(*rows)
        done.append(pltpu.make_async_copy(wide.at[rows], ref.at[rows], sems.at[1, i]))
        done[-1].start()
    for c in done:
        c.wait()


def cot_halo_kernel(cot, main, lat, diag, sems):
    copies = halo_copies(cot, main, lat, diag, sems)
    for c in copies:
        c.start()
    for c in copies:
        c.wait()


def weights_kernel(wqkv_hbm, wout_hbm, wqkv, wout, sems):
    copies = [pltpu.make_async_copy(wout_hbm, wout, sems.at[4])]
    for i in range(4):
        rows = slice(256 * i, 256 * i + 256)
        copies.append(pltpu.make_async_copy(wqkv_hbm.at[rows], wqkv.at[rows], sems.at[i]))
    for c in copies:
        c.start()
    for c in copies:
        c.wait()


def land_column(cells, first_row, rows):
    count = rows * 12
    token = lax.broadcasted_iota(jnp.int32, (count, 128), 0)
    lane = lax.broadcasted_iota(jnp.int32, (count, 128), 1)
    cell = lax.broadcasted_iota(jnp.int32, (count, 12), 0) % 12
    pick = (cell == lax.broadcasted_iota(jnp.int32, (count, 12), 1)).astype(F32)
    wide = nn(pick, cells)
    return jnp.sum(jnp.where(lane == token // 12 + first_row, wide, 0.0), 1, keepdims=True)


def forward_kernel(
    bias, tok, main, lat, diag, land, wqkv,
    nrm, inv_s, qkv, attn_s, att, att_left,
):
    for w in range(WINS):
        x = window_rows(tok, main, lat, diag, w)
        centred = x - jnp.mean(x, -1, keepdims=True)
        inverse = lax.rsqrt(jnp.mean(centred * centred, -1, keepdims=True) + 1e-05)
        rows = slice(WIN * w, WIN * w + WIN)
        inv_s[rows] = jnp.broadcast_to(inverse, (WIN, 128))
        nrm[rows] = (centred * inverse).astype(BF)
    for i in range(3):
        cols = slice(HD * i, HD * i + HD)
        r = nn(nrm[...], wqkv[:, cols])
        qkv[:, cols] = (r.astype(BF) * FACTOR).astype(BF) if i == 0 else r.astype(BF)

    by_row = jnp.concatenate([land[...].astype(F32), jnp.zeros((12, 104), F32)], 1)
    own_cells = jnp.broadcast_to(by_row[6:12][:, None, :], (6, 2, 128)).reshape(12, 128)
    main_cells, lat_cells, diag_cells = (
        r[r.shape[0] - 1, :, :, 0:128].astype(F32).reshape(12, 128) for r in (main, lat, diag)
    )
    first = lax.broadcasted_iota(jnp.int32, (WIN, SLAB), 1) < HSIZE
    zero = jnp.zeros((WIN, SLAB), BF)
    for w in range(WINS):
        rows = slice(WIN * w, WIN * w + WIN)
        if w < WINS - 1:
            parts = [land_column(own_cells, 3 + 6 * w, 6), land_column(main_cells, 3 + 6 * w, 6)]
            mask = None
        else:
            parts = [
                land_column(c, at, 3)
                for c, at in ((own_cells, 21), (lat_cells, 0), (main_cells, 21), (diag_cells, 0))
            ]
            k_at = lax.broadcasted_iota(jnp.int32, (WIN, WIN), 0) % HALF
            q_at = lax.broadcasted_iota(jnp.int32, (WIN, WIN), 1) % HALF
            apart = (k_at >= HALF // 2) != (q_at >= HALF // 2)
            mask = jnp.where(jnp.logical_and(apart, lax.axis_index("lat") == 1), FAR, 0.0)
        land_key = jnp.broadcast_to(jnp.concatenate(parts, 0), (WIN, WIN))
        for s in range(HEADS // 2):
            q = qkv[rows, SLAB * s : SLAB * s + SLAB]
            k = qkv[rows, HD + SLAB * s : HD + SLAB * s + SLAB]
            v = qkv[rows, 2 * HD + SLAB * s : 2 * HD + SLAB * s + SLAB]
            both = jnp.concatenate([jnp.where(first, k, zero), jnp.where(first, zero, k)], 0)
            sc = nt(both, q).reshape(2, WIN, WIN)
            sc = jnp.stack([sc[e] + land_key * bias[2 * s + e] for e in range(2)])
            if mask is not None:
                sc = sc + mask[None]
            ex = jnp.exp(sc - jnp.max(sc, 1, keepdims=True))
            attn = ex * (1.0 / jnp.sum(ex, 1, keepdims=True))
            attn_s[w, s] = attn
            attn_b = attn.astype(BF)
            o = jnp.where(first, tn(attn_b[0], v), tn(attn_b[1], v))
            att[rows, SLAB * s : SLAB * s + SLAB] = o.astype(BF)
            att_left[w, :, SLAB * s : SLAB * s + SLAB] = o[HALF:].astype(BF)


def backward_kernel(
    cot, main, lat, diag, nrm, qkv, attn_s, att, wout,
    keep, send, dqkv, cotb, datt,
):
    core = lax.axis_index("core")
    for w in range(WINS):
        cotb[WIN * w : WIN * w + WIN] = window_rows(cot, main, lat, diag, w).astype(BF)
    datt[...] = nt(cotb[...], wout[...]).astype(BF)

    first = lax.broadcasted_iota(jnp.int32, (WIN, SLAB), 1) < HSIZE
    zero = jnp.zeros((WIN, SLAB), BF)
    for w in range(WINS):
        rows = slice(WIN * w, WIN * w + WIN)
        for s in range(HEADS // 2):
            q_cols, k_cols, v_cols = (
                slice(HD * i + SLAB * s, HD * i + SLAB * s + SLAB) for i in range(3)
            )
            q, k, v = qkv[rows, q_cols], qkv[rows, k_cols], qkv[rows, v_cols]
            do = datt[rows, q_cols]
            attn = attn_s[w, s]
            both = jnp.concatenate([jnp.where(first, v, zero), jnp.where(first, zero, v)], 0)
            d_attn = nt(both, do).reshape(2, WIN, WIN)
            delta = jnp.sum(attn * d_attn, 1, keepdims=True)
            d_sc = (attn * (d_attn - delta)).astype(BF)
            d_v = nn(attn.astype(BF).reshape(2 * WIN, WIN), do)
            d_k = nn(d_sc.reshape(2 * WIN, WIN), q)
            d_q = jnp.where(first, tn(d_sc[0], k), tn(d_sc[1], k))
            dqkv[rows, q_cols] = (d_q * FACTOR).astype(BF)
            dqkv[rows, k_cols] = jnp.where(first, d_k[:WIN], d_k[WIN:]).astype(BF)
            dqkv[rows, v_cols] = jnp.where(first, d_v[:WIN], d_v[WIN:]).astype(BF)

    def put(r, i, lo):
        wide = r.shape[1]
        r = r.reshape(2, 4, 2, 2, 8, wide)
        cols = slice(lo, lo + wide)
        for z in range(2):
            for y in range(4):
                even = r[z, y, :, 0].reshape(16, wide)
                odd = r[z, y, :, 1].reshape(16, wide)
                at = y * 8 + 2 * i + z
                keep[at, :, cols] = jnp.where(core == 0, even, odd)
                send[at, :, cols] = jnp.where(core == 0, odd, even).astype(BF)

    for i in range(4):
        feats = slice(256 * i, 256 * i + 256)
        put(tn(nrm[:, feats], dqkv[...]), i, 0)
        put(tn(cotb[:, feats], att[...]), i, 3 * HD)


def store_rows(r, own, main, lat, w):
    r = r.astype(BF)
    if w < WINS - 1:
        own[3 + 6 * w : 9 + 6 * w, 6:12] = r[:HALF].reshape(6, 6, 2, D)
        main[6 * w : 6 * w + 6] = r[HALF:].reshape(6, 6, 2, D)
    else:
        own[21:24, 6:12] = r[:36].reshape(3, 6, 2, D)
        lat[...] = r[36:72].reshape(3, 6, 2, D)
        main[18:21] = r[72:108].reshape(3, 6, 2, D)
        main[21:24] = r[108:].reshape(3, 6, 2, D)


def out_kernel(att, wout, own, lat):
    for w in range(WINS):
        r = nn(att[WIN * w : WIN * w + 80], wout[...]).astype(BF)
        if w < WINS - 1:
            own[3 + 6 * w : 9 + 6 * w, 6:12] = r[:HALF].reshape(6, 6, 2, D)
        else:
            own[21:24, 6:12] = r[:36].reshape(3, 6, 2, D)
            lat[...] = r[36:72].reshape(3, 6, 2, D)


def home_kernel(att_left, wout, main):
    for w in range(WINS):
        main[6 * w : 6 * w + 6] = nn(att_left[w], wout[...]).astype(BF).reshape(6, 6, 2, D)


def token_kernel(dqkv, wqkv, nrm, inv_s, own, main, lat):
    for w in range(WINS):
        rows = slice(WIN * w, WIN * w + WIN)
        d_normed = nt(dqkv[rows], wqkv[...])
        unit = nrm[rows].astype(F32)
        d_flat = inv_s[rows, 0:1] * (
            d_normed
            - jnp.mean(d_normed, -1, keepdims=True)
            - unit * jnp.mean(d_normed * unit, -1, keepdims=True)
        )
        store_rows(d_flat, own, main, lat, w)


def gray(label):
    return label ^ (label >> 1)


def paired(z):
    return 2 * gray(z >> 1) + (z & 1)


def labels():
    core = lax.axis_index("core")
    y = gray((lax.axis_index("y") + core) & 3)
    return y, paired((lax.axis_index("z") + core) & 7), core


def core_kernel(keep, arrived, kept, s1, s2, s3):
    y_label, z_label, core = labels()
    for (dy, dz), ref in zip(((0, 0),) + PEERS, (kept, s1, s2, s3)):
        y0, z0 = (y_label & 1) ^ dy, (z_label & 1) ^ dz
        for n, (y1, z1, z2) in enumerate(np.ndindex(2, 2, 2)):
            y = (gray(2 * y1 + y0) - core + 4) & 3
            z = (paired(4 * z2 + 2 * z1 + z0) - core + 8) & 7
            at = y * 8 + z
            ref[n] = (keep[at] + arrived[at].astype(F32)).astype(ref.dtype)


def middle_kernel(keep, a1, a2, a3, kept, s1, s2, s3):
    def total(i):
        at = pl.ds(2 * i, 2)
        return keep[at] + a1[at].astype(F32) + a2[at].astype(F32) + a3[at].astype(F32)

    y_label, z_label, _ = labels()
    mine = (y_label >> 1) * 2 + ((z_label >> 1) & 1)
    kept[...] = total(mine)
    for n, ref in enumerate((s1, s2, s3)):
        ref[...] = total(mine ^ (n + 1)).astype(BF)


def late_kernel(keep, a1, a2, a3, kept, send, work):
    work[...] = keep[...] + a1[...].astype(F32) + a2[...].astype(F32) + a3[...].astype(F32)
    _, z_label, _ = labels()
    z = z_label >> 2
    kept[...] = work[z]
    send[...] = work[z ^ 1].astype(BF)


def ring_kernel(keep, arrived, kept, send, work):
    total = keep[...] + arrived[...].astype(F32)
    work[...] = total.reshape(2, 8, 2 * D)
    x = lax.axis_index("xh")
    for ref, at in ((kept, x), (send, x ^ 1)):
        r = work[at]
        ref[...] = jnp.concatenate([r[:, :D], r[:, D:]], 0).astype(BF)


def last_kernel(keep, a1, a2, a3, qkv, out):
    wide = [r[...].astype(F32) for r in (keep, a1, a2, a3)]
    total = ((wide[0] + wide[1]) + (wide[2] + wide[3])) * GRAD_SCALE
    qkv[...] = jnp.concatenate([total[:8], total[8:, :HD]], 1)
    out[...] = total[8:, HD:]


def gather_kernel(o_main, t_main, o_lat, t_lat, lat, sems):
    copies = []
    for i, (main, edge) in enumerate(((o_main, o_lat), (t_main, t_lat))):
        copies += [
            pltpu.make_async_copy(main.at[21:24], lat.at[i, :, 0:6], sems.at[i, 0]),
            pltpu.make_async_copy(edge, lat.at[i, :, 6:12], sems.at[i, 1]),
        ]
    for c in copies:
        c.start()
    for c in copies:
        c.wait()


def finish_kernel(out_own, tok_own, o_main, t_main, lat, out, tok, sems):
    copies = []
    for i, (ref, main) in enumerate(((out, o_main), (tok, t_main))):
        copies += [
            pltpu.make_async_copy(main.at[0:21], ref.at[3:24, 0:6], sems.at[i, 0]),
            pltpu.make_async_copy(lat.at[i], ref.at[0:3], sems.at[i, 1]),
        ]
    for c in copies:
        c.start()
    for c in copies:
        c.wait()


VM = pl.BlockSpec(memory_space=pltpu.VMEM)
SM = pl.BlockSpec(memory_space=pltpu.SMEM)
ANY = pl.BlockSpec(memory_space=pl.ANY)


def shaped(dims, kind=BF):
    return jax.ShapeDtypeStruct(dims, kind)


def call(body, ins, outs, scratch=(), limit=16, flops=0, name=None, aliases=None, out_spec=VM, moved=8):
    return pl.pallas_call(
        body,
        in_specs=ins,
        out_specs=out_spec if isinstance(out_spec, list) else [out_spec] * len(outs),
        out_shape=outs,
        scratch_shapes=list(scratch),
        input_output_aliases=aliases or {},
        compiler_params=pltpu.CompilerParams(vmem_limit_bytes=limit * 2**20),
        cost_estimate=pl.CostEstimate(flops=0, bytes_accessed=moved * 2**20, transcendentals=0),
        name=name,
    )


def shift(block, axis, step):
    count = lax.axis_size(axis)
    return lax.ppermute(block, axis, [(i, (i + step) % count) for i in range(count)])


def shift_both(block, step):
    count = lax.axis_size(LON)
    route = [
        (i * 2 + b, ((i + step) % count) * 2 + 1 - b) for i in range(count) for b in range(2)
    ]
    return lax.ppermute(block, ALL, route)


def flipped(at, y_bits, z_bits, xh):
    z, y, x, core, lat = at
    y_label = gray((y + core) % 4) ^ y_bits
    y2, z2 = gray(y_label), paired(paired((z + core) % 8) ^ z_bits)
    return ((z2 - core) % 8, (y2 - core) % 4, x ^ xh, core, lat)


def shift_both_x(block):
    return lax.ppermute(block, ("xh", "lat"), [(i, 3 - i) for i in range(4)])


def exchange(block, y_bits, z_bits, xh=0):
    route = []
    for i, at in enumerate(np.ndindex(*SIZES)):
        route.append((i, int(np.ravel_multi_index(flipped(at, y_bits, z_bits, xh), SIZES))))
    return lax.ppermute(block, ALL, route)


def per_device(tokens, land_mask, land_bias, qkv_weight, out_weight, cotangent):
    land = land_mask.T
    full, part, edge = (24, 12, 2, D), (21, 6, 2, D), (3, 6, 2, D)
    dma = pltpu.SemaphoreType.DMA

    main, lat, diag = call(
        tok_halo_kernel,
        [VM, ANY],
        [shaped((22, 6, 2, D)), shaped((4, 6, 2, D)), shaped((4, 6, 2, D))],
        scratch=[
            pltpu.VMEM((22, 6, 2, D), BF),
            pltpu.VMEM((4, 6, 2, D), BF),
            pltpu.VMEM((4, 6, 2, D), BF),
            dma((2, 5)),
        ],
        out_spec=ANY,
        limit=60,
        name="tok_halo",
    )(land, tokens)
    main, qkv_weight, out_weight = lax.optimization_barrier((main, qkv_weight, out_weight))
    main, lat, diag = shift(main, LON, -1), shift(lat, "lat", -1), shift_both(diag, -1)
    wqkv, wout = call(
        weights_kernel,
        [ANY] * 2,
        [shaped((D, 3 * HD)), shaped((HD, D))],
        scratch=[dma((5,))],
        limit=16,
        name="weights",
    )(qkv_weight, out_weight)
    lat, diag, cotangent, wqkv = lax.optimization_barrier((lat, diag, cotangent, wqkv))
    cot_main, cot_lat, cot_diag = call(
        cot_halo_kernel,
        [ANY],
        [shaped(part), shaped(edge), shaped(edge)],
        scratch=[dma((5,))],
        out_spec=ANY,
        limit=16,
        name="cot_halo",
    )(cotangent)
    cot_main = shift(cot_main, LON, -1)
    cot_lat, cot_diag = shift(cot_lat, "lat", -1), shift_both(cot_diag, -1)

    nrm, inverse, qkv, attn, att, att_left = call(
        forward_kernel,
        [SM] + [VM] * 6,
        [
            shaped((TOK, D)),
            shaped((TOK, 128), F32),
            shaped((TOK, 3 * HD)),
            shaped((WINS, HEADS // 2, 2, WIN, WIN), F32),
            shaped((TOK, HD)),
            shaped((WINS, HALF, HD)),
        ],
        limit=16,
        flops=4 * 10**9,
        name="forward",
    )(land_bias, tokens, main, lat, diag, land, wqkv)

    chunks = (32, 16, 2 * D)
    keep, send, dqkv = call(
        backward_kernel,
        [VM] * 9,
        [shaped(chunks, F32), shaped(chunks), shaped((TOK, 3 * HD))],
        scratch=[pltpu.VMEM((TOK, D), BF), pltpu.VMEM((TOK, HD), BF)],
        limit=18,
        flops=4 * 10**9,
        name="backward",
    )(cotangent, cot_main, cot_lat, cot_diag, nrm, qkv, attn, att, wout)

    def summed(body, operands, rows, sent, sends, name, scratch=(), kind=F32, moved=8):
        kept, *rest = call(
            body,
            [VM] * len(operands),
            [shaped(rows, kind)] + [shaped(sent)] * sends,
            scratch=scratch,
            limit=16,
            name=name,
            moved=moved,
        )(*operands)
        return kept, rest

    arrived = shift(send, "core", 1)
    whole = (24, 6, 2, D)
    send, att = lax.optimization_barrier((send, att))
    att_left = shift(att_left, LON, 1)
    out_own, out_lat = call(
        out_kernel,
        [VM] * 2,
        [shaped(full), shaped(edge)],
        limit=16,
        flops=10**9,
        name="out",
    )(att, wout)
    out_lat, keep = lax.optimization_barrier((out_lat, keep))
    eighth, small = (8, 16, 2 * D), (2, 16, 2 * D)
    kept, sends = summed(core_kernel, (keep, arrived), eighth, eighth, 3, "sum_core")
    a = [exchange(s, dy, dz) for (dy, dz), s in zip(PEERS, sends)]
    dqkv, kept, att_left = lax.optimization_barrier((dqkv, kept, att_left))
    tok_own, tok_main, tok_lat = call(
        token_kernel,
        [VM] * 4,
        [shaped(full), shaped(whole), shaped(edge)],
        limit=16,
        flops=2 * 10**9,
        name="token_grad",
    )(dqkv, wqkv, nrm, inverse)
    tok_main = shift(tok_main, LON, 1)
    (out_main,) = call(
        home_kernel, [VM] * 2, [shaped(whole)], limit=16, flops=10**9, name="out_left"
    )(att_left, wout)
    out_main, kept = lax.optimization_barrier((out_main, kept))
    kept, sends = summed(middle_kernel, [kept] + a, small, small, 3, "sum_low")
    a = [exchange(s, 2 * dy, 2 * dz) for (dy, dz), s in zip(PEERS, sends)]
    kept, (s,) = summed(
        late_kernel, [kept] + a, small[1:], small[1:], 1, "sum_next", [pltpu.VMEM(small, F32)]
    )
    out_main, kept = lax.optimization_barrier((out_main, kept))
    (lat,) = call(
        gather_kernel,
        [ANY] * 4,
        [shaped((2, 3, 12, 2, D))],
        scratch=[dma((2, 2))],
        out_spec=ANY,
        name="gather",
    )(out_main, tok_main, out_lat, tok_lat)
    kept, (s,) = summed(
        ring_kernel,
        (kept, exchange(s, 0, 4)),
        (16, D),
        (16, D),
        1,
        "sum_z",
        [pltpu.VMEM((2, 8, 2 * D), F32)],
        BF,
        64,
    )
    a = [shift(kept, "lat", 1), shift(s, "xh", 1), shift_both_x(s)]
    block_out, grad_tokens = call(
        finish_kernel,
        [ANY] * 5,
        [shaped(full), shaped(full)],
        scratch=[dma((2, 2))],
        aliases={0: 0, 1: 1},
        out_spec=ANY,
        name="assemble",
    )(out_own, tok_own, out_main, tok_main, shift(lat, "lat", 1))
    block_out, kept = lax.optimization_barrier((block_out, kept))
    grad_qkv, grad_out = call(
        last_kernel,
        [VM] * 4,
        [shaped((8, 3 * HD), F32), shaped((8, HD), F32)],
        name="sum_x",
    )(kept, *a)
    return (block_out, grad_tokens, grad_qkv, grad_out.T)


def solution(mesh):
    fine = Mesh(mesh.devices.reshape(SIZES), ALL)
    grid = P("lat", LON, None, None)
    in_specs = (grid, P("lat", LON), P(), P(), P(), grid)
    out_specs = (grid, grid, P(LON, None), P(None, LON))
    return jax.shard_map(
        per_device, mesh=fine, in_specs=in_specs, out_specs=out_specs, check_vma=False
    )
```
